32 devices in a mesh: dp: 4 (over y, core), fsdp: 8 (over z, x).
Axes of the slice: x: 2, y: 2, z: 4, core: 2. Of those that a mesh axis runs over, the one named last changes fastest.
Arguments:
- block_input: bfloat16 [32, 1024, 1280], P(('dp', 'fsdp')), may hold values from -6 to 6
- cotangent: bfloat16 [32, 1024, 1280], P(('dp', 'fsdp')), may hold values from -6 to 6
- protein_lengths: int32 [32, 4], P(('dp', 'fsdp')), may hold values from 1 to 512, 1024 in all within a row
- weight_in: float32 [1280, 640], P('fsdp', 'dp'), may hold values from -0.15625 to 0.15625
- moment_in: float32 [1280, 640], P('fsdp', 'dp'), may hold values from -1 to 1
- square_in: float32 [1280, 640], P('fsdp', 'dp'), may hold values from 0 to 1, as said below
- weight_conv: float32 [5, 640, 640], P(None, 'fsdp', 'dp'), may hold values from -0.109375 to 0.109375
- moment_conv: float32 [5, 640, 640], P(None, 'fsdp', 'dp'), may hold values from -1 to 1
- square_conv: float32 [5, 640, 640], P(None, 'fsdp', 'dp'), may hold values from 0 to 1, as said below
- weight_out: float32 [640, 1280], P('fsdp', 'dp'), may hold values from -0.25 to 0.25
- moment_out: float32 [640, 1280], P('fsdp', 'dp'), may hold values from -1 to 1
- square_out: float32 [640, 1280], P('fsdp', 'dp'), may hold values from 0 to 1, as said below
- vectors: float32 [7680], replicated, may hold values from -2 to 4, as said below
- moment_vectors: float32 [7680], replicated, may hold values from -1 to 1
- square_vectors: float32 [7680], replicated, may hold values from 0 to 1, as said below
Outputs:
- block_output: bfloat16 [32, 1024, 1280], P(('dp', 'fsdp'))
- input_grad: bfloat16 [32, 1024, 1280], P(('dp', 'fsdp'))
- grad_norm: float32 [], replicated
- new_weight_in: float32 [1280, 640], P('fsdp', 'dp')
- new_moment_in: float32 [1280, 640], P('fsdp', 'dp')
- new_square_in: float32 [1280, 640], P('fsdp', 'dp')
- new_weight_conv: float32 [5, 640, 640], P(None, 'fsdp', 'dp')
- new_moment_conv: float32 [5, 640, 640], P(None, 'fsdp', 'dp')
- new_square_conv: float32 [5, 640, 640], P(None, 'fsdp', 'dp')
- new_weight_out: float32 [640, 1280], P('fsdp', 'dp')
- new_moment_out: float32 [640, 1280], P('fsdp', 'dp')
- new_square_out: float32 [640, 1280], P('fsdp', 'dp')
- new_vectors: float32 [7680], replicated
- new_moment_vectors: float32 [7680], replicated
- new_square_vectors: float32 [7680], replicated
The draws below stay inside these ranges and needn't reach their ends.
Inputs may be any that keep to these rules, and one draw needn't show every extreme that they name: `vectors`: gains positive, shifts and biases of both signs. `square_in`: positive. `square_conv`: positive. `square_out`: positive. `square_vectors`: positive.
All inputs are finite; a program needn't handle non-finite values.
Results may differ from the reference program's by a relative error of at most 0.02.
Values may be sent and summed in bfloat16 or wider, within the bound.
No kernel may reach another device: no remote copies, remote signals or barrier semaphores. Data moves between devices by JAX's collectives and lax.ppermute only.
A program may use at most 128 MiB of HBM per device.

```python
import math
import jax
import jax.numpy as jnp
import numpy as np
from jax import lax

D = 1280
INNER = 640
KERNEL = 5
DILATION = 64
LENGTH = 1024
PROTEINS = 4
LONGEST = 512
STEP = 10
ROWS = 32
SMALL_PARAMS = 7680
PARAM_COUNT = 3694080


def first_moment(key, array_shape):
    return 0.11 * PARAM_COUNT ** (-0.5) * jax.random.truncated_normal(key, -4.0, 4.0, array_shape, jnp.float32)


def second_moment(key, array_shape):
    factor = jnp.exp(jax.random.uniform(key, array_shape, jnp.float32, math.log(0.5), math.log(8.0)))
    return 0.0526 / PARAM_COUNT * factor


def draw_moment_in(key, part):
    key = jax.random.fold_in(key, 21)
    return first_moment(key, (D, INNER))


def draw_square_in(key, part):
    key = jax.random.fold_in(key, 22)
    return second_moment(key, (D, INNER))


def draw_moment_conv(key, part):
    key = jax.random.fold_in(key, 23)
    return first_moment(key, (KERNEL, INNER, INNER))


def draw_square_conv(key, part):
    key = jax.random.fold_in(key, 24)
    return second_moment(key, (KERNEL, INNER, INNER))


def draw_moment_out(key, part):
    key = jax.random.fold_in(key, 25)
    return first_moment(key, (INNER, D))


def draw_square_out(key, part):
    key = jax.random.fold_in(key, 26)
    return second_moment(key, (INNER, D))


def draw_moment_vectors(key, part):
    key = jax.random.fold_in(key, 27)
    return first_moment(key, (SMALL_PARAMS,))


def draw_square_vectors(key, part):
    key = jax.random.fold_in(key, 28)
    return second_moment(key, (SMALL_PARAMS,))


def rising_gain(key, width_count, low_end, high_end):
    levels = jnp.exp(jnp.linspace(math.log(low_end), math.log(high_end), width_count))
    return levels * jax.random.uniform(key, (width_count,), jnp.float32, 0.8, 1.25)


def shift_values(key, width_count):
    return 0.3 * jax.random.truncated_normal(key, -4.0, 4.0, (width_count,), jnp.float32)


def draw_vectors(key, part):
    key = jax.random.fold_in(key, 11)
    low_end = 0.6
    high_end = 1.8
    subkeys = jax.random.split(key, 9)
    return jnp.concatenate([rising_gain(subkeys[0], D, low_end, high_end), shift_values(subkeys[1], D), rising_gain(subkeys[2], INNER, low_end, high_end), shift_values(subkeys[3], INNER), rising_gain(subkeys[4], INNER, low_end, high_end), shift_values(subkeys[5], INNER), shift_values(subkeys[6], INNER), shift_values(subkeys[7], INNER), shift_values(subkeys[8], D)])


def shard_levels(own_key, extent, cuts, smallest, high):
    def one(axis_at, shards_of):
        draws = jax.random.uniform(jax.random.fold_in(jax.random.fold_in(own_key, 6), axis_at), (shards_of,), jnp.float32, smallest / len(cuts), high / len(cuts))
        return jnp.repeat(jnp.exp(draws), extent[axis_at] // shards_of).reshape((-1,) + (1,) * (len(extent) - axis_at - 1))

    level = one(*cuts[0])
    for cut in cuts[1:]:
        level = level * one(*cut)
    return level


def profile(amount, total, bound, lean):
    loads = [(1 << 20) // math.isqrt(grade ** lean) + 1 for grade in range(2, amount + 1)]
    surplus, counts = total - bound - (amount - 1), [1] * (amount - 1)
    while surplus > 0:
        free = [i for i in range(amount - 1) if counts[i] < bound]
        mass, left = sum([loads[i] for i in free]), surplus
        for i in free:
            more = min(bound - counts[i], max(1, left * loads[i] // mass), surplus)
            counts[i] = counts[i] + more
            surplus = surplus - more
    return np.array([bound] + counts)


def ragged_sizes(own_key, count, total, limit, skew):
    if count == 2:
        one = jax.random.randint(own_key, (), max(1, total - limit), min(limit, total - 1) + 1)
        return jnp.stack([one, total - one])
    tallies = jnp.asarray(profile(count, total, limit, skew), jnp.int32)
    twos = (count - 1) // 2
    giver, receiver = tallies[1:1 + 2 * twos:2], tallies[2:2 + 2 * twos:2]
    slack = jnp.minimum(giver - 1, limit - receiver)
    moved = jax.random.randint(jax.random.fold_in(own_key, 1), (twos,), 0, 1 << 20) % (slack + 1)
    tallies = tallies.at[1:1 + 2 * twos:2].set(giver - moved).at[2:2 + 2 * twos:2].set(receiver + moved)
    return tallies[jax.random.permutation(jax.random.fold_in(own_key, 2), count)]


def scatter_about(key, shape, scale, bound, cuts=(), held_as=jnp.bfloat16):
    result = scale * jax.random.normal(key, shape, jnp.float32)
    if cuts:
        result = result * shard_levels(key, shape, cuts, -0.22, 0.18)
    return jnp.clip(result, -bound, bound).astype(held_as)


def setup_inputs(seed: int = 0) -> dict:
    key_list = jax.random.split(jax.random.key(seed), 16)
    block_input = scatter_about(key_list[0], (ROWS, LENGTH, D), 1.0, 6.0, ((0, 32),))
    cotangent = scatter_about(key_list[1], (ROWS, LENGTH, D), 1.0, 6.0, ((0, 32),))
    protein_lengths = jax.vmap(lambda own: ragged_sizes(own, PROTEINS, LENGTH, LONGEST, 2))(jax.random.split(key_list[2], ROWS)).reshape((ROWS, PROTEINS)).astype(jnp.int32)
    weight_in = scatter_about(key_list[3], (D, INNER), D ** -0.5, 0.15625, ((0, 8), (1, 4)), jnp.float32)
    moment_in = draw_moment_in(jax.random.fold_in(key_list[15], 71), 0)
    square_in = draw_square_in(jax.random.fold_in(key_list[15], 71), 0)
    weight_conv = scatter_about(key_list[6], (KERNEL, INNER, INNER), (KERNEL * INNER) ** -0.5, 0.109375, ((1, 8), (2, 4)), jnp.float32)
    moment_conv = draw_moment_conv(jax.random.fold_in(key_list[15], 71), 0)
    square_conv = draw_square_conv(jax.random.fold_in(key_list[15], 71), 0)
    weight_out = scatter_about(key_list[9], (INNER, D), INNER ** -0.5, 0.25, ((0, 8), (1, 4)), jnp.float32)
    moment_out = draw_moment_out(jax.random.fold_in(key_list[15], 71), 0)
    square_out = draw_square_out(jax.random.fold_in(key_list[15], 71), 0)
    vectors = draw_vectors(jax.random.fold_in(key_list[15], 71), 0)
    moment_vectors = draw_moment_vectors(jax.random.fold_in(key_list[15], 71), 0)
    square_vectors = draw_square_vectors(jax.random.fold_in(key_list[15], 71), 0)
    return {"block_input": block_input, "cotangent": cotangent, "protein_lengths": protein_lengths, "weight_in": weight_in, "moment_in": moment_in, "square_in": square_in, "weight_conv": weight_conv, "moment_conv": moment_conv, "square_conv": square_conv, "weight_out": weight_out, "moment_out": moment_out, "square_out": square_out, "vectors": vectors, "moment_vectors": moment_vectors, "square_vectors": square_vectors}


PRECISE = lax.Precision.HIGHEST
NORM_EPS = 1e-05
ADAM_EPS = 1e-08
BETA_ONE = 0.9
BETA_TWO = 0.95
CLIP_LIMIT = 1.0
RATE_MATRIX = 0.04
RATE_VECTOR = 0.3
DECAY_MATRIX = 0.1

@jax.custom_vjp
def low(v):
    return lax.optimization_barrier(v.astype(jnp.bfloat16)).astype(jnp.float32)

@jax.custom_vjp
def low_back(v):
    return v

def low_keep(v):
    return (low(v), None)

def low_pass(kept, grad):
    return (grad,)

def back_keep(v):
    return (v, None)

def back_low(kept, grad):
    return (low(grad),)
low.defvjp(low_keep, low_pass)
low_back.defvjp(back_keep, back_low)

def layer_norm(values, gain, shift):
    center = values - lax.optimization_barrier(jnp.mean(values, axis=-1, keepdims=True))
    spread = lax.optimization_barrier(jnp.mean(center * center, axis=-1, keepdims=True))
    return center * lax.rsqrt(spread + NORM_EPS) * gain + shift

def norm_gelu(values, gain, shift):
    return jax.nn.gelu(layer_norm(values, gain, shift))

def split_vectors(vectors):
    widths = [D, D, INNER, INNER, INNER, INNER, INNER, INNER, D]
    pieces = []
    offset = 0
    for width_count in widths:
        pieces.append(vectors[offset:offset + width_count])
        offset = offset + width_count
    return pieces

def tap_masks(protein_lengths):
    run_ends = jnp.cumsum(protein_lengths, axis=1).astype(jnp.int32)
    run_starts = (run_ends - protein_lengths).astype(jnp.int32)
    position = jnp.arange(LENGTH, dtype=jnp.int32)
    inside = (position[None, :, None] >= run_starts[:, None, :]) & (position[None, :, None] < run_ends[:, None, :])
    lower_bound = lax.optimization_barrier(jnp.sum(jnp.where(inside, run_starts[:, None, :], 0), axis=2)).astype(jnp.int32)
    upper_bound = lax.optimization_barrier(jnp.sum(jnp.where(inside, run_ends[:, None, :], 0), axis=2)).astype(jnp.int32)
    layers = []
    for tap_index in range(KERNEL):
        target = position[None, :] + (tap_index - KERNEL // 2) * DILATION
        layers.append(((target >= lower_bound) & (target < upper_bound)).astype(jnp.float32))
    return jnp.stack(layers, axis=1)

def shifted(values, offset):
    margin = KERNEL // 2 * DILATION
    padded = jnp.pad(values, ((0, 0), (margin, margin), (0, 0)))
    return lax.slice_in_dim(padded, margin + offset, margin + offset + values.shape[1], axis=1)

def dilated(hidden, kernel_weights, tap_mask):
    total = jnp.zeros(hidden.shape[:2] + (kernel_weights.shape[2],), jnp.float32)
    for tap_index in range(KERNEL):
        offset = (tap_index - KERNEL // 2) * DILATION
        source = shifted(hidden, offset) * tap_mask[:, tap_index, :, None]
        total = total + jnp.einsum('rli,io->rlo', source, kernel_weights[tap_index], precision=PRECISE, preferred_element_type=jnp.float32)
    return total

def forward(block_input, weight_in, weight_conv, weight_out, vectors, tap_mask):
    gain_one, shift_one, gain_two, shift_two, gain_three, shift_three, bias_one, bias_two, bias_three = split_vectors(vectors)
    rounded_in = low(weight_in)
    rounded_conv = low(weight_conv)
    rounded_out = low(weight_out)
    hidden_one = low(norm_gelu(block_input, gain_one, shift_one))
    mixed_one = low_back(jnp.einsum('rld,di->rli', hidden_one, rounded_in, precision=PRECISE, preferred_element_type=jnp.float32) + bias_one)
    hidden_two = low(norm_gelu(mixed_one, gain_two, shift_two))
    mixed_two = low_back(dilated(hidden_two, rounded_conv, tap_mask) + bias_two)
    hidden_three = low(norm_gelu(mixed_two, gain_three, shift_three))
    branch = low_back(jnp.einsum('rli,id->rld', hidden_three, rounded_out, precision=PRECISE, preferred_element_type=jnp.float32) + bias_three)
    return block_input + branch

def adamw_update(weight, moment, square, gradient, step_rate, weight_decay):
    new_moment = BETA_ONE * moment + (1.0 - BETA_ONE) * gradient
    new_square = BETA_TWO * square + (1.0 - BETA_TWO) * gradient * gradient
    moment_hat = new_moment / (1.0 - BETA_ONE ** STEP)
    square_hat = new_square / (1.0 - BETA_TWO ** STEP)
    update = moment_hat / (jnp.sqrt(square_hat) + ADAM_EPS)
    return (weight - step_rate * (update + weight_decay * weight), new_moment, new_square)

def reference(block_input, cotangent, protein_lengths, weight_in, moment_in, square_in, weight_conv, moment_conv, square_conv, weight_out, moment_out, square_out, vectors, moment_vectors, square_vectors):
    group_rows = math.gcd(ROWS, max(1, 4096 // LENGTH))
    block_count = ROWS // group_rows
    input_blocks = block_input.reshape(block_count, group_rows, LENGTH, D)
    cotangent_blocks = cotangent.reshape(block_count, group_rows, LENGTH, D)
    length_blocks = protein_lengths.reshape(block_count, group_rows, PROTEINS)

    def block_step(totals, block_items):
        input_block, cotangent_block, length_block = block_items
        tap_mask = tap_masks(length_block)

        def local_forward(first, second, third, fourth, fifth):
            return forward(first, second, third, fourth, fifth, tap_mask)
        output, pullback = jax.vjp(local_forward, input_block.astype(jnp.float32), weight_in, weight_conv, weight_out, vectors)
        gradients = pullback(cotangent_block.astype(jnp.float32))
        totals = tuple((total + gradient for total, gradient in zip(totals, gradients[1:])))
        return (totals, (output.astype(jnp.bfloat16), gradients[0].astype(jnp.bfloat16)))
    initial = (jnp.zeros_like(weight_in), jnp.zeros_like(weight_conv), jnp.zeros_like(weight_out), jnp.zeros_like(vectors))
    grad_totals, (outputs, input_grads) = lax.scan(block_step, initial, (input_blocks, cotangent_blocks, length_blocks))
    grad_in, grad_conv, grad_out, grad_vectors = grad_totals
    squares = jnp.sum(grad_in * grad_in) + jnp.sum(grad_conv * grad_conv) + jnp.sum(grad_out * grad_out) + jnp.sum(grad_vectors * grad_vectors)
    grad_norm = jnp.sqrt(squares)
    clip_factor = jnp.minimum(1.0, CLIP_LIMIT / (grad_norm + 1e-06))
    new_in = adamw_update(weight_in, moment_in, square_in, clip_factor * grad_in, RATE_MATRIX, DECAY_MATRIX)
    new_conv = adamw_update(weight_conv, moment_conv, square_conv, clip_factor * grad_conv, RATE_MATRIX, DECAY_MATRIX)
    new_out = adamw_update(weight_out, moment_out, square_out, clip_factor * grad_out, RATE_MATRIX, DECAY_MATRIX)
    new_vec = adamw_update(vectors, moment_vectors, square_vectors, clip_factor * grad_vectors, RATE_VECTOR, 0.0)
    return (outputs.reshape(ROWS, LENGTH, D), input_grads.reshape(ROWS, LENGTH, D), grad_norm, new_in[0], new_in[1], new_in[2], new_conv[0], new_conv[1], new_conv[2], new_out[0], new_out[1], new_out[2], new_vec[0], new_vec[1], new_vec[2])
```

```python
import functools

import jax
import jax.numpy as jnp
from jax import lax
from jax.experimental import pallas as pl
from jax.experimental.pallas import tpu as pltpu
from jax.sharding import PartitionSpec as P

D = 1280
INNER = 640
KERNEL = 5
DILATION = 64
LENGTH = 1024
STEP = 10
MARGIN = KERNEL // 2 * DILATION
OFFSETS = tuple((k - KERNEL // 2) * DILATION for k in range(KERNEL))
BLOCK = 256
STEPS = LENGTH // BLOCK

NORM_EPS = 1e-05
ADAM_EPS = 1e-08
BETA_ONE = 0.9
BETA_TWO = 0.95
CLIP_LIMIT = 1.0
RATE_MATRIX = 0.04
RATE_VECTOR = 0.3
DECAY_MATRIX = 0.1
GELU_C = 0.7978845608
GELU_K = 0.044715

GAIN_ONE, SHIFT_ONE = (0, 1280), (1280, 1280)
GAIN_TWO, SHIFT_TWO = (2560, 640), (3200, 640)
GAIN_THREE, SHIFT_THREE = (3840, 640), (4480, 640)
BIAS_ONE, BIAS_TWO, BIAS_THREE = (5120, 640), (5760, 640), (6400, 1280)

BF16 = jnp.bfloat16
F32 = jnp.float32
AXES = ("dp", "fsdp")
VMEM_LIMIT = 56 * 1024 * 1024


def round16(n):
    return -(-n // 16) * 16


class Geometry:
    def __init__(self, taps, rows, cols):
        self.taps, self.rows, self.cols = taps, rows, cols
        self.height = taps * rows
        self.tiles, self.rest = divmod(cols, 128)
        self.groups = 128 // self.rest if self.rest and 128 % self.rest == 0 else 1
        self.tile_rows = round16(self.height)
        self.rest_rows = round16(-(-self.height // self.groups)) if self.rest else 0
        self.packed = self.tiles * self.tile_rows + self.rest_rows

    def pack(self, value):
        pieces = [value[:, 128 * t : 128 * t + 128] for t in range(self.tiles)]
        more = self.tile_rows - self.height
        if more:
            empty = jnp.zeros((more, 128), value.dtype)
            pieces = [jnp.concatenate([piece, empty], axis=0) for piece in pieces]
        if self.rest:
            rest = value[:, 128 * self.tiles :]
            spare = self.groups * self.rest_rows - self.height
            if spare:
                rest = jnp.concatenate([rest, jnp.zeros((spare, self.rest), value.dtype)], axis=0)
            n = self.rest_rows
            parts = [rest[n * g : n * g + n] for g in range(self.groups)]
            empty = 128 - self.groups * self.rest
            if empty:
                parts.append(jnp.zeros((n, empty), value.dtype))
            pieces.append(jnp.concatenate(parts, axis=1))
        return jnp.concatenate(pieces, axis=0)

    def unpack(self, packed):
        pieces = [
            packed[self.tile_rows * t : self.tile_rows * t + self.height]
            for t in range(self.tiles)
        ]
        if self.rest:
            base = self.tiles * self.tile_rows
            n, w = self.rest_rows, self.rest
            parts = []
            for g in range(self.groups):
                have = min(n, self.height - n * g)
                if have > 0:
                    parts.append(packed[base : base + have, w * g : w * g + w])
            pieces.append(jnp.concatenate(parts, axis=0))
        return jnp.concatenate(pieces, axis=1)


class Network:
    def __init__(self, dp, fsdp):
        self.dp, self.fsdp = dp, fsdp
        self.half = dp * fsdp // 2
        far = [("f", b) for b in range(fsdp.bit_length() - 2, 0, -1)]
        near = [("f", 0)] if fsdp > 1 else []
        rows = [("d", b) for b in range(dp.bit_length() - 2, 0, -1)]
        self.order = (far + near + rows, far + rows + near)

    def flip(self, stage, device):
        d, f = divmod(device, self.fsdp)
        kind, bit = self.order[d & 1][stage]
        if kind == "f":
            f ^= 1 << bit
        else:
            d ^= 1 << bit
        return d * self.fsdp + f

    def stage(self, stage):
        return [(i, self.flip(stage, i)) for i in range(self.dp * self.fsdp)]

    def core(self):
        return [(i, i ^ self.fsdp) for i in range(self.dp * self.fsdp)]

    def stages(self):
        return len(self.order[0])

    def slot(self, d, f, me_d, me_f):
        d_bits = jnp.bitwise_xor(me_d, d)
        f_bits = jnp.bitwise_xor(me_f, f)
        total = jnp.int32(0)
        for i, (kind, bit) in enumerate(self.order[d & 1]):
            source = f_bits if kind == "f" else d_bits
            total = total + (jnp.bitwise_and(lax.shift_right_logical(source, bit), 1) << i)
        return total


def call(kernel, name, out_shape, in_specs, out_specs, grid=(), scratch=(), flops=0, bytes_accessed=0):
    return pl.pallas_call(
        kernel,
        name=name,
        grid=grid,
        out_shape=out_shape,
        in_specs=in_specs,
        out_specs=out_specs,
        scratch_shapes=list(scratch),
        compiler_params=pltpu.CompilerParams(vmem_limit_bytes=VMEM_LIMIT),
        cost_estimate=pl.CostEstimate(
            flops=flops, bytes_accessed=bytes_accessed, transcendentals=0
        ),
    )


def whole(shape):
    return pl.BlockSpec(shape, lambda *_: (0,) * len(shape))


def tokens(width):
    return pl.BlockSpec((BLOCK, width), lambda i: (i, 0))


SMEM = pl.BlockSpec(memory_space=pltpu.SMEM)
ANY = pl.BlockSpec(memory_space=pl.ANY)


def shape(dims, dtype):
    return jax.ShapeDtypeStruct(dims, dtype)


def part(vec_ref, span):
    return vec_ref[:, span[0] : span[0] + span[1]]


def add_rows(ref, value, first):
    row = jnp.sum(value, axis=0, keepdims=True)

    @pl.when(first)
    def _():
        ref[...] = row

    @pl.when(jnp.logical_not(first))
    def _():
        ref[...] += row


def statistics(values):
    width = values.shape[1]
    mean = jnp.sum(values, axis=1, keepdims=True) * (1.0 / width)
    center = values - mean
    spread = jnp.sum(center * center, axis=1, keepdims=True) * (1.0 / width)
    return center, lax.rsqrt(spread + NORM_EPS)


def gelu(a):
    t = jnp.tanh(GELU_C * (a + GELU_K * (a * a * a)))
    return 0.5 * a * (1.0 + t)


def gelu_slope(a):
    square = a * a
    t = jnp.tanh(GELU_C * a * (1.0 + GELU_K * square))
    half = 0.5 * (1.0 + t)
    return half + half * (1.0 - t) * a * (GELU_C + (3.0 * GELU_C * GELU_K) * square)


def norm_backward(grad, normed, root, gain, shift):
    width = grad.shape[1]
    d_a = grad * gelu_slope(normed * gain + shift)
    scaled = d_a * gain
    mean_one = jnp.sum(scaled, axis=1, keepdims=True) * (1.0 / width)
    mean_two = jnp.sum(scaled * normed, axis=1, keepdims=True) * (1.0 / width)
    return root * (scaled - mean_one - normed * mean_two), d_a * normed, d_a


def tap_mask(ends_ref, start, rows, offset, width):
    position = start + lax.broadcasted_iota(jnp.int32, (rows, 128), 0)
    count = ends_ref.shape[0]
    lower = jnp.zeros((rows, 128), jnp.int32)
    upper = jnp.full((rows, 128), ends_ref[count - 1], jnp.int32)
    for j in range(count - 1):
        lower = jnp.where(position >= ends_ref[j], ends_ref[j], lower)
    for j in range(count - 2, -1, -1):
        upper = jnp.where(position < ends_ref[j], ends_ref[j], upper)
    target = position + offset
    mask = jnp.where((target >= lower) & (target < upper), 1.0, 0.0).astype(BF16)
    return jnp.concatenate([mask] * (width // 128), axis=1)


def fill_padded(padded, source):
    padded[0:MARGIN] = jnp.zeros((MARGIN, source.shape[1]), source.dtype)
    padded[MARGIN : MARGIN + LENGTH] = source[...]
    padded[MARGIN + LENGTH : MARGIN + LENGTH + MARGIN] = jnp.zeros(
        (MARGIN, source.shape[1]), source.dtype
    )


def dot(a, b):
    return jnp.dot(a, b, preferred_element_type=F32)


def dot_nt(a, b):
    return lax.dot_general(a, b, (((1,), (1,)), ((), ())), preferred_element_type=F32)


def assemble(net, geo, me_ref, own, peer, buffer, sems, full):
    core = jnp.bitwise_and(me_ref[0], 1)
    first = pltpu.make_async_copy(own, buffer.at[core], sems.at[0])
    second = pltpu.make_async_copy(peer, buffer.at[1 - core], sems.at[1])
    first.start()
    second.start()
    first.wait()
    second.wait()
    for f in range(net.fsdp):
        blocks = [
            geo.unpack(buffer[d & 1, net.slot(d, f, me_ref[0], me_ref[1])])
            for d in range(net.dp)
        ]
        row = jnp.concatenate(blocks, axis=1)
        for k in range(geo.taps):
            start = k * geo.rows * net.fsdp + f * geo.rows
            full[start : start + geo.rows] = row[k * geo.rows : k * geo.rows + geo.rows]


def distribute(net, geo, me_ref, full, buffer, sems, keep, send):
    for f in range(net.fsdp):
        pieces = [
            full[
                k * geo.rows * net.fsdp + f * geo.rows : k * geo.rows * net.fsdp
                + f * geo.rows
                + geo.rows
            ]
            for k in range(geo.taps)
        ]
        row = pieces[0] if geo.taps == 1 else jnp.concatenate(pieces, axis=0)
        for d in range(net.dp):
            buffer[d & 1, net.slot(d, f, me_ref[0], me_ref[1])] = geo.pack(
                row[:, d * geo.cols : d * geo.cols + geo.cols]
            )
    core = jnp.bitwise_and(me_ref[0], 1)
    first = pltpu.make_async_copy(buffer.at[1 - core], send, sems.at[0])
    second = pltpu.make_async_copy(buffer.at[core], keep, sems.at[1])
    first.start()
    second.start()
    first.wait()
    second.wait()


def slots(net, geo):
    return (net.half, geo.packed, 128)


def piece_scratch(net, geo):
    return [pltpu.VMEM((2,) + slots(net, geo), BF16), pltpu.SemaphoreType.DMA((2,))]


def pack_weights(geos, weights):
    def kernel(*refs):
        n = len(geos)
        for geo, source, target in zip(geos, refs[:n], refs[n:]):
            target[...] = geo.pack(source[...].astype(BF16))

    return call(
        kernel,
        "pack_weights",
        [shape((geo.packed, 128), BF16) for geo in geos],
        [whole(w.shape) for w in weights],
        [whole((geo.packed, 128)) for geo in geos],
        bytes_accessed=1_000_000,
    )(*weights)


def first_norm(block_input, cotangent, vec):
    def kernel(x_ref, cot_ref, vec_ref, h_ref, ht_ref, stat_ref, bias_ref):
        values = x_ref[...].astype(F32)
        center, root = statistics(values)
        normed = center * root
        hidden = gelu(normed * part(vec_ref, GAIN_ONE) + part(vec_ref, SHIFT_ONE)).astype(BF16)
        h_ref[...] = hidden
        ht_ref[...] = hidden.T
        lane = lax.broadcasted_iota(jnp.int32, (BLOCK, 128), 1)
        stat_ref[...] = jnp.where(lane == 0, values[:, :1] - center[:, :1], root)
        add_rows(bias_ref, cot_ref[...].astype(F32), pl.program_id(0) == 0)

    return call(
        kernel,
        "first_norm",
        [
            shape((LENGTH, D), BF16),
            shape((D, LENGTH), BF16),
            shape((LENGTH, 128), F32),
            shape((1, D), F32),
        ],
        [tokens(D), tokens(D), whole(vec.shape)],
        [tokens(D), pl.BlockSpec((D, BLOCK), lambda i: (0, i)), tokens(128), whole((1, D))],
        grid=(STEPS,),
        flops=30 * LENGTH * D,
        bytes_accessed=8 * LENGTH * D,
    )(block_input, cotangent, vec)


def norm_out(mixed, vec_ref, gain, shift_span, h_ref, ht_ref, normed_ref, root_ref):
    center, root = statistics(mixed)
    normed = center * root
    hidden = gelu(normed * part(vec_ref, gain) + part(vec_ref, shift_span)).astype(BF16)
    h_ref[...] = hidden
    ht_ref[...] = hidden.T
    normed_ref[...] = normed
    root_ref[...] = jnp.broadcast_to(root, (BLOCK, 128))


NORM_SHAPES = [
    shape((LENGTH, INNER), BF16),
    shape((INNER, LENGTH), BF16),
    shape((LENGTH, INNER), F32),
    shape((LENGTH, 128), F32),
]


def norm_specs():
    return [
        tokens(INNER),
        pl.BlockSpec((INNER, BLOCK), lambda i: (0, i)),
        tokens(INNER),
        tokens(128),
    ]


def mix_one(net, geo, me, own, peer, hidden_one, vec):
    def kernel(me_ref, own_ref, peer_ref, h1_ref, vec_ref, h_ref, ht_ref, n_ref, r_ref, full, buf, sems):
        @pl.when(pl.program_id(0) == 0)
        def _():
            assemble(net, geo, me_ref, own_ref, peer_ref, buf, sems, full)

        mixed = dot(h1_ref[...], full[...]) + part(vec_ref, BIAS_ONE)
        norm_out(mixed, vec_ref, GAIN_TWO, SHIFT_TWO, h_ref, ht_ref, n_ref, r_ref)

    return call(
        kernel,
        "mix_one",
        NORM_SHAPES + [shape((D, INNER), BF16)],
        [SMEM, ANY, ANY, tokens(D), whole(vec.shape)],
        norm_specs() + [whole((D, INNER))],
        grid=(STEPS,),
        scratch=piece_scratch(net, geo),
        flops=2 * LENGTH * D * INNER,
        bytes_accessed=12_000_000,
    )(me, own, peer, hidden_one, vec)


def mix_two(net, geo, me, ends, own, peer, hidden_two, vec):
    def kernel(
        me_ref, ends_ref, own_ref, peer_ref, h2_ref, vec_ref, h_ref, ht_ref, n_ref, r_ref, full, buf, sems, pad
    ):
        step = pl.program_id(0)

        @pl.when(step == 0)
        def _():
            assemble(net, geo, me_ref, own_ref, peer_ref, buf, sems, full)
            fill_padded(pad, h2_ref)

        start = step * BLOCK
        mixed = jnp.zeros((BLOCK, INNER), F32)
        for k, offset in enumerate(OFFSETS):
            source = pad[pl.ds(pl.multiple_of(start + MARGIN + offset, DILATION), BLOCK)]
            source = source * tap_mask(ends_ref, start, BLOCK, offset, INNER)
            mixed = mixed + dot(source, full[k * INNER : k * INNER + INNER])
        mixed = mixed + part(vec_ref, BIAS_TWO)
        norm_out(mixed, vec_ref, GAIN_THREE, SHIFT_THREE, h_ref, ht_ref, n_ref, r_ref)

    return call(
        kernel,
        "mix_two",
        NORM_SHAPES + [shape((KERNEL * INNER, INNER), BF16)],
        [SMEM, SMEM, ANY, ANY, whole((LENGTH, INNER)), whole(vec.shape)],
        norm_specs() + [whole((KERNEL * INNER, INNER))],
        grid=(STEPS,),
        scratch=piece_scratch(net, geo) + [pltpu.VMEM((LENGTH + 2 * MARGIN, INNER), BF16)],
        flops=2 * LENGTH * KERNEL * INNER * INNER,
        bytes_accessed=18_000_000,
    )(me, ends, own, peer, hidden_two, vec)


def gradient_shapes(net, geo):
    return [shape(slots(net, geo), BF16)] * 2


def weight_gradient(net, geo, me, left, right, name):
    dims = (left.shape[0], right.shape[1])

    def kernel(me_ref, left_ref, right_ref, keep, send, full, buf, sems):
        full[...] = dot(left_ref[...], right_ref[...]).astype(BF16)
        distribute(net, geo, me_ref, full, buf, sems, keep, send)

    return call(
        kernel,
        name,
        gradient_shapes(net, geo),
        [SMEM, whole(left.shape), whole(right.shape)],
        [ANY, ANY],
        grid=(1,),
        scratch=[pltpu.VMEM(dims, BF16)] + piece_scratch(net, geo),
        flops=2 * LENGTH * dims[0] * dims[1],
        bytes_accessed=6_000_000,
    )(me, left, right)


def back_through_out(net, geo, me, own, peer, cotangent, normed, root, vec):
    def kernel(
        me_ref, own_ref, peer_ref, cot_ref, n_ref, r_ref, vec_ref, back_ref, gg_ref, gs_ref, gb_ref, full, buf, sems
    ):
        first = pl.program_id(0) == 0

        @pl.when(first)
        def _():
            assemble(net, geo, me_ref, own_ref, peer_ref, buf, sems, full)

        grad = dot_nt(cot_ref[...], full[...])
        back, to_gain, to_shift = norm_backward(
            grad, n_ref[...], r_ref[:, :1], part(vec_ref, GAIN_THREE), part(vec_ref, SHIFT_THREE)
        )
        back = back.astype(BF16)
        back_ref[...] = back
        add_rows(gg_ref, to_gain, first)
        add_rows(gs_ref, to_shift, first)
        add_rows(gb_ref, back.astype(F32), first)

    row = shape((1, INNER), F32)
    return call(
        kernel,
        "back_through_out",
        [shape((LENGTH, INNER), BF16), row, row, row, shape((INNER, D), BF16)],
        [SMEM, ANY, ANY, tokens(D), tokens(INNER), tokens(128), whole(vec.shape)],
        [tokens(INNER)] + [whole((1, INNER))] * 3 + [whole((INNER, D))],
        grid=(STEPS,),
        scratch=piece_scratch(net, geo),
        flops=2 * LENGTH * D * INNER,
        bytes_accessed=12_000_000,
    )(me, own, peer, cotangent, normed, root, vec)


def block_result(block_input, hidden_three, full_out, vec):
    def kernel(x_ref, h_ref, w_ref, vec_ref, out_ref):
        branch = dot(h_ref[...], w_ref[...]) + part(vec_ref, BIAS_THREE)
        out_ref[...] = (x_ref[...].astype(F32) + branch).astype(BF16)

    return call(
        kernel,
        "block_result",
        shape((LENGTH, D), BF16),
        [tokens(D), tokens(INNER), whole((INNER, D)), whole(vec.shape)],
        tokens(D),
        grid=(STEPS,),
        flops=2 * LENGTH * D * INNER,
        bytes_accessed=8_000_000,
    )(block_input, hidden_three, full_out, vec)


def conv_gradient(net, geo, me, ends, hidden_two_t, back_two):
    def kernel(me_ref, ends_ref, left_ref, back_ref, keep, send, full, pad, buf, sems):
        fill_padded(pad, back_ref)
        for k, offset in enumerate(OFFSETS):
            source = pad[MARGIN - offset : MARGIN - offset + LENGTH]
            source = source * tap_mask(ends_ref, 0, LENGTH, -offset, INNER)
            full[k * INNER : k * INNER + INNER] = dot(left_ref[...], source).astype(BF16)
        distribute(net, geo, me_ref, full, buf, sems, keep, send)

    return call(
        kernel,
        "conv_gradient",
        gradient_shapes(net, geo),
        [SMEM, SMEM, whole((INNER, LENGTH)), whole((LENGTH, INNER))],
        [ANY, ANY],
        grid=(1,),
        scratch=[
            pltpu.VMEM((KERNEL * INNER, INNER), BF16),
            pltpu.VMEM((LENGTH + 2 * MARGIN, INNER), BF16),
        ]
        + piece_scratch(net, geo),
        flops=2 * LENGTH * KERNEL * INNER * INNER,
        bytes_accessed=7_000_000,
    )(me, ends, hidden_two_t, back_two)


def back_through_conv(ends, back_two, full_conv, normed, root, vec):
    def kernel(ends_ref, back_ref, w_ref, n_ref, r_ref, vec_ref, out_ref, gg_ref, gs_ref, gb_ref, pad):
        step = pl.program_id(0)
        first = step == 0

        @pl.when(first)
        def _():
            fill_padded(pad, back_ref)

        start = step * BLOCK
        grad = jnp.zeros((BLOCK, INNER), F32)
        for k, offset in enumerate(OFFSETS):
            source = pad[pl.ds(pl.multiple_of(start + MARGIN - offset, DILATION), BLOCK)]
            source = source * tap_mask(ends_ref, start, BLOCK, -offset, INNER)
            grad = grad + dot_nt(source, w_ref[k * INNER : k * INNER + INNER])
        back, to_gain, to_shift = norm_backward(
            grad, n_ref[...], r_ref[:, :1], part(vec_ref, GAIN_TWO), part(vec_ref, SHIFT_TWO)
        )
        back = back.astype(BF16)
        out_ref[...] = back
        add_rows(gg_ref, to_gain, first)
        add_rows(gs_ref, to_shift, first)
        add_rows(gb_ref, back.astype(F32), first)

    row = shape((1, INNER), F32)
    return call(
        kernel,
        "back_through_conv",
        [shape((LENGTH, INNER), BF16), row, row, row],
        [
            SMEM,
            whole((LENGTH, INNER)),
            whole((KERNEL * INNER, INNER)),
            tokens(INNER),
            tokens(128),
            whole(vec.shape),
        ],
        [tokens(INNER)] + [whole((1, INNER))] * 3,
        grid=(STEPS,),
        scratch=[pltpu.VMEM((LENGTH + 2 * MARGIN, INNER), BF16)],
        flops=2 * LENGTH * KERNEL * INNER * INNER,
        bytes_accessed=10_000_000,
    )(ends, back_two, full_conv, normed, root, vec)


def back_through_in(back_one, full_in, block_input, cotangent, stat, vec):
    def kernel(back_ref, w_ref, x_ref, cot_ref, stat_ref, vec_ref, out_ref, gg_ref, gs_ref):
        first = pl.program_id(0) == 0
        grad = dot_nt(back_ref[...], w_ref[...])
        root = stat_ref[:, 1:2]
        normed = (x_ref[...].astype(F32) - stat_ref[:, :1]) * root
        back, to_gain, to_shift = norm_backward(
            grad, normed, root, part(vec_ref, GAIN_ONE), part(vec_ref, SHIFT_ONE)
        )
        out_ref[...] = (cot_ref[...].astype(F32) + back).astype(BF16)
        add_rows(gg_ref, to_gain, first)
        add_rows(gs_ref, to_shift, first)

    row = shape((1, D), F32)
    return call(
        kernel,
        "back_through_in",
        [shape((LENGTH, D), BF16), row, row],
        [tokens(INNER), whole((D, INNER)), tokens(D), tokens(D), tokens(128), whole(vec.shape)],
        [tokens(D)] + [whole((1, D))] * 2,
        grid=(STEPS,),
        flops=2 * LENGTH * D * INNER,
        bytes_accessed=12_000_000,
    )(back_one, full_in, block_input, cotangent, stat, vec)


def sum_squares(owned):
    def kernel(*refs):
        total = jnp.zeros((1, 128), F32)
        for ref in refs[:-1]:
            value = ref[...].astype(F32)
            total = total + jnp.sum(value * value, axis=0, keepdims=True)
        refs[-1][...] = total

    return call(
        kernel,
        "sum_squares",
        shape((1, 128), F32),
        [whole(v.shape) for v in owned],
        whole((1, 128)),
        bytes_accessed=1_000_000,
    )(*owned)


def adamw(weight, moment, square, gradient, rate, decay):
    new_moment = BETA_ONE * moment + (1.0 - BETA_ONE) * gradient
    new_square = BETA_TWO * square + (1.0 - BETA_TWO) * gradient * gradient
    moment_hat = new_moment * (1.0 / (1.0 - BETA_ONE**STEP))
    square_hat = new_square * (1.0 / (1.0 - BETA_TWO**STEP))
    update = moment_hat / (jnp.sqrt(square_hat) + ADAM_EPS)
    return weight - rate * (update + decay * weight), new_moment, new_square


def update_all(geos, owned, totals, weights, vectors):
    n = len(geos)
    size = vectors[0].shape[1]

    def kernel(*refs):
        owned_refs, total_ref = refs[:n], refs[n]
        ins = refs[n + 1 : n + 1 + 3 * n + 3]
        outs = refs[n + 1 + 3 * n + 3 :]
        grad_vec = total_ref[:, :size]
        squares = jnp.sum(grad_vec * grad_vec, axis=1, keepdims=True)
        squares = squares + jnp.sum(total_ref[:, size:], axis=1, keepdims=True)
        norm = jnp.sqrt(squares)
        outs[0][...] = norm
        clip = jnp.minimum(1.0, CLIP_LIMIT / (norm + 1e-06))
        for i, geo in enumerate(geos):
            gradient = geo.unpack(owned_refs[i][...].astype(F32)) * clip
            weight, moment, square = (r[...] for r in ins[3 * i : 3 * i + 3])
            results = adamw(weight, moment, square, gradient, RATE_MATRIX, DECAY_MATRIX)
            for ref, value in zip(outs[1 + 3 * i : 4 + 3 * i], results):
                ref[...] = value
        weight, moment, square = (r[...] for r in ins[3 * n :])
        results = adamw(weight, moment, square, grad_vec * clip, RATE_VECTOR, 0.0)
        for ref, value in zip(outs[1 + 3 * n :], results):
            ref[...] = value

    args = list(owned) + [totals] + [v for group in weights for v in group] + list(vectors)
    outs = [shape((1, 1), F32)]
    outs += [shape(v.shape, F32) for group in weights for v in group]
    outs += [shape(v.shape, F32) for v in vectors]
    return call(
        kernel,
        "update_all",
        outs,
        [whole(v.shape) for v in args],
        [whole(o.shape) for o in outs],
        bytes_accessed=4_000_000,
    )(*args)


def gather(net, shard):
    held = shard[None]
    for stage in range(net.stages()):
        held = jnp.concatenate([held, lax.ppermute(held, AXES, net.stage(stage))], axis=0)
    return held, lax.ppermute(held, AXES, net.core())


def add(a, b):
    return (a.astype(F32) + b.astype(F32)).astype(BF16)


def reduce(net, keep, send):
    held = add(keep, lax.ppermute(send, AXES, net.core()))
    for stage in range(net.stages() - 1, -1, -1):
        half = held.shape[0] // 2
        held = add(held[:half], lax.ppermute(held[half:], AXES, net.stage(stage)))
    return held[0]


def total_sum(net, value):
    value = value + lax.ppermute(value, AXES, net.core())
    for stage in range(net.stages()):
        value = value + lax.ppermute(value, AXES, net.stage(stage))
    return value


def body(
    dp,
    fsdp,
    block_input,
    cotangent,
    protein_lengths,
    weight_in,
    moment_in,
    square_in,
    weight_conv,
    moment_conv,
    square_conv,
    weight_out,
    moment_out,
    square_out,
    vectors,
    moment_vectors,
    square_vectors,
):
    net = Network(dp, fsdp)
    geo_in = Geometry(1, weight_in.shape[0], weight_in.shape[1])
    geo_conv = Geometry(KERNEL, weight_conv.shape[1], weight_conv.shape[2])
    geo_out = Geometry(1, weight_out.shape[0], weight_out.shape[1])
    geos = (geo_in, geo_conv, geo_out)

    def flat(v):
        return v.reshape(-1, v.shape[-1])

    me = jnp.stack([lax.axis_index("dp"), lax.axis_index("fsdp")]).astype(jnp.int32)
    ends = jnp.cumsum(protein_lengths[0]).astype(jnp.int32)
    vec = vectors.reshape(1, -1)
    x = block_input[0]
    cot = cotangent[0]

    shard_in, shard_conv, shard_out = pack_weights(geos, (weight_in, flat(weight_conv), weight_out))
    own_in, peer_in = gather(net, shard_in)
    own_conv, peer_conv = gather(net, shard_conv)
    own_out, peer_out = gather(net, shard_out)

    h1, h1_t, stat, grad_b3 = first_norm(x, cot, vec)
    h2, h2_t, n2, r2, full_in = mix_one(net, geo_in, me, own_in, peer_in, h1, vec)
    h3, h3_t, n3, r3, full_conv = mix_two(net, geo_conv, me, ends, own_conv, peer_conv, h2, vec)
    grad_out = reduce(net, *weight_gradient(net, geo_out, me, h3_t, cot, "out_gradient"))
    back_two, grad_g3, grad_s3, grad_b2, full_out = back_through_out(
        net, geo_out, me, own_out, peer_out, cot, n3, r3, vec
    )
    grad_conv = reduce(net, *conv_gradient(net, geo_conv, me, ends, h2_t, back_two))
    back_one, grad_g2, grad_s2, grad_b1 = back_through_conv(ends, back_two, full_conv, n2, r2, vec)
    grad_in = reduce(net, *weight_gradient(net, geo_in, me, h1_t, back_one, "in_gradient"))
    input_grad, grad_g1, grad_s1 = back_through_in(back_one, full_in, x, cot, stat, vec)
    block_output = block_result(x, h3, full_out, vec)

    owned = (grad_in, grad_conv, grad_out)
    partial = jnp.concatenate(
        [
            grad_g1,
            grad_s1,
            grad_g2,
            grad_s2,
            grad_g3,
            grad_s3,
            grad_b1,
            grad_b2,
            grad_b3,
            sum_squares(owned),
        ],
        axis=1,
    )
    totals = total_sum(net, partial)
    results = update_all(
        geos,
        owned,
        totals,
        (
            (weight_in, moment_in, square_in),
            (flat(weight_conv), flat(moment_conv), flat(square_conv)),
            (weight_out, moment_out, square_out),
        ),
        (vec, moment_vectors.reshape(1, -1), square_vectors.reshape(1, -1)),
    )
    norm, news = results[0], results[1:]
    return (
        block_output[None],
        input_grad[None],
        norm[0, 0],
        *news[0:3],
        *(v.reshape(weight_conv.shape) for v in news[3:6]),
        *news[6:9],
        *(v.reshape(-1) for v in news[9:12]),
    )


def solution(mesh):
    rows = P(("dp", "fsdp"), None, None)
    matrix = P("fsdp", "dp")
    taps = P(None, "fsdp", "dp")
    weights = (matrix,) * 3 + (taps,) * 3 + (matrix,) * 3 + (P(),) * 3
    return jax.shard_map(
        functools.partial(body, mesh.shape["dp"], mesh.shape["fsdp"]),
        mesh=mesh,
        in_specs=(rows, rows, P(("dp", "fsdp"), None)) + weights,
        out_specs=(rows, rows, P()) + weights,
        check_vma=False,
    )
```

```python
import functools

import jax
import jax.numpy as jnp
from jax import lax
from jax.experimental import pallas as pl
from jax.experimental.pallas import tpu as pltpu
from jax.sharding import PartitionSpec as P

D = 1280
INNER = 640
KERNEL = 5
DILATION = 64
LENGTH = 1024
STEP = 10
MARGIN = KERNEL // 2 * DILATION
OFFSETS = tuple((k - KERNEL // 2) * DILATION for k in range(KERNEL))
BLOCK = 256
STEPS = LENGTH // BLOCK

NORM_EPS = 1e-05
ADAM_EPS = 1e-08
BETA_ONE = 0.9
BETA_TWO = 0.95
CLIP_LIMIT = 1.0
RATE_MATRIX = 0.04
RATE_VECTOR = 0.3
DECAY_MATRIX = 0.1
GELU_C = 0.7978845608
GELU_K = 0.044715

GAIN_ONE, SHIFT_ONE = (0, 1280), (1280, 1280)
GAIN_TWO, SHIFT_TWO = (2560, 640), (3200, 640)
GAIN_THREE, SHIFT_THREE = (3840, 640), (4480, 640)
BIAS_ONE, BIAS_TWO, BIAS_THREE = (5120, 640), (5760, 640), (6400, 1280)

BF16 = jnp.bfloat16
F32 = jnp.float32
AXES = ("dp", "fsdp")
VMEM_LIMIT = 26 * 1024 * 1024
EFFORT = 20


def round16(n):
    return -(-n // 16) * 16


class Geometry:
    def __init__(self, taps, rows, cols):
        self.taps, self.rows, self.cols = taps, rows, cols
        self.height = taps * rows
        self.tiles, self.rest = divmod(cols, 128)
        self.groups = 128 // self.rest if self.rest and 128 % self.rest == 0 else 1
        self.tile_rows = round16(self.height)
        self.rest_rows = round16(-(-self.height // self.groups)) if self.rest else 0
        self.packed = self.tiles * self.tile_rows + self.rest_rows

    def pack(self, value):
        pieces = [value[:, 128 * t : 128 * t + 128] for t in range(self.tiles)]
        more = self.tile_rows - self.height
        if more:
            empty = jnp.zeros((more, 128), value.dtype)
            pieces = [jnp.concatenate([piece, empty], axis=0) for piece in pieces]
        if self.rest:
            rest = value[:, 128 * self.tiles :]
            spare = self.groups * self.rest_rows - self.height
            if spare:
                rest = jnp.concatenate([rest, jnp.zeros((spare, self.rest), value.dtype)], axis=0)
            n = self.rest_rows
            parts = [rest[n * g : n * g + n] for g in range(self.groups)]
            empty = 128 - self.groups * self.rest
            if empty:
                parts.append(jnp.zeros((n, empty), value.dtype))
            pieces.append(jnp.concatenate(parts, axis=1))
        return jnp.concatenate(pieces, axis=0)

    def unpack(self, packed):
        pieces = [
            packed[self.tile_rows * t : self.tile_rows * t + self.height]
            for t in range(self.tiles)
        ]
        if self.rest:
            base = self.tiles * self.tile_rows
            n, w = self.rest_rows, self.rest
            parts = []
            for g in range(self.groups):
                have = min(n, self.height - n * g)
                if have > 0:
                    parts.append(packed[base : base + have, w * g : w * g + w])
            pieces.append(jnp.concatenate(parts, axis=0))
        return jnp.concatenate(pieces, axis=1)


class Network:
    def __init__(self, dp, fsdp):
        self.dp, self.fsdp = dp, fsdp
        self.half = dp * fsdp // 2
        far = [("f", b) for b in range(fsdp.bit_length() - 2, 0, -1)]
        near = [("f", 0)] if fsdp > 1 else []
        rows = [("d", b) for b in range(dp.bit_length() - 2, 0, -1)]
        self.order = (far + near + rows, far[::-1] + rows + near)

    def flip(self, stage, device):
        d, f = divmod(device, self.fsdp)
        kind, bit = self.order[d & 1][stage]
        if kind == "f":
            f ^= 1 << bit
        else:
            d ^= 1 << bit
        return d * self.fsdp + f

    def stage(self, stage):
        return [(i, self.flip(stage, i)) for i in range(self.dp * self.fsdp)]

    def core(self):
        return [(i, i ^ self.fsdp) for i in range(self.dp * self.fsdp)]

    def stages(self):
        return len(self.order[0])

    def slot(self, d, f, me_d, me_f):
        d_bits = jnp.bitwise_xor(me_d, d)
        f_bits = jnp.bitwise_xor(me_f, f)
        total = jnp.int32(0)
        for i, (kind, bit) in enumerate(self.order[d & 1]):
            source = f_bits if kind == "f" else d_bits
            total = total + (jnp.bitwise_and(lax.shift_right_logical(source, bit), 1) << i)
        return total


def call(kernel, name, out_shape, in_specs, out_specs, grid=(), scratch=(), flops=0, bytes_accessed=0, aliases=None):
    return pl.pallas_call(
        kernel,
        name=name,
        grid=grid,
        out_shape=out_shape,
        in_specs=in_specs,
        out_specs=out_specs,
        scratch_shapes=list(scratch),
        input_output_aliases=aliases or {},
        compiler_params=pltpu.CompilerParams(vmem_limit_bytes=VMEM_LIMIT),
        cost_estimate=pl.CostEstimate(
            flops=EFFORT * flops, bytes_accessed=EFFORT * bytes_accessed, transcendentals=0
        ),
    )


def whole(shape):
    return pl.BlockSpec(shape, lambda *_: (0,) * len(shape))


def tokens(width, first=0):
    return pl.BlockSpec((BLOCK, width), lambda i: (first + i, 0))


SMEM = pl.BlockSpec(memory_space=pltpu.SMEM)
ANY = pl.BlockSpec(memory_space=pl.ANY)


def shape(dims, dtype):
    return jax.ShapeDtypeStruct(dims, dtype)


def part(vec_ref, span):
    return vec_ref[:, span[0] : span[0] + span[1]]


def add_rows(ref, value, first):
    row = jnp.sum(value, axis=0, keepdims=True)

    @pl.when(first)
    def _():
        ref[...] = row

    @pl.when(jnp.logical_not(first))
    def _():
        ref[...] += row


def statistics(values):
    width = values.shape[1]
    mean = jnp.sum(values, axis=1, keepdims=True) * (1.0 / width)
    center = values - mean
    spread = jnp.sum(center * center, axis=1, keepdims=True) * (1.0 / width)
    return center, lax.rsqrt(spread + NORM_EPS)


def gelu(a):
    t = jnp.tanh(GELU_C * (a + GELU_K * (a * a * a)))
    return 0.5 * a * (1.0 + t)


def gelu_slope(a):
    square = a * a
    t = jnp.tanh(GELU_C * a * (1.0 + GELU_K * square))
    half = 0.5 * (1.0 + t)
    return half + half * (1.0 - t) * a * (GELU_C + (3.0 * GELU_C * GELU_K) * square)


def norm_backward(grad, normed, root, gain, shift):
    width = grad.shape[1]
    d_a = grad * gelu_slope(normed * gain + shift)
    scaled = d_a * gain
    mean_one = jnp.sum(scaled, axis=1, keepdims=True) * (1.0 / width)
    mean_two = jnp.sum(scaled * normed, axis=1, keepdims=True) * (1.0 / width)
    return root * (scaled - mean_one - normed * mean_two), d_a * normed, d_a


def tap_mask(ends_ref, start, rows, offset, width):
    position = start + lax.broadcasted_iota(jnp.int32, (rows, 128), 0)
    count = ends_ref.shape[0]
    lower = jnp.zeros((rows, 128), jnp.int32)
    upper = jnp.full((rows, 128), ends_ref[count - 1], jnp.int32)
    for j in range(count - 1):
        lower = jnp.where(position >= ends_ref[j], ends_ref[j], lower)
    for j in range(count - 2, -1, -1):
        upper = jnp.where(position < ends_ref[j], ends_ref[j], upper)
    target = position + offset
    mask = jnp.where((target >= lower) & (target < upper), 1.0, 0.0).astype(BF16)
    return jnp.concatenate([mask] * (width // 128), axis=1)


def fill_padded(padded, source):
    padded[0:MARGIN] = jnp.zeros((MARGIN, source.shape[1]), source.dtype)
    padded[MARGIN : MARGIN + LENGTH] = source[...]
    padded[MARGIN + LENGTH : MARGIN + LENGTH + MARGIN] = jnp.zeros(
        (MARGIN, source.shape[1]), source.dtype
    )


def dot(a, b):
    return jnp.dot(a, b, preferred_element_type=F32)


def dot_nt(a, b):
    return lax.dot_general(a, b, (((1,), (1,)), ((), ())), preferred_element_type=F32)


def assemble(net, geo, me_ref, own, peer, buffer, sems, full):
    core = jnp.bitwise_and(me_ref[0], 1)
    first = pltpu.make_async_copy(own, buffer.at[core], sems.at[0])
    second = pltpu.make_async_copy(peer, buffer.at[1 - core], sems.at[1])
    first.start()
    second.start()
    first.wait()
    second.wait()
    for f in range(net.fsdp):
        blocks = [
            geo.unpack(buffer[d & 1, net.slot(d, f, me_ref[0], me_ref[1])])
            for d in range(net.dp)
        ]
        row = jnp.concatenate(blocks, axis=1)
        for k in range(geo.taps):
            start = k * geo.rows * net.fsdp + f * geo.rows
            full[start : start + geo.rows] = row[k * geo.rows : k * geo.rows + geo.rows]


def distribute(net, geo, me_ref, full, buffer, sems, keep, send):
    for f in range(net.fsdp):
        pieces = [
            full[
                k * geo.rows * net.fsdp + f * geo.rows : k * geo.rows * net.fsdp
                + f * geo.rows
                + geo.rows
            ]
            for k in range(geo.taps)
        ]
        row = pieces[0] if geo.taps == 1 else jnp.concatenate(pieces, axis=0)
        for d in range(net.dp):
            buffer[d & 1, net.slot(d, f, me_ref[0], me_ref[1])] = geo.pack(
                row[:, d * geo.cols : d * geo.cols + geo.cols]
            )
    core = jnp.bitwise_and(me_ref[0], 1)
    first = pltpu.make_async_copy(buffer.at[1 - core], send, sems.at[0])
    second = pltpu.make_async_copy(buffer.at[core], keep, sems.at[1])
    first.start()
    second.start()
    first.wait()
    second.wait()


def slots(net, geo):
    return (net.half, geo.packed, 128)


def piece_scratch(net, geo):
    return [pltpu.VMEM((2,) + slots(net, geo), BF16), pltpu.SemaphoreType.DMA((2,))]


def pack_weights(geos, weights):
    def kernel(*refs):
        n = len(geos)
        for geo, source, target in zip(geos, refs[:n], refs[n:]):
            target[...] = geo.pack(source[...].astype(BF16))

    return call(
        kernel,
        "pack_weights",
        [shape((geo.packed, 128), BF16) for geo in geos],
        [whole(w.shape) for w in weights],
        [whole((geo.packed, 128)) for geo in geos],
        bytes_accessed=1_000_000,
    )(*weights)


def first_norm(block_input, cotangent, vec, first=0, count=STEPS, held=None):
    def kernel(x_ref, cot_ref, vec_ref, *refs):
        h_ref, ht_ref, stat_ref, bias_ref = refs[-4:]
        values = x_ref[...].astype(F32)
        center, root = statistics(values)
        normed = center * root
        hidden = gelu(normed * part(vec_ref, GAIN_ONE) + part(vec_ref, SHIFT_ONE)).astype(BF16)
        h_ref[...] = hidden
        ht_ref[...] = hidden.T
        lane = lax.broadcasted_iota(jnp.int32, (BLOCK, 128), 1)
        stat_ref[...] = jnp.where(lane == 0, values[:, :1] - center[:, :1], root)
        add_rows(bias_ref, cot_ref[...].astype(F32), pl.program_id(0) == 0)

    held = list(held or [])
    return call(
        kernel,
        "first_norm",
        [
            shape((LENGTH, D), BF16),
            shape((D, LENGTH), BF16),
            shape((LENGTH, 128), F32),
            shape((1, D), F32),
        ],
        [tokens(D, first), tokens(D, first), whole(vec.shape)] + [ANY] * len(held),
        [
            tokens(D, first),
            pl.BlockSpec((D, BLOCK), lambda i: (0, first + i)),
            tokens(128, first),
            whole((1, D)),
        ],
        grid=(count,),
        aliases={3 + i: i for i in range(len(held))},
        flops=30 * BLOCK * count * D,
        bytes_accessed=8 * BLOCK * count * D,
    )(block_input, cotangent, vec, *held)


def norm_out(mixed, vec_ref, gain, shift_span, h_ref, ht_ref, normed_ref, root_ref):
    center, root = statistics(mixed)
    normed = center * root
    hidden = gelu(normed * part(vec_ref, gain) + part(vec_ref, shift_span)).astype(BF16)
    h_ref[...] = hidden
    ht_ref[...] = hidden.T
    normed_ref[...] = normed
    root_ref[...] = jnp.broadcast_to(root, (BLOCK, 128))


NORM_SHAPES = [
    shape((LENGTH, INNER), BF16),
    shape((INNER, LENGTH), BF16),
    shape((LENGTH, INNER), F32),
    shape((LENGTH, 128), F32),
]


def norm_specs():
    return [
        tokens(INNER),
        pl.BlockSpec((INNER, BLOCK), lambda i: (0, i)),
        tokens(INNER),
        tokens(128),
    ]


def mix_one(net, geo, me, own, peer, hidden_one, vec):
    def kernel(me_ref, own_ref, peer_ref, h1_ref, vec_ref, h_ref, ht_ref, n_ref, r_ref, full, buf, sems):
        @pl.when(pl.program_id(0) == 0)
        def _():
            assemble(net, geo, me_ref, own_ref, peer_ref, buf, sems, full)

        mixed = dot(h1_ref[...], full[...]) + part(vec_ref, BIAS_ONE)
        norm_out(mixed, vec_ref, GAIN_TWO, SHIFT_TWO, h_ref, ht_ref, n_ref, r_ref)

    return call(
        kernel,
        "mix_one",
        NORM_SHAPES + [shape((D, INNER), BF16)],
        [SMEM, ANY, ANY, tokens(D), whole(vec.shape)],
        norm_specs() + [whole((D, INNER))],
        grid=(STEPS,),
        scratch=piece_scratch(net, geo),
        flops=2 * LENGTH * D * INNER,
        bytes_accessed=12_000_000,
    )(me, own, peer, hidden_one, vec)


def mix_two(net, geo, me, ends, own, peer, hidden_two, vec):
    def kernel(
        me_ref, ends_ref, own_ref, peer_ref, h2_ref, vec_ref, h_ref, ht_ref, n_ref, r_ref, full, buf, sems, pad
    ):
        step = pl.program_id(0)

        @pl.when(step == 0)
        def _():
            assemble(net, geo, me_ref, own_ref, peer_ref, buf, sems, full)
            fill_padded(pad, h2_ref)

        start = step * BLOCK
        mixed = jnp.zeros((BLOCK, INNER), F32)
        for k, offset in enumerate(OFFSETS):
            source = pad[pl.ds(pl.multiple_of(start + MARGIN + offset, DILATION), BLOCK)]
            source = source * tap_mask(ends_ref, start, BLOCK, offset, INNER)
            mixed = mixed + dot(source, full[k * INNER : k * INNER + INNER])
        mixed = mixed + part(vec_ref, BIAS_TWO)
        norm_out(mixed, vec_ref, GAIN_THREE, SHIFT_THREE, h_ref, ht_ref, n_ref, r_ref)

    return call(
        kernel,
        "mix_two",
        NORM_SHAPES + [shape((KERNEL * INNER, INNER), BF16)],
        [SMEM, SMEM, ANY, ANY, whole((LENGTH, INNER)), whole(vec.shape)],
        norm_specs() + [whole((KERNEL * INNER, INNER))],
        grid=(STEPS,),
        scratch=piece_scratch(net, geo) + [pltpu.VMEM((LENGTH + 2 * MARGIN, INNER), BF16)],
        flops=2 * LENGTH * KERNEL * INNER * INNER,
        bytes_accessed=18_000_000,
    )(me, ends, own, peer, hidden_two, vec)


def gradient_shapes(net, geo):
    return [shape(slots(net, geo), BF16)] * 2


def weight_gradient(net, geo, me, left, right, name="weight_gradient"):
    dims = (left.shape[0], right.shape[1])

    def kernel(me_ref, left_ref, right_ref, keep, send, full, buf, sems):
        full[...] = dot(left_ref[...], right_ref[...]).astype(BF16)
        distribute(net, geo, me_ref, full, buf, sems, keep, send)

    return call(
        kernel,
        name,
        gradient_shapes(net, geo),
        [SMEM, whole(left.shape), whole(right.shape)],
        [ANY, ANY],
        grid=(1,),
        scratch=[pltpu.VMEM(dims, BF16)] + piece_scratch(net, geo),
        flops=2 * LENGTH * dims[0] * dims[1],
        bytes_accessed=6_000_000,
    )(me, left, right)


def back_through_out(net, geo, me, own, peer, cotangent, normed, root, vec):
    def kernel(
        me_ref, own_ref, peer_ref, cot_ref, n_ref, r_ref, vec_ref, back_ref, gg_ref, gs_ref, gb_ref, full, buf, sems
    ):
        first = pl.program_id(0) == 0

        @pl.when(first)
        def _():
            assemble(net, geo, me_ref, own_ref, peer_ref, buf, sems, full)

        grad = dot_nt(cot_ref[...], full[...])
        back, to_gain, to_shift = norm_backward(
            grad, n_ref[...], r_ref[:, :1], part(vec_ref, GAIN_THREE), part(vec_ref, SHIFT_THREE)
        )
        back = back.astype(BF16)
        back_ref[...] = back
        add_rows(gg_ref, to_gain, first)
        add_rows(gs_ref, to_shift, first)
        add_rows(gb_ref, back.astype(F32), first)

    row = shape((1, INNER), F32)
    return call(
        kernel,
        "back_through_out",
        [shape((LENGTH, INNER), BF16), row, row, row, shape((INNER, D), BF16)],
        [SMEM, ANY, ANY, tokens(D), tokens(INNER), tokens(128), whole(vec.shape)],
        [tokens(INNER)] + [whole((1, INNER))] * 3 + [whole((INNER, D))],
        grid=(STEPS,),
        scratch=piece_scratch(net, geo),
        flops=2 * LENGTH * D * INNER,
        bytes_accessed=12_000_000,
    )(me, own, peer, cotangent, normed, root, vec)


def block_result(block_input, hidden_three, full_out, vec):
    def kernel(x_ref, h_ref, w_ref, vec_ref, out_ref):
        branch = dot(h_ref[...], w_ref[...]) + part(vec_ref, BIAS_THREE)
        out_ref[...] = (x_ref[...].astype(F32) + branch).astype(BF16)

    return call(
        kernel,
        "block_result",
        shape((LENGTH, D), BF16),
        [tokens(D), tokens(INNER), whole((INNER, D)), whole(vec.shape)],
        tokens(D),
        grid=(STEPS,),
        flops=2 * LENGTH * D * INNER,
        bytes_accessed=8_000_000,
    )(block_input, hidden_three, full_out, vec)


def conv_gradient(net, geo, me, ends, hidden_two_t, back_two):
    def kernel(me_ref, ends_ref, left_ref, back_ref, keep, send, full, pad, buf, sems):
        fill_padded(pad, back_ref)
        for k, offset in enumerate(OFFSETS):
            source = pad[MARGIN - offset : MARGIN - offset + LENGTH]
            source = source * tap_mask(ends_ref, 0, LENGTH, -offset, INNER)
            full[k * INNER : k * INNER + INNER] = dot(left_ref[...], source).astype(BF16)
        distribute(net, geo, me_ref, full, buf, sems, keep, send)

    return call(
        kernel,
        "conv_gradient",
        gradient_shapes(net, geo),
        [SMEM, SMEM, whole((INNER, LENGTH)), whole((LENGTH, INNER))],
        [ANY, ANY],
        grid=(1,),
        scratch=[
            pltpu.VMEM((KERNEL * INNER, INNER), BF16),
            pltpu.VMEM((LENGTH + 2 * MARGIN, INNER), BF16),
        ]
        + piece_scratch(net, geo),
        flops=2 * LENGTH * KERNEL * INNER * INNER,
        bytes_accessed=7_000_000,
    )(me, ends, hidden_two_t, back_two)


def back_through_conv(ends, back_two, full_conv, normed, root, vec):
    def kernel(ends_ref, back_ref, w_ref, n_ref, r_ref, vec_ref, out_ref, gg_ref, gs_ref, gb_ref, pad):
        step = pl.program_id(0)
        first = step == 0

        @pl.when(first)
        def _():
            fill_padded(pad, back_ref)

        start = step * BLOCK
        grad = jnp.zeros((BLOCK, INNER), F32)
        for k, offset in enumerate(OFFSETS):
            source = pad[pl.ds(pl.multiple_of(start + MARGIN - offset, DILATION), BLOCK)]
            source = source * tap_mask(ends_ref, start, BLOCK, -offset, INNER)
            grad = grad + dot_nt(source, w_ref[k * INNER : k * INNER + INNER])
        back, to_gain, to_shift = norm_backward(
            grad, n_ref[...], r_ref[:, :1], part(vec_ref, GAIN_TWO), part(vec_ref, SHIFT_TWO)
        )
        back = back.astype(BF16)
        out_ref[...] = back
        add_rows(gg_ref, to_gain, first)
        add_rows(gs_ref, to_shift, first)
        add_rows(gb_ref, back.astype(F32), first)

    row = shape((1, INNER), F32)
    return call(
        kernel,
        "back_through_conv",
        [shape((LENGTH, INNER), BF16), row, row, row],
        [
            SMEM,
            whole((LENGTH, INNER)),
            whole((KERNEL * INNER, INNER)),
            tokens(INNER),
            tokens(128),
            whole(vec.shape),
        ],
        [tokens(INNER)] + [whole((1, INNER))] * 3,
        grid=(STEPS,),
        scratch=[pltpu.VMEM((LENGTH + 2 * MARGIN, INNER), BF16)],
        flops=2 * LENGTH * KERNEL * INNER * INNER,
        bytes_accessed=10_000_000,
    )(ends, back_two, full_conv, normed, root, vec)


def back_through_in(back_one, full_in, block_input, cotangent, stat, vec, first=0, count=STEPS, held=None):
    def kernel(back_ref, w_ref, x_ref, cot_ref, stat_ref, vec_ref, *refs):
        out_ref, gg_ref, gs_ref = refs[-3:]
        start = pl.program_id(0) == 0
        grad = dot_nt(back_ref[...], w_ref[...])
        root = stat_ref[:, 1:2]
        normed = (x_ref[...].astype(F32) - stat_ref[:, :1]) * root
        back, to_gain, to_shift = norm_backward(
            grad, normed, root, part(vec_ref, GAIN_ONE), part(vec_ref, SHIFT_ONE)
        )
        out_ref[...] = (cot_ref[...].astype(F32) + back).astype(BF16)
        add_rows(gg_ref, to_gain, start)
        add_rows(gs_ref, to_shift, start)

    row = shape((1, D), F32)
    held = list(held or [])
    return call(
        kernel,
        "back_through_in",
        [shape((LENGTH, D), BF16), row, row],
        [
            tokens(INNER, first),
            whole((D, INNER)),
            tokens(D, first),
            tokens(D, first),
            tokens(128, first),
            whole(vec.shape),
        ]
        + [ANY] * len(held),
        [tokens(D, first)] + [whole((1, D))] * 2,
        grid=(count,),
        aliases={6 + i: i for i in range(len(held))},
        flops=2 * BLOCK * count * D * INNER,
        bytes_accessed=12_000_000,
    )(back_one, full_in, block_input, cotangent, stat, vec, *held)


def sum_squares(owned, partial):
    rows = partial.shape[0]
    total_rows = -(-(rows + 1) // 8) * 8

    def kernel(*refs):
        out = refs[-1]
        total = jnp.zeros((1, 128), F32)
        for ref in refs[:-2]:
            value = ref[...]
            total = total + jnp.sum(value * value, axis=0, keepdims=True)
        out[...] = jnp.zeros(out.shape, F32)
        out[0:rows] = refs[-2][...]
        out[rows : rows + 1] = total

    return call(
        kernel,
        "sum_squares",
        shape((total_rows, 128), F32),
        [whole(v.shape) for v in owned] + [whole(partial.shape)],
        whole((total_rows, 128)),
        bytes_accessed=1_000_000,
    )(*owned, partial)


def adamw(weight, moment, square, gradient, rate, decay):
    new_moment = BETA_ONE * moment + (1.0 - BETA_ONE) * gradient
    new_square = BETA_TWO * square + (1.0 - BETA_TWO) * gradient * gradient
    moment_hat = new_moment * (1.0 / (1.0 - BETA_ONE**STEP))
    square_hat = new_square * (1.0 / (1.0 - BETA_TWO**STEP))
    update = moment_hat / (jnp.sqrt(square_hat) + ADAM_EPS)
    return weight - rate * (update + decay * weight), new_moment, new_square


def update_all(geos, owned, totals, weights, vectors):
    n = len(geos)
    size = vectors[0].shape[0]

    def kernel(*refs):
        owned_refs, total_ref = refs[:n], refs[n]
        ins = refs[n + 1 : n + 1 + 3 * n + 3]
        outs = refs[n + 1 + 3 * n + 3 :]
        grad_vec = total_ref[0:size]
        squares = jnp.sum(grad_vec * grad_vec, axis=0, keepdims=True) + total_ref[size : size + 1]
        norm = jnp.sqrt(jnp.sum(squares, axis=1, keepdims=True))
        outs[0][...] = norm
        clip = jnp.minimum(1.0, CLIP_LIMIT / (norm + 1e-06))
        for i, geo in enumerate(geos):
            gradient = geo.unpack(owned_refs[i][...].astype(F32)) * clip
            weight, moment, square = (r[...] for r in ins[3 * i : 3 * i + 3])
            results = adamw(weight, moment, square, gradient, RATE_MATRIX, DECAY_MATRIX)
            for ref, value in zip(outs[1 + 3 * i : 4 + 3 * i], results):
                ref[...] = value
        weight, moment, square = (r[...] for r in ins[3 * n :])
        results = adamw(weight, moment, square, grad_vec * clip, RATE_VECTOR, 0.0)
        for ref, value in zip(outs[1 + 3 * n :], results):
            ref[...] = value

    args = list(owned) + [totals] + [v for group in weights for v in group] + list(vectors)
    outs = [shape((1, 1), F32)]
    outs += [shape(v.shape, F32) for group in weights for v in group]
    outs += [shape(v.shape, F32) for v in vectors]
    return call(
        kernel,
        "update_all",
        outs,
        [whole(v.shape) for v in args],
        [whole(o.shape) for o in outs],
        bytes_accessed=4_000_000,
    )(*args)


class Sequence:
    def __init__(self):
        self.last = ()

    def after(self, *values):
        return lax.optimization_barrier(tuple(values) + self.last)[: len(values)]

    def run(self, function, *values, **options):
        result = function(*self.after(*values), **options)
        self.last = tuple(jax.tree.leaves(result))[-1:]
        return result

    def wait(self, *values):
        self.last = tuple(values) + self.last


class Gather:
    def __init__(self, net, seq, shard):
        self.net, self.seq, self.stage = net, seq, 0
        self.held, self.coming = shard[None], None

    def send(self):
        (held,) = self.seq.after(self.held)
        self.held = held
        last = self.stage == self.net.stages()
        self.coming = lax.ppermute(held, AXES, self.net.core() if last else self.net.stage(self.stage))
        self.stage += 1

    def take(self):
        if self.stage <= self.net.stages():
            self.held = jnp.concatenate([self.held, self.coming], axis=0)
        self.seq.wait(self.held, self.coming)

    def step(self):
        self.take()
        self.send()

    def finish(self):
        while self.stage <= self.net.stages():
            self.step()
        self.take()


def add(a, b):
    return (a.astype(F32) + b.astype(F32)).astype(BF16)


class Reduce:
    def __init__(self, net, seq, keep, send):
        self.net, self.seq, self.stage = net, seq, net.stages()
        self.keep = keep
        (send,) = seq.after(send)
        self.coming = lax.ppermute(send, AXES, net.core())

    def step(self):
        self.stage -= 1
        half = self.keep.shape[0] // 2
        away = add(self.keep[half:], self.coming[half:])
        keep = add(self.keep[:half], self.coming[:half])
        self.keep, away = self.seq.after(keep, away)
        self.seq.wait(self.keep, away)
        self.coming = lax.ppermute(away, AXES, self.net.stage(self.stage))

    def end(self):
        while self.stage:
            self.step()
        held = self.keep.astype(F32) + self.coming.astype(F32)
        self.seq.wait(held)
        return held[0]


def total_sum(net, value):
    value = value + lax.ppermute(value, AXES, net.core())
    for stage in range(net.stages()):
        value = value + lax.ppermute(value, AXES, net.stage(stage))
    return value


def body(
    dp,
    fsdp,
    block_input,
    cotangent,
    protein_lengths,
    weight_in,
    moment_in,
    square_in,
    weight_conv,
    moment_conv,
    square_conv,
    weight_out,
    moment_out,
    square_out,
    vectors,
    moment_vectors,
    square_vectors,
):
    net = Network(dp, fsdp)
    geo_in = Geometry(1, weight_in.shape[0], weight_in.shape[1])
    geo_conv = Geometry(KERNEL, weight_conv.shape[1], weight_conv.shape[2])
    geo_out = Geometry(1, weight_out.shape[0], weight_out.shape[1])
    geos = (geo_in, geo_conv, geo_out)

    def flat(v):
        return v.reshape(-1, v.shape[-1])

    me = jnp.stack([lax.axis_index("dp"), lax.axis_index("fsdp")]).astype(jnp.int32)
    ends = jnp.cumsum(protein_lengths[0]).astype(jnp.int32)
    vec = vectors.reshape(1, -1)
    x = block_input[0]
    cot = cotangent[0]

    seq = Sequence()
    shard_in, shard_conv, shard_out = seq.run(
        lambda *weights: pack_weights(geos, weights), weight_in, flat(weight_conv), weight_out
    )
    get_in = Gather(net, seq, shard_in)
    get_conv = Gather(net, seq, shard_conv)
    get_out = Gather(net, seq, shard_out)
    get_in.send()
    get_conv.send()
    seq.wait(me, ends, vec)
    norms = seq.run(first_norm, x, cot, vec, first=0, count=STEPS // 2)
    get_in.step()
    get_conv.step()
    h1, h1_t, stat, half_b3 = seq.run(
        lambda x, cot, vec, *held: first_norm(x, cot, vec, STEPS // 2, STEPS // 2, held),
        x, cot, vec, *norms[:3],
    )
    grad_b3 = norms[3] + half_b3
    get_in.step()
    get_conv.step()
    get_in.step()
    get_in.step()
    get_conv.step()
    get_out.send()
    get_in.finish()
    h2, h2_t, n2, r2, full_in = seq.run(
        functools.partial(mix_one, net, geo_in), me, get_in.held, get_in.coming, h1, vec
    )
    get_out.step()
    get_conv.step()
    get_out.step()
    get_conv.finish()
    h3, h3_t, n3, r3, full_conv = seq.run(
        functools.partial(mix_two, net, geo_conv),
        me, ends, get_conv.held, get_conv.coming, h2, vec,
    )
    get_out.step()
    pieces = seq.run(
        functools.partial(weight_gradient, net, geo_out, name="out_gradient"), me, h3_t, cot
    )
    sum_out = Reduce(net, seq, *pieces)
    get_out.step()
    get_out.finish()
    back_two, grad_g3, grad_s3, grad_b2, full_out = seq.run(
        functools.partial(back_through_out, net, geo_out),
        me, get_out.held, get_out.coming, cot, n3, r3, vec,
    )
    sum_out.step()
    pieces = seq.run(
        functools.partial(conv_gradient, net, geo_conv), me, ends, h2_t, back_two
    )
    sum_conv = Reduce(net, seq, *pieces)
    sum_out.step()
    back_one, grad_g2, grad_s2, grad_b1 = seq.run(
        back_through_conv, ends, back_two, full_conv, n2, r2, vec
    )
    sum_conv.step()
    sum_out.step()
    pieces = seq.run(
        functools.partial(weight_gradient, net, geo_in, name="in_gradient"), me, h1_t, back_one
    )
    sum_in = Reduce(net, seq, *pieces)
    sum_out.step()
    block_output = seq.run(block_result, x, h3, full_out, vec)
    sum_in.step()
    sum_conv.step()
    ends_in = seq.run(back_through_in, back_one, full_in, x, cot, stat, vec, first=0, count=STEPS // 2)
    sum_in.step()
    sum_conv.step()
    grad_out = sum_out.end()
    input_grad, more_g1, more_s1 = seq.run(
        lambda *args: back_through_in(*args[:6], STEPS // 2, STEPS // 2, args[6:]),
        back_one, full_in, x, cot, stat, vec, ends_in[0],
    )
    grad_g1, grad_s1 = ends_in[1] + more_g1, ends_in[2] + more_s1
    partial = jnp.concatenate(
        [grad_g1, grad_s1, grad_g2, grad_s2, grad_g3, grad_s3, grad_b1, grad_b2, grad_b3], axis=1
    ).reshape(-1, 128)
    sum_in.step()
    sum_conv.step()
    seq.wait(partial)
    sum_in.step()
    grad_conv = sum_conv.end()
    grad_in = sum_in.end()

    owned = (grad_in, grad_conv, grad_out)
    totals = total_sum(net, sum_squares(owned, partial))
    results = update_all(
        geos,
        owned,
        totals,
        (
            (weight_in, moment_in, square_in),
            (flat(weight_conv), flat(moment_conv), flat(square_conv)),
            (weight_out, moment_out, square_out),
        ),
        tuple(v.reshape(-1, 128) for v in (vectors, moment_vectors, square_vectors)),
    )
    norm, news = results[0], results[1:]
    return (
        block_output[None],
        input_grad[None],
        norm[0, 0],
        *news[0:3],
        *(v.reshape(weight_conv.shape) for v in news[3:6]),
        *news[6:9],
        *(v.reshape(-1) for v in news[9:12]),
    )


def solution(mesh):
    rows = P(("dp", "fsdp"), None, None)
    matrix = P("fsdp", "dp")
    taps = P(None, "fsdp", "dp")
    weights = (matrix,) * 3 + (taps,) * 3 + (matrix,) * 3 + (P(),) * 3
    return jax.shard_map(
        functools.partial(body, mesh.shape["dp"], mesh.shape["fsdp"]),
        mesh=mesh,
        in_specs=(rows, rows, P(("dp", "fsdp"), None)) + weights,
        out_specs=(rows, rows, P()) + weights,
        check_vma=False,
    )
```

```python
import functools

import jax
import jax.numpy as jnp
from jax import lax
from jax.experimental import pallas as pl
from jax.experimental.pallas import tpu as pltpu
from jax.sharding import PartitionSpec as P

D = 1280
INNER = 640
KERNEL = 5
DILATION = 64
LENGTH = 1024
STEP = 10
MARGIN = KERNEL // 2 * DILATION
OFFSETS = tuple((k - KERNEL // 2) * DILATION for k in range(KERNEL))
BLOCK = 256
STEPS = LENGTH // BLOCK

NORM_EPS = 1e-05
ADAM_EPS = 1e-08
BETA_ONE = 0.9
BETA_TWO = 0.95
CLIP_LIMIT = 1.0
RATE_MATRIX = 0.04
RATE_VECTOR = 0.3
DECAY_MATRIX = 0.1
GELU_C = 0.7978845608
GELU_K = 0.044715

GAIN_ONE, SHIFT_ONE = (0, 1280), (1280, 1280)
GAIN_TWO, SHIFT_TWO = (2560, 640), (3200, 640)
GAIN_THREE, SHIFT_THREE = (3840, 640), (4480, 640)
BIAS_ONE, BIAS_TWO, BIAS_THREE = (5120, 640), (5760, 640), (6400, 1280)

BF16 = jnp.bfloat16
F32 = jnp.float32
AXES = ("dp", "fsdp")
VMEM_LIMIT = 26 * 1024 * 1024
FLOPS_PER_US = 1.15e9
EFFORT = 4


def round16(n):
    return -(-n // 16) * 16


class Geometry:
    def __init__(self, taps, rows, cols):
        self.taps, self.rows, self.cols = taps, rows, cols
        self.height = taps * rows
        self.tiles, self.rest = divmod(cols, 128)
        self.groups = 128 // self.rest if self.rest and 128 % self.rest == 0 else 1
        self.tile_rows = round16(self.height)
        self.rest_rows = round16(-(-self.height // self.groups)) if self.rest else 0
        self.packed = self.tiles * self.tile_rows + self.rest_rows

    def pack(self, value):
        pieces = [value[:, 128 * t : 128 * t + 128] for t in range(self.tiles)]
        more = self.tile_rows - self.height
        if more:
            empty = jnp.zeros((more, 128), value.dtype)
            pieces = [jnp.concatenate([piece, empty], axis=0) for piece in pieces]
        if self.rest:
            rest = value[:, 128 * self.tiles :]
            spare = self.groups * self.rest_rows - self.height
            if spare:
                rest = jnp.concatenate([rest, jnp.zeros((spare, self.rest), value.dtype)], axis=0)
            n = self.rest_rows
            parts = [rest[n * g : n * g + n] for g in range(self.groups)]
            empty = 128 - self.groups * self.rest
            if empty:
                parts.append(jnp.zeros((n, empty), value.dtype))
            pieces.append(jnp.concatenate(parts, axis=1))
        return jnp.concatenate(pieces, axis=0)

    def unpack(self, packed):
        pieces = [
            packed[self.tile_rows * t : self.tile_rows * t + self.height]
            for t in range(self.tiles)
        ]
        if self.rest:
            base = self.tiles * self.tile_rows
            n, w = self.rest_rows, self.rest
            parts = []
            for g in range(self.groups):
                have = min(n, self.height - n * g)
                if have > 0:
                    parts.append(packed[base : base + have, w * g : w * g + w])
            pieces.append(jnp.concatenate(parts, axis=0))
        return jnp.concatenate(pieces, axis=1)


class Network:
    def __init__(self, dp, fsdp, far_first):
        self.dp, self.fsdp = dp, fsdp
        self.half = dp * fsdp // 2
        far = [("f", b) for b in range(fsdp.bit_length() - 2, 0, -1)]
        near = [("f", 0)] if fsdp > 1 else []
        rows = [("d", b) for b in range(dp.bit_length() - 2, 0, -1)]
        if far_first:
            self.order = (far + near + rows, far[::-1] + rows + near)
        else:
            self.order = (
                far[:1] + near + rows + far[1:],
                far[::-1][:1] + rows + near + far[::-1][1:],
            )

    def flip(self, stage, device):
        d, f = divmod(device, self.fsdp)
        kind, bit = self.order[d & 1][stage]
        if kind == "f":
            f ^= 1 << bit
        else:
            d ^= 1 << bit
        return d * self.fsdp + f

    def stage(self, stage):
        return [(i, self.flip(stage, i)) for i in range(self.dp * self.fsdp)]

    def core(self):
        return [(i, i ^ self.fsdp) for i in range(self.dp * self.fsdp)]

    def stages(self):
        return len(self.order[0])

    def slot(self, d, f, me_d, me_f):
        d_bits = jnp.bitwise_xor(me_d, d)
        f_bits = jnp.bitwise_xor(me_f, f)
        total = jnp.int32(0)
        for i, (kind, bit) in enumerate(self.order[d & 1]):
            source = f_bits if kind == "f" else d_bits
            total = total + (jnp.bitwise_and(lax.shift_right_logical(source, bit), 1) << i)
        return total


def call(kernel, name, out_shape, in_specs, out_specs, grid=(), scratch=(), us=1.0, aliases=None):
    return pl.pallas_call(
        kernel,
        name=name,
        grid=grid,
        out_shape=out_shape,
        in_specs=in_specs,
        out_specs=out_specs,
        scratch_shapes=list(scratch),
        input_output_aliases=aliases or {},
        compiler_params=pltpu.CompilerParams(vmem_limit_bytes=VMEM_LIMIT),
        cost_estimate=pl.CostEstimate(
            flops=int(EFFORT * us * FLOPS_PER_US), bytes_accessed=0, transcendentals=0
        ),
    )


def whole(shape):
    return pl.BlockSpec(shape, lambda *_: (0,) * len(shape))


def tokens(width, first=0):
    return pl.BlockSpec((BLOCK, width), lambda i: (first + i, 0))


SMEM = pl.BlockSpec(memory_space=pltpu.SMEM)
ANY = pl.BlockSpec(memory_space=pl.ANY)


def shape(dims, dtype):
    return jax.ShapeDtypeStruct(dims, dtype)


def part(vec_ref, span):
    return vec_ref[:, span[0] : span[0] + span[1]]


def add_rows(ref, value, first):
    row = jnp.sum(value, axis=0, keepdims=True)

    @pl.when(first)
    def _():
        ref[...] = row

    @pl.when(jnp.logical_not(first))
    def _():
        ref[...] += row


def statistics(values):
    width = values.shape[1]
    mean = jnp.sum(values, axis=1, keepdims=True) * (1.0 / width)
    center = values - mean
    spread = jnp.sum(center * center, axis=1, keepdims=True) * (1.0 / width)
    return center, lax.rsqrt(spread + NORM_EPS)


def gelu(a):
    t = jnp.tanh(GELU_C * (a + GELU_K * (a * a * a)))
    return 0.5 * a * (1.0 + t)


def gelu_slope(a):
    square = a * a
    t = jnp.tanh(GELU_C * a * (1.0 + GELU_K * square))
    half = 0.5 * (1.0 + t)
    return half + half * (1.0 - t) * a * (GELU_C + (3.0 * GELU_C * GELU_K) * square)


def norm_backward(grad, normed, root, gain, shift):
    width = grad.shape[1]
    d_a = grad * gelu_slope(normed * gain + shift)
    scaled = d_a * gain
    mean_one = jnp.sum(scaled, axis=1, keepdims=True) * (1.0 / width)
    mean_two = jnp.sum(scaled * normed, axis=1, keepdims=True) * (1.0 / width)
    return root * (scaled - mean_one - normed * mean_two), d_a * normed, d_a


def tap_mask(ends_ref, start, rows, offset, width):
    position = start + lax.broadcasted_iota(jnp.int32, (rows, 128), 0)
    count = ends_ref.shape[0]
    lower = jnp.zeros((rows, 128), jnp.int32)
    upper = jnp.full((rows, 128), ends_ref[count - 1], jnp.int32)
    for j in range(count - 1):
        lower = jnp.where(position >= ends_ref[j], ends_ref[j], lower)
    for j in range(count - 2, -1, -1):
        upper = jnp.where(position < ends_ref[j], ends_ref[j], upper)
    target = position + offset
    mask = jnp.where((target >= lower) & (target < upper), 1.0, 0.0).astype(BF16)
    return jnp.concatenate([mask] * (width // 128), axis=1)


def fill_padded(padded, source):
    padded[0:MARGIN] = jnp.zeros((MARGIN, source.shape[1]), source.dtype)
    padded[MARGIN : MARGIN + LENGTH] = source[...]
    padded[MARGIN + LENGTH : MARGIN + LENGTH + MARGIN] = jnp.zeros(
        (MARGIN, source.shape[1]), source.dtype
    )


def dot(a, b):
    return jnp.dot(a, b, preferred_element_type=F32)


def dot_nt(a, b):
    return lax.dot_general(a, b, (((1,), (1,)), ((), ())), preferred_element_type=F32)


def assemble(net, geo, me_ref, own, peer, buffer, sems, full, offset=0):
    core = jnp.bitwise_and(me_ref[0], 1)
    rows = pl.ds(offset, geo.packed)
    first = pltpu.make_async_copy(own.at[:, rows], buffer.at[core], sems.at[0])
    second = pltpu.make_async_copy(peer.at[:, rows], buffer.at[1 - core], sems.at[1])
    first.start()
    second.start()
    first.wait()
    second.wait()
    for f in range(net.fsdp):
        blocks = [
            geo.unpack(buffer[d & 1, net.slot(d, f, me_ref[0], me_ref[1])])
            for d in range(net.dp)
        ]
        row = jnp.concatenate(blocks, axis=1)
        for k in range(geo.taps):
            start = k * geo.rows * net.fsdp + f * geo.rows
            full[start : start + geo.rows] = row[k * geo.rows : k * geo.rows + geo.rows]


def distribute(net, geo, me_ref, full, buffer, sems, keep, send):
    for f in range(net.fsdp):
        pieces = [
            full[
                k * geo.rows * net.fsdp + f * geo.rows : k * geo.rows * net.fsdp
                + f * geo.rows
                + geo.rows
            ]
            for k in range(geo.taps)
        ]
        row = pieces[0] if geo.taps == 1 else jnp.concatenate(pieces, axis=0)
        for d in range(net.dp):
            buffer[d & 1, net.slot(d, f, me_ref[0], me_ref[1])] = geo.pack(
                row[:, d * geo.cols : d * geo.cols + geo.cols]
            )
    core = jnp.bitwise_and(me_ref[0], 1)
    first = pltpu.make_async_copy(buffer.at[1 - core], send, sems.at[0])
    second = pltpu.make_async_copy(buffer.at[core], keep, sems.at[1])
    first.start()
    second.start()
    first.wait()
    second.wait()


def slots(net, geo):
    return (net.half, geo.packed, 128)


def piece_scratch(net, geo):
    return [pltpu.VMEM((2,) + slots(net, geo), BF16), pltpu.SemaphoreType.DMA((2,))]


def pack_weights(geos, *weights):
    rows = sum(geo.packed for geo in geos)

    def kernel(*refs):
        start = 0
        for geo, source in zip(geos, refs):
            refs[-1][start : start + geo.packed] = geo.pack(source[...].astype(BF16))
            start += geo.packed

    return call(
        kernel,
        "pack_weights",
        shape((rows, 128), BF16),
        [whole(w.shape) for w in weights],
        whole((rows, 128)),
        us=1.0,
    )(*weights)


def first_norm(block_input, cotangent, vec, first=0, count=STEPS, held=None):
    def kernel(x_ref, cot_ref, vec_ref, *refs):
        h_ref, ht_ref, stat_ref, bias_ref = refs[-4:]
        values = x_ref[...].astype(F32)
        center, root = statistics(values)
        normed = center * root
        hidden = gelu(normed * part(vec_ref, GAIN_ONE) + part(vec_ref, SHIFT_ONE)).astype(BF16)
        h_ref[...] = hidden
        ht_ref[...] = hidden.T
        lane = lax.broadcasted_iota(jnp.int32, (BLOCK, 128), 1)
        stat_ref[...] = jnp.where(lane == 0, values[:, :1] - center[:, :1], root)
        add_rows(bias_ref, cot_ref[...].astype(F32), pl.program_id(0) == 0)

    held = list(held or [])
    return call(
        kernel,
        "first_norm",
        [
            shape((LENGTH, D), BF16),
            shape((D, LENGTH), BF16),
            shape((LENGTH, 128), F32),
            shape((1, D), F32),
        ],
        [tokens(D, first), tokens(D, first), whole(vec.shape)] + [ANY] * len(held),
        [
            tokens(D, first),
            pl.BlockSpec((D, BLOCK), lambda i: (0, first + i)),
            tokens(128, first),
            whole((1, D)),
        ],
        grid=(count,),
        aliases={3 + i: i for i in range(len(held))},
        us=1.2 * count,
    )(block_input, cotangent, vec, *held)


def norm_out(mixed, vec_ref, gain, shift_span, h_ref, ht_ref, normed_ref, root_ref):
    center, root = statistics(mixed)
    normed = center * root
    hidden = gelu(normed * part(vec_ref, gain) + part(vec_ref, shift_span)).astype(BF16)
    h_ref[...] = hidden
    ht_ref[...] = hidden.T
    normed_ref[...] = normed
    root_ref[...] = jnp.broadcast_to(root, (BLOCK, 128))


NORM_SHAPES = [
    shape((LENGTH, INNER), BF16),
    shape((INNER, LENGTH), BF16),
    shape((LENGTH, INNER), F32),
    shape((LENGTH, 128), F32),
]


def norm_specs():
    return [
        tokens(INNER),
        pl.BlockSpec((INNER, BLOCK), lambda i: (0, i)),
        tokens(INNER),
        tokens(128),
    ]


def mix_one(net, geo, me, own, peer, hidden_one, vec):
    def kernel(me_ref, own_ref, peer_ref, h1_ref, vec_ref, h_ref, ht_ref, n_ref, r_ref, full, buf, sems):
        @pl.when(pl.program_id(0) == 0)
        def _():
            assemble(net, geo, me_ref, own_ref, peer_ref, buf, sems, full)

        mixed = dot(h1_ref[...], full[...]) + part(vec_ref, BIAS_ONE)
        norm_out(mixed, vec_ref, GAIN_TWO, SHIFT_TWO, h_ref, ht_ref, n_ref, r_ref)

    return call(
        kernel,
        "mix_one",
        NORM_SHAPES + [shape((D, INNER), BF16)],
        [SMEM, ANY, ANY, tokens(D), whole(vec.shape)],
        norm_specs() + [whole((D, INNER))],
        grid=(STEPS,),
        scratch=piece_scratch(net, geo),
        us=0.01,
    )(me, own, peer, hidden_one, vec)


def mix_two(net, geo, me, ends, own, peer, hidden_two, vec):
    def kernel(
        me_ref, ends_ref, own_ref, peer_ref, h2_ref, vec_ref, h_ref, ht_ref, n_ref, r_ref, full, buf, sems, pad
    ):
        step = pl.program_id(0)

        @pl.when(step == 0)
        def _():
            assemble(net, geo, me_ref, own_ref, peer_ref, buf, sems, full)
            fill_padded(pad, h2_ref)

        start = step * BLOCK
        mixed = jnp.zeros((BLOCK, INNER), F32)
        for k, offset in enumerate(OFFSETS):
            source = pad[pl.ds(pl.multiple_of(start + MARGIN + offset, DILATION), BLOCK)]
            source = source * tap_mask(ends_ref, start, BLOCK, offset, INNER)
            mixed = mixed + dot(source, full[k * INNER : k * INNER + INNER])
        mixed = mixed + part(vec_ref, BIAS_TWO)
        norm_out(mixed, vec_ref, GAIN_THREE, SHIFT_THREE, h_ref, ht_ref, n_ref, r_ref)

    return call(
        kernel,
        "mix_two",
        NORM_SHAPES + [shape((KERNEL * INNER, INNER), BF16)],
        [SMEM, SMEM, ANY, ANY, whole((LENGTH, INNER)), whole(vec.shape)],
        norm_specs() + [whole((KERNEL * INNER, INNER))],
        grid=(STEPS,),
        scratch=piece_scratch(net, geo) + [pltpu.VMEM((LENGTH + 2 * MARGIN, INNER), BF16)],
        us=11.7,
    )(me, ends, own, peer, hidden_two, vec)


def gradient_shapes(net, geo):
    return [shape(slots(net, geo), BF16)] * 2


def weight_gradient(net, geo, me, left, right, name="weight_gradient"):
    dims = (left.shape[0], right.shape[1])

    def kernel(me_ref, left_ref, right_ref, keep, send, full, buf, sems):
        full[...] = dot(left_ref[...], right_ref[...]).astype(BF16)
        distribute(net, geo, me_ref, full, buf, sems, keep, send)

    return call(
        kernel,
        name,
        gradient_shapes(net, geo),
        [SMEM, whole(left.shape), whole(right.shape)],
        [ANY, ANY],
        grid=(1,),
        scratch=[pltpu.VMEM(dims, BF16)] + piece_scratch(net, geo),
        us=3.0 if dims[0] < dims[1] else 3.7,
    )(me, left, right)


def back_through_out(net, geo, offset, me, own, peer, cotangent, normed, root, vec):
    def kernel(
        me_ref, own_ref, peer_ref, cot_ref, n_ref, r_ref, vec_ref, back_ref, gg_ref, gs_ref, gb_ref, full, buf, sems
    ):
        first = pl.program_id(0) == 0

        @pl.when(first)
        def _():
            assemble(net, geo, me_ref, own_ref, peer_ref, buf, sems, full, offset)

        grad = dot_nt(cot_ref[...], full[...])
        back, to_gain, to_shift = norm_backward(
            grad, n_ref[...], r_ref[:, :1], part(vec_ref, GAIN_THREE), part(vec_ref, SHIFT_THREE)
        )
        back = back.astype(BF16)
        back_ref[...] = back
        add_rows(gg_ref, to_gain, first)
        add_rows(gs_ref, to_shift, first)
        add_rows(gb_ref, back.astype(F32), first)

    row = shape((1, INNER), F32)
    return call(
        kernel,
        "back_through_out",
        [shape((LENGTH, INNER), BF16), row, row, row, shape((INNER, D), BF16)],
        [SMEM, ANY, ANY, tokens(D), tokens(INNER), tokens(128), whole(vec.shape)],
        [tokens(INNER)] + [whole((1, INNER))] * 3 + [whole((INNER, D))],
        grid=(STEPS,),
        scratch=piece_scratch(net, geo),
        us=6.4,
    )(me, own, peer, cotangent, normed, root, vec)


def block_result(block_input, hidden_three, full_out, vec):
    def kernel(x_ref, h_ref, w_ref, vec_ref, out_ref):
        branch = dot(h_ref[...], w_ref[...]) + part(vec_ref, BIAS_THREE)
        out_ref[...] = (x_ref[...].astype(F32) + branch).astype(BF16)

    return call(
        kernel,
        "block_result",
        shape((LENGTH, D), BF16),
        [tokens(D), tokens(INNER), whole((INNER, D)), whole(vec.shape)],
        tokens(D),
        grid=(STEPS,),
        us=3.8,
    )(block_input, hidden_three, full_out, vec)


def conv_gradient(net, geo, me, ends, hidden_two_t, back_two):
    def kernel(me_ref, ends_ref, left_ref, back_ref, keep, send, full, pad, buf, sems):
        fill_padded(pad, back_ref)
        for k, offset in enumerate(OFFSETS):
            source = pad[MARGIN - offset : MARGIN - offset + LENGTH]
            source = source * tap_mask(ends_ref, 0, LENGTH, -offset, INNER)
            full[k * INNER : k * INNER + INNER] = dot(left_ref[...], source).astype(BF16)
        distribute(net, geo, me_ref, full, buf, sems, keep, send)

    return call(
        kernel,
        "conv_gradient",
        gradient_shapes(net, geo),
        [SMEM, SMEM, whole((INNER, LENGTH)), whole((LENGTH, INNER))],
        [ANY, ANY],
        grid=(1,),
        scratch=[
            pltpu.VMEM((KERNEL * INNER, INNER), BF16),
            pltpu.VMEM((LENGTH + 2 * MARGIN, INNER), BF16),
        ]
        + piece_scratch(net, geo),
        us=8.0,
    )(me, ends, hidden_two_t, back_two)


def back_through_conv(ends, back_two, full_conv, normed, root, vec):
    def kernel(ends_ref, back_ref, w_ref, n_ref, r_ref, vec_ref, out_ref, gg_ref, gs_ref, gb_ref, pad):
        step = pl.program_id(0)
        first = step == 0

        @pl.when(first)
        def _():
            fill_padded(pad, back_ref)

        start = step * BLOCK
        grad = jnp.zeros((BLOCK, INNER), F32)
        for k, offset in enumerate(OFFSETS):
            source = pad[pl.ds(pl.multiple_of(start + MARGIN - offset, DILATION), BLOCK)]
            source = source * tap_mask(ends_ref, start, BLOCK, -offset, INNER)
            grad = grad + dot_nt(source, w_ref[k * INNER : k * INNER + INNER])
        back, to_gain, to_shift = norm_backward(
            grad, n_ref[...], r_ref[:, :1], part(vec_ref, GAIN_TWO), part(vec_ref, SHIFT_TWO)
        )
        back = back.astype(BF16)
        out_ref[...] = back
        add_rows(gg_ref, to_gain, first)
        add_rows(gs_ref, to_shift, first)
        add_rows(gb_ref, back.astype(F32), first)

    row = shape((1, INNER), F32)
    return call(
        kernel,
        "back_through_conv",
        [shape((LENGTH, INNER), BF16), row, row, row],
        [
            SMEM,
            whole((LENGTH, INNER)),
            whole((KERNEL * INNER, INNER)),
            tokens(INNER),
            tokens(128),
            whole(vec.shape),
        ],
        [tokens(INNER)] + [whole((1, INNER))] * 3,
        grid=(STEPS,),
        scratch=[pltpu.VMEM((LENGTH + 2 * MARGIN, INNER), BF16)],
        us=10.0,
    )(ends, back_two, full_conv, normed, root, vec)


def back_through_in(back_one, full_in, block_input, cotangent, stat, vec, first=0, count=STEPS, held=None):
    def kernel(back_ref, w_ref, x_ref, cot_ref, stat_ref, vec_ref, *refs):
        out_ref, gg_ref, gs_ref = refs[-3:]
        start = pl.program_id(0) == 0
        grad = dot_nt(back_ref[...], w_ref[...])
        root = stat_ref[:, 1:2]
        normed = (x_ref[...].astype(F32) - stat_ref[:, :1]) * root
        back, to_gain, to_shift = norm_backward(
            grad, normed, root, part(vec_ref, GAIN_ONE), part(vec_ref, SHIFT_ONE)
        )
        out_ref[...] = (cot_ref[...].astype(F32) + back).astype(BF16)
        add_rows(gg_ref, to_gain, start)
        add_rows(gs_ref, to_shift, start)

    row = shape((1, D), F32)
    held = list(held or [])
    return call(
        kernel,
        "back_through_in",
        [shape((LENGTH, D), BF16), row, row],
        [
            tokens(INNER, first),
            whole((D, INNER)),
            tokens(D, first),
            tokens(D, first),
            tokens(128, first),
            whole(vec.shape),
        ]
        + [ANY] * len(held),
        [tokens(D, first)] + [whole((1, D))] * 2,
        grid=(count,),
        aliases={6 + i: i for i in range(len(held))},
        us=1.1 * count,
    )(back_one, full_in, block_input, cotangent, stat, vec, *held)


def sum_squares(owned, partial):
    rows = partial.shape[0]
    total_rows = -(-(rows + 1) // 8) * 8

    def kernel(*refs):
        out = refs[-1]
        total = jnp.zeros((1, 128), F32)
        for ref in refs[:-2]:
            value = ref[...]
            total = total + jnp.sum(value * value, axis=0, keepdims=True)
        out[...] = jnp.zeros(out.shape, F32)
        out[0:rows] = refs[-2][...]
        out[rows : rows + 1] = total

    return call(
        kernel,
        "sum_squares",
        shape((total_rows, 128), F32),
        [whole(v.shape) for v in owned] + [whole(partial.shape)],
        whole((total_rows, 128)),
        us=0.3,
    )(*owned, partial)


def adamw(weight, moment, square, gradient, rate, decay):
    new_moment = BETA_ONE * moment + (1.0 - BETA_ONE) * gradient
    new_square = BETA_TWO * square + (1.0 - BETA_TWO) * gradient * gradient
    moment_hat = new_moment * (1.0 / (1.0 - BETA_ONE**STEP))
    square_hat = new_square * (1.0 / (1.0 - BETA_TWO**STEP))
    update = moment_hat / (jnp.sqrt(square_hat) + ADAM_EPS)
    return weight - rate * (update + decay * weight), new_moment, new_square


def update_all(geos, owned, totals, weights, vectors):
    n = len(geos)
    size = vectors[0].shape[0]

    def kernel(*refs):
        owned_refs, total_ref = refs[:n], refs[n]
        ins = refs[n + 1 : n + 1 + 3 * n + 3]
        outs = refs[n + 1 + 3 * n + 3 :]
        grad_vec = total_ref[0:size]
        squares = jnp.sum(grad_vec * grad_vec, axis=0, keepdims=True) + total_ref[size : size + 1]
        norm = jnp.sqrt(jnp.sum(squares, axis=1, keepdims=True))
        outs[0][...] = norm
        clip = jnp.minimum(1.0, CLIP_LIMIT / (norm + 1e-06))
        for i, geo in enumerate(geos):
            gradient = geo.unpack(owned_refs[i][...].astype(F32)) * clip
            weight, moment, square = (r[...] for r in ins[3 * i : 3 * i + 3])
            results = adamw(weight, moment, square, gradient, RATE_MATRIX, DECAY_MATRIX)
            for ref, value in zip(outs[1 + 3 * i : 4 + 3 * i], results):
                ref[...] = value
        weight, moment, square = (r[...] for r in ins[3 * n :])
        results = adamw(weight, moment, square, grad_vec * clip, RATE_VECTOR, 0.0)
        for ref, value in zip(outs[1 + 3 * n :], results):
            ref[...] = value

    args = list(owned) + [totals] + [v for group in weights for v in group] + list(vectors)
    outs = [shape((1, 1), F32)]
    outs += [shape(v.shape, F32) for group in weights for v in group]
    outs += [shape(v.shape, F32) for v in vectors]
    return call(
        kernel,
        "update_all",
        outs,
        [whole(v.shape) for v in args],
        [whole(o.shape) for o in outs],
        us=2.0,
    )(*args)


class Sequence:
    def __init__(self):
        self.last = ()

    def after(self, *values):
        return lax.optimization_barrier(tuple(values) + self.last)[: len(values)]

    def run(self, function, *values, **options):
        result = function(*self.after(*values), **options)
        self.last = tuple(jax.tree.leaves(result))[-1:]
        return result

    def wait(self, *values):
        self.last = tuple(values) + self.last


class Gather:
    def __init__(self, net, seq, shard):
        self.net, self.seq, self.stage = net, seq, 0
        self.held, self.coming = shard[None], None

    def send(self):
        (held,) = self.seq.after(self.held)
        self.held = held
        last = self.stage == self.net.stages()
        self.coming = lax.ppermute(held, AXES, self.net.core() if last else self.net.stage(self.stage))
        self.stage += 1

    def take(self):
        self.held, self.coming = self.seq.after(self.held, self.coming)
        if self.stage <= self.net.stages():
            self.held = jnp.concatenate([self.held, self.coming], axis=0)
        self.seq.wait(self.held, self.coming)

    def step(self):
        self.take()
        self.send()

    def finish(self):
        while self.stage <= self.net.stages():
            self.step()
        self.take()


def add(a, b):
    return (a.astype(F32) + b.astype(F32)).astype(BF16)


class Reduce:
    def __init__(self, net, seq, keep, send):
        self.net, self.seq, self.stage = net, seq, net.stages()
        self.keep = keep
        (send,) = seq.after(send)
        self.coming = lax.ppermute(send, AXES, net.core())

    def step(self):
        self.stage -= 1
        self.keep, self.coming = self.seq.after(self.keep, self.coming)
        half = self.keep.shape[0] // 2
        away = add(self.keep[half:], self.coming[half:])
        keep = add(self.keep[:half], self.coming[:half])
        self.keep, away = self.seq.after(keep, away)
        self.seq.wait(self.keep, away)
        self.coming = lax.ppermute(away, AXES, self.net.stage(self.stage))

    def end(self):
        while self.stage:
            self.step()
        self.keep, self.coming = self.seq.after(self.keep, self.coming)
        held = self.keep.astype(F32) + self.coming.astype(F32)
        self.seq.wait(held)
        return held[0]


def total_sum(net, value):
    value = value + lax.ppermute(value, AXES, net.core())
    for stage in range(net.stages()):
        value = value + lax.ppermute(value, AXES, net.stage(stage))
    return value


def body(
    dp,
    fsdp,
    block_input,
    cotangent,
    protein_lengths,
    weight_in,
    moment_in,
    square_in,
    weight_conv,
    moment_conv,
    square_conv,
    weight_out,
    moment_out,
    square_out,
    vectors,
    moment_vectors,
    square_vectors,
):
    net = Network(dp, fsdp, True)
    net_ends = Network(dp, fsdp, False)
    geo_in = Geometry(1, weight_in.shape[0], weight_in.shape[1])
    geo_conv = Geometry(KERNEL, weight_conv.shape[1], weight_conv.shape[2])
    geo_out = Geometry(1, weight_out.shape[0], weight_out.shape[1])
    geos = (geo_in, geo_conv, geo_out)

    def flat(v):
        return v.reshape(-1, v.shape[-1])

    me = jnp.stack([lax.axis_index("dp"), lax.axis_index("fsdp")]).astype(jnp.int32)
    ends = jnp.cumsum(protein_lengths[0]).astype(jnp.int32)
    vec = vectors.reshape(1, -1)
    x = block_input[0]
    cot = cotangent[0]

    seq = Sequence()
    shard_in = seq.run(functools.partial(pack_weights, (geo_in,)), weight_in)
    get_in = Gather(net_ends, seq, shard_in)
    get_in.send()
    shard_conv = seq.run(functools.partial(pack_weights, (geo_conv,)), flat(weight_conv))
    get_conv = Gather(net, seq, shard_conv)
    get_conv.send()
    shard_out = seq.run(functools.partial(pack_weights, (geo_out,)), weight_out)
    get_out = Gather(net, seq, shard_out)
    seq.wait(me, ends, vec)
    norms = seq.run(first_norm, x, cot, vec, first=0, count=1)
    biases = [norms[3]]
    for step in range(1, STEPS):
        get_in.step()
        get_conv.step()
        if step == 1:
            get_out.send()
        elif step == 2:
            get_out.step()
        norms = seq.run(
            lambda x, cot, vec, *held: first_norm(x, cot, vec, step, 1, held), x, cot, vec, *norms[:3]
        )
        biases.append(norms[3])
    h1, h1_t, stat = norms[:3]
    grad_b3 = sum(biases)
    get_in.finish()
    h2, h2_t, n2, r2, full_in = seq.run(
        functools.partial(mix_one, net_ends, geo_in), me, get_in.held, get_in.coming, h1, vec
    )
    get_out.step()
    get_conv.step()
    get_conv.finish()
    get_out.step()
    h3, h3_t, n3, r3, full_conv = seq.run(
        functools.partial(mix_two, net, geo_conv),
        me, ends, get_conv.held, get_conv.coming, h2, vec,
    )
    get_out.step()
    pieces = seq.run(
        functools.partial(weight_gradient, net_ends, geo_out, name="out_gradient"), me, h3_t, cot
    )
    sum_out = Reduce(net_ends, seq, *pieces)
    get_out.finish()
    back_two, grad_g3, grad_s3, grad_b2, full_out = seq.run(
        functools.partial(back_through_out, net, geo_out, 0),
        me, get_out.held, get_out.coming, cot, n3, r3, vec,
    )
    sum_out.step()
    pieces = seq.run(
        functools.partial(conv_gradient, net, geo_conv), me, ends, h2_t, back_two
    )
    sum_conv = Reduce(net, seq, *pieces)
    sum_out.step()
    back_one, grad_g2, grad_s2, grad_b1 = seq.run(
        back_through_conv, ends, back_two, full_conv, n2, r2, vec
    )
    sum_conv.step()
    sum_out.step()
    pieces = seq.run(
        functools.partial(weight_gradient, net_ends, geo_in, name="in_gradient"),
        me, h1_t, back_one,
    )
    sum_in = Reduce(net_ends, seq, *pieces)
    block_output = seq.run(block_result, x, h3, full_out, vec)
    sum_in.step()
    sum_out.step()
    sum_conv.step()
    ends_in = seq.run(back_through_in, back_one, full_in, x, cot, stat, vec, first=0, count=STEPS // 2)
    sum_in.step()
    sum_conv.step()
    grad_out = sum_out.end()
    input_grad, more_g1, more_s1 = seq.run(
        lambda *args: back_through_in(*args[:6], STEPS // 2, STEPS // 2, args[6:]),
        back_one, full_in, x, cot, stat, vec, ends_in[0],
    )
    sum_in.step()
    sum_conv.step()
    grad_g1, grad_s1 = ends_in[1] + more_g1, ends_in[2] + more_s1
    partial = jnp.concatenate(
        [grad_g1, grad_s1, grad_g2, grad_s2, grad_g3, grad_s3, grad_b1, grad_b2, grad_b3], axis=1
    ).reshape(-1, 128)
    seq.wait(partial)
    sum_in.step()
    grad_conv = sum_conv.end()
    grad_in = sum_in.end()

    owned = (grad_in, grad_conv, grad_out)
    totals = total_sum(net, sum_squares(owned, partial))
    results = update_all(
        geos,
        owned,
        totals,
        (
            (weight_in, moment_in, square_in),
            (flat(weight_conv), flat(moment_conv), flat(square_conv)),
            (weight_out, moment_out, square_out),
        ),
        tuple(v.reshape(-1, 128) for v in (vectors, moment_vectors, square_vectors)),
    )
    norm, news = results[0], results[1:]
    return (
        block_output[None],
        input_grad[None],
        norm[0, 0],
        *news[0:3],
        *(v.reshape(weight_conv.shape) for v in news[3:6]),
        *news[6:9],
        *(v.reshape(-1) for v in news[9:12]),
    )


def solution(mesh):
    rows = P(("dp", "fsdp"), None, None)
    matrix = P("fsdp", "dp")
    taps = P(None, "fsdp", "dp")
    weights = (matrix,) * 3 + (taps,) * 3 + (matrix,) * 3 + (P(),) * 3
    return jax.shard_map(
        functools.partial(body, mesh.shape["dp"], mesh.shape["fsdp"]),
        mesh=mesh,
        in_specs=(rows, rows, P(("dp", "fsdp"), None)) + weights,
        out_specs=(rows, rows, P()) + weights,
        check_vma=False,
    )
```

```python
import functools

import jax
import jax.numpy as jnp
from jax import lax
from jax.experimental import pallas as pl
from jax.experimental.pallas import tpu as pltpu
from jax.sharding import PartitionSpec as P

D = 1280
INNER = 640
KERNEL = 5
DILATION = 64
LENGTH = 1024
STEP = 10
MARGIN = KERNEL // 2 * DILATION
OFFSETS = tuple((k - KERNEL // 2) * DILATION for k in range(KERNEL))
BLOCK = 256
STEPS = LENGTH // BLOCK

NORM_EPS = 1e-05
ADAM_EPS = 1e-08
BETA_ONE = 0.9
BETA_TWO = 0.95
CLIP_LIMIT = 1.0
RATE_MATRIX = 0.04
RATE_VECTOR = 0.3
DECAY_MATRIX = 0.1
GELU_C = 0.7978845608
GELU_K = 0.044715

GAIN_ONE, SHIFT_ONE = (0, 1280), (1280, 1280)
GAIN_TWO, SHIFT_TWO = (2560, 640), (3200, 640)
GAIN_THREE, SHIFT_THREE = (3840, 640), (4480, 640)
BIAS_ONE, BIAS_TWO, BIAS_THREE = (5120, 640), (5760, 640), (6400, 1280)

BF16 = jnp.bfloat16
F32 = jnp.float32
AXES = ("dp", "fsdp")
VMEM_LIMIT = 18 * 1024 * 1024
MIDDLE_LIMIT = 26 * 1024 * 1024
WIDE_LIMIT = 32 * 1024 * 1024
FLOPS_PER_US = 1.15e9
EFFORT = 4


def round16(n):
    return -(-n // 16) * 16


class Geometry:
    def __init__(self, taps, rows, cols):
        self.taps, self.rows, self.cols = taps, rows, cols
        self.height = taps * rows
        self.tiles, self.rest = divmod(cols, 128)
        self.groups = 128 // self.rest if self.rest and 128 % self.rest == 0 else 1
        self.tile_rows = round16(self.height)
        self.rest_rows = round16(-(-self.height // self.groups)) if self.rest else 0
        self.packed = self.tiles * self.tile_rows + self.rest_rows

    def pack(self, value):
        pieces = [value[:, 128 * t : 128 * t + 128] for t in range(self.tiles)]
        more = self.tile_rows - self.height
        if more:
            empty = jnp.zeros((more, 128), value.dtype)
            pieces = [jnp.concatenate([piece, empty], axis=0) for piece in pieces]
        if self.rest:
            rest = value[:, 128 * self.tiles :]
            spare = self.groups * self.rest_rows - self.height
            if spare:
                rest = jnp.concatenate([rest, jnp.zeros((spare, self.rest), value.dtype)], axis=0)
            n = self.rest_rows
            parts = [rest[n * g : n * g + n] for g in range(self.groups)]
            empty = 128 - self.groups * self.rest
            if empty:
                parts.append(jnp.zeros((n, empty), value.dtype))
            pieces.append(jnp.concatenate(parts, axis=1))
        return jnp.concatenate(pieces, axis=0)

    def unpack(self, packed):
        pieces = [
            packed[self.tile_rows * t : self.tile_rows * t + self.height]
            for t in range(self.tiles)
        ]
        if self.rest:
            base = self.tiles * self.tile_rows
            n, w = self.rest_rows, self.rest
            parts = []
            for g in range(self.groups):
                have = min(n, self.height - n * g)
                if have > 0:
                    parts.append(packed[base : base + have, w * g : w * g + w])
            pieces.append(jnp.concatenate(parts, axis=0))
        return jnp.concatenate(pieces, axis=1)


class Network:
    def __init__(self, dp, fsdp, far_first):
        self.dp, self.fsdp = dp, fsdp
        self.half = dp * fsdp // 2
        far = [("f", b) for b in range(fsdp.bit_length() - 2, 0, -1)]
        near = [("f", 0)] if fsdp > 1 else []
        rows = [("d", b) for b in range(dp.bit_length() - 2, 0, -1)]
        if far_first:
            self.order = (far + near + rows, far[::-1] + rows + near)
        else:
            self.order = (
                far[:1] + near + rows + far[1:],
                far[::-1][:1] + rows + near + far[::-1][1:],
            )

    def flip(self, stage, device):
        d, f = divmod(device, self.fsdp)
        kind, bit = self.order[d & 1][stage]
        if kind == "f":
            f ^= 1 << bit
        else:
            d ^= 1 << bit
        return d * self.fsdp + f

    def stage(self, stage):
        return [(i, self.flip(stage, i)) for i in range(self.dp * self.fsdp)]

    def core(self):
        return [(i, i ^ self.fsdp) for i in range(self.dp * self.fsdp)]

    def stages(self):
        return len(self.order[0])

    def slot(self, d, f, me_d, me_f):
        d_bits = jnp.bitwise_xor(me_d, d)
        f_bits = jnp.bitwise_xor(me_f, f)
        total = jnp.int32(0)
        for i, (kind, bit) in enumerate(self.order[d & 1]):
            source = f_bits if kind == "f" else d_bits
            total = total + (jnp.bitwise_and(lax.shift_right_logical(source, bit), 1) << i)
        return total


def call(kernel, name, out_shape, in_specs, out_specs, grid=(), scratch=(), us=1.0, aliases=None, vmem=VMEM_LIMIT):
    return pl.pallas_call(
        kernel,
        name=name,
        grid=grid,
        out_shape=out_shape,
        in_specs=in_specs,
        out_specs=out_specs,
        scratch_shapes=list(scratch),
        input_output_aliases=aliases or {},
        compiler_params=pltpu.CompilerParams(vmem_limit_bytes=vmem),
        cost_estimate=pl.CostEstimate(
            flops=int(EFFORT * us * FLOPS_PER_US), bytes_accessed=0, transcendentals=0
        ),
    )


def whole(shape):
    return pl.BlockSpec(shape, lambda *_: (0,) * len(shape))


def tokens(width, first=0):
    return pl.BlockSpec((BLOCK, width), lambda i: (first + i, 0))


SMEM = pl.BlockSpec(memory_space=pltpu.SMEM)
ANY = pl.BlockSpec(memory_space=pl.ANY)


def shape(dims, dtype):
    return jax.ShapeDtypeStruct(dims, dtype)


def part(vec_ref, span):
    return vec_ref[:, span[0] : span[0] + span[1]]


def add_rows(ref, value, first):
    row = jnp.sum(value, axis=0, keepdims=True)
    ref[...] = row if first else ref[...] + row


BLOCKS = tuple(slice(BLOCK * step, BLOCK * step + BLOCK) for step in range(STEPS))


def statistics(values):
    width = values.shape[1]
    mean = jnp.sum(values, axis=1, keepdims=True) * (1.0 / width)
    center = values - mean
    spread = jnp.sum(center * center, axis=1, keepdims=True) * (1.0 / width)
    return center, lax.rsqrt(spread + NORM_EPS)


def gelu(a):
    t = jnp.tanh(GELU_C * (a + GELU_K * (a * a * a)))
    return 0.5 * a * (1.0 + t)


def gelu_slope(a):
    square = a * a
    t = jnp.tanh(GELU_C * a * (1.0 + GELU_K * square))
    half = 0.5 * (1.0 + t)
    return half + half * (1.0 - t) * a * (GELU_C + (3.0 * GELU_C * GELU_K) * square)


def norm_backward(grad, normed, root, gain, shift):
    width = grad.shape[1]
    d_a = grad * gelu_slope(normed * gain + shift)
    scaled = d_a * gain
    mean_one = jnp.sum(scaled, axis=1, keepdims=True) * (1.0 / width)
    mean_two = jnp.sum(scaled * normed, axis=1, keepdims=True) * (1.0 / width)
    return root * (scaled - mean_one - normed * mean_two), d_a * normed, d_a


def build_taps(ends_ref, source, target, sign):
    width = source.shape[1]
    count = ends_ref.shape[0]
    for rows in BLOCKS:
        position = rows.start + lax.broadcasted_iota(jnp.int32, (BLOCK, 128), 0)
        lower = jnp.zeros((BLOCK, 128), jnp.int32)
        upper = jnp.full((BLOCK, 128), ends_ref[count - 1], jnp.int32)
        for j in range(count - 1):
            lower = jnp.where(position >= ends_ref[j], ends_ref[j], lower)
        for j in range(count - 2, -1, -1):
            upper = jnp.where(position < ends_ref[j], ends_ref[j], upper)
        for k in range(KERNEL):
            offset = sign * OFFSETS[k]
            moved = position + offset
            mask = jnp.where((moved >= lower) & (moved < upper), 1.0, 0.0).astype(BF16)
            mask = jnp.concatenate([mask] * (width // 128), axis=1)
            columns = slice(k * width, k * width + width)
            start = max(rows.start, -offset)
            stop = min(rows.stop, LENGTH - offset)
            value = source[start + offset : stop + offset]
            target[start:stop, columns] = value * mask[start - rows.start : stop - rows.start]
            if rows.start < start:
                target[rows.start : start, columns] = jnp.zeros((start - rows.start, width), BF16)
            if stop < rows.stop:
                target[stop : rows.stop, columns] = jnp.zeros((rows.stop - stop, width), BF16)


def dot(a, b):
    return jnp.dot(a, b, preferred_element_type=F32)


def dot_nt(a, b):
    return lax.dot_general(a, b, (((1,), (1,)), ((), ())), preferred_element_type=F32)


def assemble(net, geo, me_ref, own, peer, buffer, sems, full, beside=None):
    core = jnp.bitwise_and(me_ref[0], 1)
    first = pltpu.make_async_copy(own, buffer.at[core], sems.at[0])
    second = pltpu.make_async_copy(peer, buffer.at[1 - core], sems.at[1])
    first.start()
    second.start()
    first.wait()
    second.wait()
    width = net.dp * geo.cols
    for f in range(net.fsdp):
        blocks = [
            geo.unpack(buffer[d & 1, net.slot(d, f, me_ref[0], me_ref[1])])
            for d in range(net.dp)
        ]
        row = jnp.concatenate(blocks, axis=1)
        for k in range(geo.taps):
            start = k * geo.rows * net.fsdp + f * geo.rows
            value = row[k * geo.rows : k * geo.rows + geo.rows]
            full[start : start + geo.rows] = value
            if beside is not None:
                beside[f * geo.rows : f * geo.rows + geo.rows, k * width : k * width + width] = value


def distribute(net, geo, me_ref, full, buffer, sems, keep, send):
    width = net.dp * geo.cols
    for f in range(net.fsdp):
        pieces = [
            full[f * geo.rows : f * geo.rows + geo.rows, k * width : k * width + width]
            for k in range(geo.taps)
        ]
        row = pieces[0] if geo.taps == 1 else jnp.concatenate(pieces, axis=0)
        for d in range(net.dp):
            buffer[d & 1, net.slot(d, f, me_ref[0], me_ref[1])] = geo.pack(
                row[:, d * geo.cols : d * geo.cols + geo.cols]
            )
    core = jnp.bitwise_and(me_ref[0], 1)
    first = pltpu.make_async_copy(buffer.at[1 - core], send, sems.at[0])
    second = pltpu.make_async_copy(buffer.at[core], keep, sems.at[1])
    first.start()
    second.start()
    first.wait()
    second.wait()


def slots(net, geo):
    return (net.half, geo.packed, 128)


def piece_scratch(net, geo):
    return [pltpu.VMEM((2,) + slots(net, geo), BF16), pltpu.SemaphoreType.DMA((2,))]


def pack_weights(geos, *weights):
    rows = sum(geo.packed for geo in geos)

    def kernel(*refs):
        start = 0
        for geo, source in zip(geos, refs):
            refs[-1][start : start + geo.packed] = geo.pack(source[...].astype(BF16))
            start += geo.packed

    return call(
        kernel,
        "pack_weights",
        shape((rows, 128), BF16),
        [whole(w.shape) for w in weights],
        whole((rows, 128)),
        us=1.0,
    )(*weights)


def first_norm(block_input, cotangent, vec, first, held=()):
    def kernel(x_ref, cot_ref, vec_ref, *refs):
        h_ref, ht_ref, stat_ref, bias_ref = refs[-4:]
        values = x_ref[...].astype(F32)
        center, root = statistics(values)
        normed = center * root
        hidden = gelu(normed * part(vec_ref, GAIN_ONE) + part(vec_ref, SHIFT_ONE)).astype(BF16)
        h_ref[...] = hidden
        ht_ref[...] = hidden.T
        lane = lax.broadcasted_iota(jnp.int32, (BLOCK, 128), 1)
        stat_ref[...] = jnp.where(lane == 0, values[:, :1] - center[:, :1], root)
        bias_ref[...] = jnp.sum(cot_ref[...].astype(F32), axis=0, keepdims=True)

    return call(
        kernel,
        "first_norm",
        [
            shape((LENGTH, D), BF16),
            shape((D, LENGTH), BF16),
            shape((LENGTH, 128), F32),
            shape((1, D), F32),
        ],
        [tokens(D, first), tokens(D, first), whole(vec.shape)] + [ANY] * len(held),
        [
            tokens(D, first),
            pl.BlockSpec((D, BLOCK), lambda i: (0, first + i)),
            tokens(128, first),
            whole((1, D)),
        ],
        grid=(1,),
        aliases={3 + i: i for i in range(len(held))},
        us=1.2,
    )(block_input, cotangent, vec, *held)


def norm_out(vec_ref, bias, gain, shift_span, h_ref, ht_ref, normed_ref, root_ref):
    for rows in BLOCKS:
        center, root = statistics(normed_ref[rows] + part(vec_ref, bias))
        normed = center * root
        hidden = gelu(normed * part(vec_ref, gain) + part(vec_ref, shift_span)).astype(BF16)
        h_ref[rows] = hidden
        ht_ref[:, rows] = hidden.T
        normed_ref[rows] = normed
        root_ref[rows] = jnp.broadcast_to(root, (BLOCK, 128))


NORM_SHAPES = [
    shape((LENGTH, INNER), BF16),
    shape((INNER, LENGTH), BF16),
    shape((LENGTH, INNER), F32),
    shape((LENGTH, 128), F32),
]


def wholes(shapes):
    return [whole(s.shape) for s in shapes]


def mix_one(net, geo, me, own, peer, hidden_one, vec):
    def kernel(me_ref, own_ref, peer_ref, h1_ref, vec_ref, h_ref, ht_ref, n_ref, r_ref, full, buf, sems):
        assemble(net, geo, me_ref, own_ref, peer_ref, buf, sems, full)
        n_ref[...] = dot(h1_ref[...], full[...])
        norm_out(vec_ref, BIAS_ONE, GAIN_TWO, SHIFT_TWO, h_ref, ht_ref, n_ref, r_ref)

    outs = NORM_SHAPES + [shape((D, INNER), BF16)]
    return call(
        kernel,
        "mix_one",
        outs,
        [SMEM, ANY, ANY, whole((LENGTH, D)), whole(vec.shape)],
        wholes(outs),
        scratch=piece_scratch(net, geo),
        us=0.01,
    )(me, own, peer, hidden_one, vec)


def mix_two(net, geo, me, ends, own, peer, hidden_two, vec):
    def kernel(
        me_ref, ends_ref, own_ref, peer_ref, h2_ref, vec_ref, h_ref, ht_ref, n_ref, r_ref, beside, full, buf, sems, taps
    ):
        assemble(net, geo, me_ref, own_ref, peer_ref, buf, sems, full, beside)
        build_taps(ends_ref, h2_ref, taps, 1)
        n_ref[...] = dot(taps[...], full[...])
        norm_out(vec_ref, BIAS_TWO, GAIN_THREE, SHIFT_THREE, h_ref, ht_ref, n_ref, r_ref)

    outs = NORM_SHAPES + [shape((INNER, KERNEL * INNER), BF16)]
    return call(
        kernel,
        "mix_two",
        outs,
        [SMEM, SMEM, ANY, ANY, whole((LENGTH, INNER)), whole(vec.shape)],
        wholes(outs),
        scratch=[pltpu.VMEM((KERNEL * INNER, INNER), BF16)]
        + piece_scratch(net, geo)
        + [pltpu.VMEM((LENGTH, KERNEL * INNER), BF16)],
        us=11.7,
        vmem=WIDE_LIMIT,
    )(me, ends, own, peer, hidden_two, vec)


def norm_in(vec_ref, gain, shift_span, grad, n_ref, r_ref, back_ref, gg_ref, gs_ref, gb_ref):
    for rows in BLOCKS:
        back, to_gain, to_shift = norm_backward(
            grad[rows], n_ref[rows], r_ref[rows, :1], part(vec_ref, gain), part(vec_ref, shift_span)
        )
        back = back.astype(BF16)
        back_ref[rows] = back
        first = rows.start == 0
        add_rows(gg_ref, to_gain, first)
        add_rows(gs_ref, to_shift, first)
        add_rows(gb_ref, back.astype(F32), first)


def gradient_shapes(net, geo):
    return [shape(slots(net, geo), BF16)] * 2


def weight_gradient(net, geo, me, left, right, name="weight_gradient"):
    dims = (left.shape[0], right.shape[1])

    def kernel(me_ref, left_ref, right_ref, keep, send, full, buf, sems):
        full[...] = dot(left_ref[...], right_ref[...]).astype(BF16)
        distribute(net, geo, me_ref, full, buf, sems, keep, send)

    return call(
        kernel,
        name,
        gradient_shapes(net, geo),
        [SMEM, whole(left.shape), whole(right.shape)],
        [ANY, ANY],
        scratch=[pltpu.VMEM(dims, BF16)] + piece_scratch(net, geo),
        us=3.0 if dims[0] < dims[1] else 3.7,
    )(me, left, right)


def back_through_out(net, geo, me, own, peer, cotangent, normed, root, vec):
    def kernel(
        me_ref, own_ref, peer_ref, cot_ref, n_ref, r_ref, vec_ref, back_ref, gg_ref, gs_ref, gb_ref, full, buf, sems, grad
    ):
        assemble(net, geo, me_ref, own_ref, peer_ref, buf, sems, full)
        grad[...] = dot_nt(cot_ref[...], full[...])
        norm_in(vec_ref, GAIN_THREE, SHIFT_THREE, grad, n_ref, r_ref, back_ref, gg_ref, gs_ref, gb_ref)

    row = shape((1, INNER), F32)
    outs = [shape((LENGTH, INNER), BF16), row, row, row, shape((INNER, D), BF16)]
    return call(
        kernel,
        "back_through_out",
        outs,
        [SMEM, ANY, ANY] + wholes((cotangent, normed, root, vec)),
        wholes(outs),
        scratch=piece_scratch(net, geo) + [pltpu.VMEM((LENGTH, INNER), F32)],
        us=6.4,
    )(me, own, peer, cotangent, normed, root, vec)


def block_result(block_input, hidden_three, full_out, vec):
    half = LENGTH // 2

    def kernel(x_ref, h_ref, w_ref, vec_ref, out_ref):
        branch = dot(h_ref[...], w_ref[...]) + part(vec_ref, BIAS_THREE)
        out_ref[...] = (x_ref[...].astype(F32) + branch).astype(BF16)

    def rows_of(width):
        return pl.BlockSpec((half, width), lambda i: (i, 0))

    return call(
        kernel,
        "block_result",
        shape((LENGTH, D), BF16),
        [rows_of(D), rows_of(INNER), whole((INNER, D)), whole(vec.shape)],
        rows_of(D),
        grid=(2,),
        us=3.8,
    )(block_input, hidden_three, full_out, vec)


def conv_gradient(net, geo, me, ends, hidden_two_t, back_two):
    step = 2 * INNER
    width = KERNEL * INNER

    def kernel(me_ref, ends_ref, left_ref, back_ref, keep, send, taps, full, buf, sems):
        build_taps(ends_ref, back_ref, taps, -1)
        for start in range(0, width, step):
            columns = slice(start, min(start + step, width))
            full[:, columns] = dot(left_ref[...], taps[:, columns]).astype(BF16)
        distribute(net, geo, me_ref, full, buf, sems, keep, send)

    outs = gradient_shapes(net, geo) + [shape((LENGTH, width), BF16)]
    return call(
        kernel,
        "conv_gradient",
        outs,
        [SMEM, SMEM, whole((INNER, LENGTH)), whole((LENGTH, INNER))],
        [ANY, ANY, whole((LENGTH, width))],
        scratch=[pltpu.VMEM((INNER, width), BF16)] + piece_scratch(net, geo),
        us=8.0,
        vmem=MIDDLE_LIMIT,
    )(me, ends, hidden_two_t, back_two)


def back_through_conv(taps, full_conv, normed, root, vec):
    def kernel(taps_ref, w_ref, n_ref, r_ref, vec_ref, back_ref, gg_ref, gs_ref, gb_ref, grad):
        grad[...] = dot_nt(taps_ref[...], w_ref[...])
        norm_in(vec_ref, GAIN_TWO, SHIFT_TWO, grad, n_ref, r_ref, back_ref, gg_ref, gs_ref, gb_ref)

    row = shape((1, INNER), F32)
    outs = [shape((LENGTH, INNER), BF16), row, row, row]
    return call(
        kernel,
        "back_through_conv",
        outs,
        wholes((taps, full_conv, normed, root, vec)),
        wholes(outs),
        scratch=[pltpu.VMEM((LENGTH, INNER), F32)],
        us=10.0,
    )(taps, full_conv, normed, root, vec)


def back_through_in(back_one, full_in, block_input, cotangent, stat, vec, first, held=()):
    half = LENGTH // 2

    def kernel(back_ref, w_ref, x_ref, cot_ref, stat_ref, vec_ref, *refs):
        out_ref, gg_ref, gs_ref, grad = refs[-4:]
        grad[...] = dot_nt(back_ref[...], w_ref[...])
        for rows in BLOCKS[: half // BLOCK]:
            root = stat_ref[rows, 1:2]
            normed = (x_ref[rows].astype(F32) - stat_ref[rows, :1]) * root
            back, to_gain, to_shift = norm_backward(
                grad[rows], normed, root, part(vec_ref, GAIN_ONE), part(vec_ref, SHIFT_ONE)
            )
            out_ref[rows] = (cot_ref[rows].astype(F32) + back).astype(BF16)
            add_rows(gg_ref, to_gain, rows.start == 0)
            add_rows(gs_ref, to_shift, rows.start == 0)

    def rows_of(width):
        return pl.BlockSpec((half, width), lambda i: (first, 0))

    row = shape((1, D), F32)
    return call(
        kernel,
        "back_through_in",
        [shape((LENGTH, D), BF16), row, row],
        [rows_of(INNER), whole((D, INNER)), rows_of(D), rows_of(D), rows_of(128), whole(vec.shape)]
        + [ANY] * len(held),
        [rows_of(D)] + [whole((1, D))] * 2,
        grid=(1,),
        scratch=[pltpu.VMEM((half, D), F32)],
        aliases={6 + i: i for i in range(len(held))},
        us=4.4,
    )(back_one, full_in, block_input, cotangent, stat, vec, *held)


def sum_squares(owned, partial):
    rows = partial.shape[0]
    total_rows = -(-(rows + 1) // 8) * 8

    def kernel(*refs):
        out = refs[-1]
        total = jnp.zeros((1, 128), F32)
        for ref in refs[:-2]:
            value = ref[...]
            total = total + jnp.sum(value * value, axis=0, keepdims=True)
        out[...] = jnp.zeros(out.shape, F32)
        out[0:rows] = refs[-2][...]
        out[rows : rows + 1] = total

    return call(
        kernel,
        "sum_squares",
        shape((total_rows, 128), F32),
        [whole(v.shape) for v in owned] + [whole(partial.shape)],
        whole((total_rows, 128)),
        us=0.3,
    )(*owned, partial)


def adamw(weight, moment, square, gradient, rate, decay):
    new_moment = BETA_ONE * moment + (1.0 - BETA_ONE) * gradient
    new_square = BETA_TWO * square + (1.0 - BETA_TWO) * gradient * gradient
    moment_hat = new_moment * (1.0 / (1.0 - BETA_ONE**STEP))
    square_hat = new_square * (1.0 / (1.0 - BETA_TWO**STEP))
    update = moment_hat / (jnp.sqrt(square_hat) + ADAM_EPS)
    return weight - rate * (update + decay * weight), new_moment, new_square


def update_all(geos, owned, totals, weights, vectors):
    n = len(geos)
    size = vectors[0].shape[0]

    def kernel(*refs):
        owned_refs, total_ref = refs[:n], refs[n]
        ins = refs[n + 1 : n + 1 + 3 * n + 3]
        outs = refs[n + 1 + 3 * n + 3 :]
        grad_vec = total_ref[0:size]
        squares = jnp.sum(grad_vec * grad_vec, axis=0, keepdims=True) + total_ref[size : size + 1]
        norm = jnp.sqrt(jnp.sum(squares, axis=1, keepdims=True))
        outs[0][...] = norm
        clip = jnp.minimum(1.0, CLIP_LIMIT / (norm + 1e-06))
        for i, geo in enumerate(geos):
            gradient = geo.unpack(owned_refs[i][...].astype(F32)) * clip
            weight, moment, square = (r[...] for r in ins[3 * i : 3 * i + 3])
            results = adamw(weight, moment, square, gradient, RATE_MATRIX, DECAY_MATRIX)
            for ref, value in zip(outs[1 + 3 * i : 4 + 3 * i], results):
                ref[...] = value
        weight, moment, square = (r[...] for r in ins[3 * n :])
        results = adamw(weight, moment, square, grad_vec * clip, RATE_VECTOR, 0.0)
        for ref, value in zip(outs[1 + 3 * n :], results):
            ref[...] = value

    args = list(owned) + [totals] + [v for group in weights for v in group] + list(vectors)
    outs = [shape((1, 1), F32)]
    outs += [shape(v.shape, F32) for group in weights for v in group]
    outs += [shape(v.shape, F32) for v in vectors]
    return call(
        kernel,
        "update_all",
        outs,
        [whole(v.shape) for v in args],
        [whole(o.shape) for o in outs],
        us=2.0,
    )(*args)


class Sequence:
    def __init__(self):
        self.last = ()

    def after(self, *values):
        return lax.optimization_barrier(tuple(values) + self.last)[: len(values)]

    def run(self, function, *values, **options):
        result = function(*self.after(*values), **options)
        self.last = tuple(jax.tree.leaves(result))[-1:]
        return result

    def wait(self, *values):
        self.last = tuple(values) + self.last


class Gather:
    def __init__(self, net, seq, shard):
        self.net, self.seq, self.stage = net, seq, 0
        self.held, self.coming = shard[None], None

    def send(self):
        (held,) = self.seq.after(self.held)
        self.held = held
        last = self.stage == self.net.stages()
        self.coming = lax.ppermute(held, AXES, self.net.core() if last else self.net.stage(self.stage))
        self.stage += 1

    def take(self):
        self.held, self.coming = self.seq.after(self.held, self.coming)
        if self.stage <= self.net.stages():
            self.held = jnp.concatenate([self.held, self.coming], axis=0)
        self.seq.wait(self.held, self.coming)

    def step(self):
        self.take()
        self.send()

    def finish(self):
        while self.stage <= self.net.stages():
            self.step()
        self.take()


def add(a, b):
    return (a.astype(F32) + b.astype(F32)).astype(BF16)


class Reduce:
    def __init__(self, net, seq, keep, send):
        self.net, self.seq, self.stage = net, seq, net.stages()
        self.keep = keep
        (send,) = seq.after(send)
        self.coming = lax.ppermute(send, AXES, net.core())

    def step(self):
        self.stage -= 1
        self.keep, self.coming = self.seq.after(self.keep, self.coming)
        half = self.keep.shape[0] // 2
        away = add(self.keep[half:], self.coming[half:])
        keep = add(self.keep[:half], self.coming[:half])
        self.keep, away = self.seq.after(keep, away)
        self.seq.wait(self.keep, away)
        self.coming = lax.ppermute(away, AXES, self.net.stage(self.stage))

    def end(self):
        while self.stage:
            self.step()
        self.keep, self.coming = self.seq.after(self.keep, self.coming)
        held = self.keep.astype(F32) + self.coming.astype(F32)
        self.seq.wait(held)
        return held[0]


def total_sum(net, value):
    value = value + lax.ppermute(value, AXES, net.core())
    for stage in range(net.stages()):
        value = value + lax.ppermute(value, AXES, net.stage(stage))
    return value


def body(
    dp,
    fsdp,
    block_input,
    cotangent,
    protein_lengths,
    weight_in,
    moment_in,
    square_in,
    weight_conv,
    moment_conv,
    square_conv,
    weight_out,
    moment_out,
    square_out,
    vectors,
    moment_vectors,
    square_vectors,
):
    net = Network(dp, fsdp, True)
    net_ends = Network(dp, fsdp, False)
    geo_in = Geometry(1, weight_in.shape[0], weight_in.shape[1])
    geo_conv = Geometry(KERNEL, weight_conv.shape[1], weight_conv.shape[2])
    geo_out = Geometry(1, weight_out.shape[0], weight_out.shape[1])
    geos = (geo_in, geo_conv, geo_out)

    def flat(v):
        return v.reshape(-1, v.shape[-1])

    me = jnp.stack([lax.axis_index("dp"), lax.axis_index("fsdp")]).astype(jnp.int32)
    ends = jnp.cumsum(protein_lengths[0]).astype(jnp.int32)
    vec = vectors.reshape(1, -1)
    x = block_input[0]
    cot = cotangent[0]

    seq = Sequence()
    shard_in = seq.run(functools.partial(pack_weights, (geo_in,)), weight_in)
    get_in = Gather(net_ends, seq, shard_in)
    get_in.send()
    shard_conv = seq.run(functools.partial(pack_weights, (geo_conv,)), flat(weight_conv))
    get_conv = Gather(net, seq, shard_conv)
    get_conv.send()
    shard_out = seq.run(functools.partial(pack_weights, (geo_out,)), weight_out)
    get_out = Gather(net, seq, shard_out)
    seq.wait(me, ends, vec)
    norms = seq.run(first_norm, x, cot, vec, first=0)
    biases = [norms[3]]
    for step in range(1, STEPS):
        get_in.step()
        get_conv.step()
        if step == 1:
            get_out.send()
        elif step == 2:
            get_out.step()
        norms = seq.run(
            lambda x, cot, vec, *held: first_norm(x, cot, vec, step, held), x, cot, vec, *norms[:3]
        )
        biases.append(norms[3])
    h1, h1_t, stat = norms[:3]
    grad_b3 = sum(biases)
    get_in.finish()
    h2, h2_t, n2, r2, full_in = seq.run(
        functools.partial(mix_one, net_ends, geo_in), me, get_in.held, get_in.coming, h1, vec
    )
    get_out.step()
    get_conv.step()
    get_conv.finish()
    get_out.step()
    h3, h3_t, n3, r3, full_conv = seq.run(
        functools.partial(mix_two, net, geo_conv),
        me, ends, get_conv.held, get_conv.coming, h2, vec,
    )
    get_out.step()
    pieces = seq.run(
        functools.partial(weight_gradient, net_ends, geo_out, name="out_gradient"), me, h3_t, cot
    )
    sum_out = Reduce(net_ends, seq, *pieces)
    get_out.finish()
    back_two, grad_g3, grad_s3, grad_b2, full_out = seq.run(
        functools.partial(back_through_out, net, geo_out),
        me, get_out.held, get_out.coming, cot, n3, r3, vec,
    )
    sum_out.step()
    keep, send, taps = seq.run(
        functools.partial(conv_gradient, net, geo_conv), me, ends, h2_t, back_two
    )
    sum_conv = Reduce(net, seq, keep, send)
    back_one, grad_g2, grad_s2, grad_b1 = seq.run(
        back_through_conv, taps, full_conv, n2, r2, vec
    )
    sum_conv.step()
    sum_out.step()
    pieces = seq.run(
        functools.partial(weight_gradient, net_ends, geo_in, name="in_gradient"),
        me, h1_t, back_one,
    )
    sum_in = Reduce(net_ends, seq, *pieces)
    block_output = seq.run(block_result, x, h3, full_out, vec)
    sum_in.step()
    sum_conv.step()
    sum_out.step()
    ends_in = seq.run(back_through_in, back_one, full_in, x, cot, stat, vec, first=0)
    sum_in.step()
    sum_conv.step()
    sum_out.step()
    input_grad, more_g1, more_s1 = seq.run(
        lambda *args: back_through_in(*args[:6], 1, args[6:]),
        back_one, full_in, x, cot, stat, vec, ends_in[0],
    )
    sum_in.step()
    sum_conv.step()
    grad_out = sum_out.end()
    grad_g1, grad_s1 = ends_in[1] + more_g1, ends_in[2] + more_s1
    partial = jnp.concatenate(
        [grad_g1, grad_s1, grad_g2, grad_s2, grad_g3, grad_s3, grad_b1, grad_b2, grad_b3], axis=1
    ).reshape(-1, 128)
    seq.wait(partial)
    sum_in.step()
    grad_conv = sum_conv.end()
    grad_in = sum_in.end()

    owned = (grad_in, grad_conv, grad_out)
    totals = total_sum(net, sum_squares(owned, partial))
    results = update_all(
        geos,
        owned,
        totals,
        (
            (weight_in, moment_in, square_in),
            (flat(weight_conv), flat(moment_conv), flat(square_conv)),
            (weight_out, moment_out, square_out),
        ),
        tuple(v.reshape(-1, 128) for v in (vectors, moment_vectors, square_vectors)),
    )
    norm, news = results[0], results[1:]
    return (
        block_output[None],
        input_grad[None],
        norm[0, 0],
        *news[0:3],
        *(v.reshape(weight_conv.shape) for v in news[3:6]),
        *news[6:9],
        *(v.reshape(-1) for v in news[9:12]),
    )


def solution(mesh):
    rows = P(("dp", "fsdp"), None, None)
    matrix = P("fsdp", "dp")
    taps = P(None, "fsdp", "dp")
    weights = (matrix,) * 3 + (taps,) * 3 + (matrix,) * 3 + (P(),) * 3
    return jax.shard_map(
        functools.partial(body, mesh.shape["dp"], mesh.shape["fsdp"]),
        mesh=mesh,
        in_specs=(rows, rows, P(("dp", "fsdp"), None)) + weights,
        out_specs=(rows, rows, P()) + weights,
        check_vma=False,
    )
```

```python
import functools

import jax
import jax.numpy as jnp
from jax import lax
from jax.experimental import pallas as pl
from jax.experimental.pallas import tpu as pltpu
from jax.sharding import PartitionSpec as P

D = 1280
INNER = 640
KERNEL = 5
DILATION = 64
LENGTH = 1024
STEP = 10
MARGIN = KERNEL // 2 * DILATION
OFFSETS = tuple((k - KERNEL // 2) * DILATION for k in range(KERNEL))
BLOCK = 256
STEPS = LENGTH // BLOCK

NORM_EPS = 1e-05
ADAM_EPS = 1e-08
BETA_ONE = 0.9
BETA_TWO = 0.95
CLIP_LIMIT = 1.0
RATE_MATRIX = 0.04
RATE_VECTOR = 0.3
DECAY_MATRIX = 0.1
GELU_C = 0.7978845608
GELU_K = 0.044715

GAIN_ONE, SHIFT_ONE = (0, 1280), (1280, 1280)
GAIN_TWO, SHIFT_TWO = (2560, 640), (3200, 640)
GAIN_THREE, SHIFT_THREE = (3840, 640), (4480, 640)
BIAS_ONE, BIAS_TWO, BIAS_THREE = (5120, 640), (5760, 640), (6400, 1280)

BF16 = jnp.bfloat16
F32 = jnp.float32
AXES = ("dp", "fsdp")
VMEM_LIMIT = 18 * 1024 * 1024
MIDDLE_LIMIT = 27 * 1024 * 1024
WIDE_LIMIT = 34 * 1024 * 1024
FLOPS_PER_US = 1.15e9
EFFORT = 4


def round16(n):
    return -(-n // 16) * 16


class Geometry:
    def __init__(self, taps, rows, cols):
        self.taps, self.rows, self.cols = taps, rows, cols
        self.height = taps * rows
        self.tiles, self.rest = divmod(cols, 128)
        self.groups = 128 // self.rest if self.rest and 128 % self.rest == 0 else 1
        self.tile_rows = round16(self.height)
        self.rest_rows = round16(-(-self.height // self.groups)) if self.rest else 0
        self.packed = self.tiles * self.tile_rows + self.rest_rows

    def pack(self, value):
        pieces = [value[:, 128 * t : 128 * t + 128] for t in range(self.tiles)]
        more = self.tile_rows - self.height
        if more:
            empty = jnp.zeros((more, 128), value.dtype)
            pieces = [jnp.concatenate([piece, empty], axis=0) for piece in pieces]
        if self.rest:
            rest = value[:, 128 * self.tiles :]
            spare = self.groups * self.rest_rows - self.height
            if spare:
                rest = jnp.concatenate([rest, jnp.zeros((spare, self.rest), value.dtype)], axis=0)
            n = self.rest_rows
            parts = [rest[n * g : n * g + n] for g in range(self.groups)]
            empty = 128 - self.groups * self.rest
            if empty:
                parts.append(jnp.zeros((n, empty), value.dtype))
            pieces.append(jnp.concatenate(parts, axis=1))
        return jnp.concatenate(pieces, axis=0)

    def unpack(self, packed):
        pieces = [
            packed[self.tile_rows * t : self.tile_rows * t + self.height]
            for t in range(self.tiles)
        ]
        if self.rest:
            base = self.tiles * self.tile_rows
            n, w = self.rest_rows, self.rest
            parts = []
            for g in range(self.groups):
                have = min(n, self.height - n * g)
                if have > 0:
                    parts.append(packed[base : base + have, w * g : w * g + w])
            pieces.append(jnp.concatenate(parts, axis=0))
        return jnp.concatenate(pieces, axis=1)


class Network:
    def __init__(self, dp, fsdp, far_first):
        self.dp, self.fsdp = dp, fsdp
        self.half = dp * fsdp // 2
        far = [("f", b) for b in range(fsdp.bit_length() - 2, 0, -1)]
        near = [("f", 0)] if fsdp > 1 else []
        rows = [("d", b) for b in range(dp.bit_length() - 2, 0, -1)]
        if far_first:
            self.order = (far + near + rows, far[::-1] + rows + near)
        else:
            self.order = (
                far[:1] + near + rows + far[1:],
                far[::-1][:1] + rows + near + far[::-1][1:],
            )

    def flip(self, stage, device):
        d, f = divmod(device, self.fsdp)
        kind, bit = self.order[d & 1][stage]
        if kind == "f":
            f ^= 1 << bit
        else:
            d ^= 1 << bit
        return d * self.fsdp + f

    def stage(self, stage):
        return [(i, self.flip(stage, i)) for i in range(self.dp * self.fsdp)]

    def core(self):
        return [(i, i ^ self.fsdp) for i in range(self.dp * self.fsdp)]

    def stages(self):
        return len(self.order[0])

    def slot(self, d, f, me_d, me_f):
        d_bits = jnp.bitwise_xor(me_d, d)
        f_bits = jnp.bitwise_xor(me_f, f)
        total = jnp.int32(0)
        for i, (kind, bit) in enumerate(self.order[d & 1]):
            source = f_bits if kind == "f" else d_bits
            total = total + (jnp.bitwise_and(lax.shift_right_logical(source, bit), 1) << i)
        return total


def call(kernel, name, out_shape, in_specs, out_specs, grid=(), scratch=(), us=1.0, aliases=None, vmem=VMEM_LIMIT):
    return pl.pallas_call(
        kernel,
        name=name,
        grid=grid,
        out_shape=out_shape,
        in_specs=in_specs,
        out_specs=out_specs,
        scratch_shapes=list(scratch),
        input_output_aliases=aliases or {},
        compiler_params=pltpu.CompilerParams(vmem_limit_bytes=vmem),
        cost_estimate=pl.CostEstimate(
            flops=int(EFFORT * us * FLOPS_PER_US), bytes_accessed=0, transcendentals=0
        ),
    )


def whole(shape):
    return pl.BlockSpec(shape, lambda *_: (0,) * len(shape))


def tokens(width, first=0):
    return pl.BlockSpec((BLOCK, width), lambda i: (first + i, 0))


SMEM = pl.BlockSpec(memory_space=pltpu.SMEM)
ANY = pl.BlockSpec(memory_space=pl.ANY)


def shape(dims, dtype):
    return jax.ShapeDtypeStruct(dims, dtype)


def part(vec_ref, span):
    return vec_ref[:, span[0] : span[0] + span[1]]


def add_rows(ref, value):
    ref[...] += jnp.sum(value, axis=0, keepdims=True)


HALF = LENGTH // 2


def for_halves(body, *sums):
    for ref in sums:
        ref[...] = jnp.zeros(ref.shape, ref.dtype)

    @pl.loop(0, 2)
    def _(step):
        body(pl.multiple_of(step * HALF, HALF))


def blocks_of(start):
    return [
        (slice(offset, offset + BLOCK), pl.ds(pl.multiple_of(start + offset, BLOCK), BLOCK))
        for offset in range(0, HALF, BLOCK)
    ]


def for_rows(count, size, loop, body):
    if loop:

        @pl.loop(0, count)
        def _(step):
            body(pl.ds(pl.multiple_of(step * size, size), size))
    else:
        for step in range(count):
            body(slice(step * size, step * size + size))


def statistics(values):
    width = values.shape[1]
    mean = jnp.sum(values, axis=1, keepdims=True) * (1.0 / width)
    center = values - mean
    spread = jnp.sum(center * center, axis=1, keepdims=True) * (1.0 / width)
    return center, lax.rsqrt(spread + NORM_EPS)


def gelu(a):
    t = jnp.tanh(GELU_C * (a + GELU_K * (a * a * a)))
    return 0.5 * a * (1.0 + t)


def gelu_slope(a):
    square = a * a
    t = jnp.tanh(GELU_C * a * (1.0 + GELU_K * square))
    half = 0.5 * (1.0 + t)
    return half + half * (1.0 - t) * a * (GELU_C + (3.0 * GELU_C * GELU_K) * square)


def norm_backward(grad, normed, root, gain, shift):
    width = grad.shape[1]
    d_a = grad * gelu_slope(normed * gain + shift)
    scaled = d_a * gain
    mean_one = jnp.sum(scaled, axis=1, keepdims=True) * (1.0 / width)
    mean_two = jnp.sum(scaled * normed, axis=1, keepdims=True) * (1.0 / width)
    return root * (scaled - mean_one - normed * mean_two), d_a * normed, d_a


def build_taps(ends_ref, source, padded, target, sign):
    width = source.shape[1]
    count = ends_ref.shape[0]
    empty = jnp.zeros((MARGIN, width), BF16)
    padded[0:MARGIN] = empty
    padded[MARGIN : MARGIN + LENGTH] = source[...]
    padded[MARGIN + LENGTH : MARGIN + LENGTH + MARGIN] = empty

    @pl.loop(0, STEPS)
    def _(step):
        start = pl.multiple_of(step * BLOCK, BLOCK)
        position = start + lax.broadcasted_iota(jnp.int32, (BLOCK, 128), 0)
        lower = jnp.zeros((BLOCK, 128), jnp.int32)
        upper = jnp.full((BLOCK, 128), ends_ref[count - 1], jnp.int32)
        for j in range(count - 1):
            lower = jnp.where(position >= ends_ref[j], ends_ref[j], lower)
        for j in range(count - 2, -1, -1):
            upper = jnp.where(position < ends_ref[j], ends_ref[j], upper)
        for k in range(KERNEL):
            offset = sign * OFFSETS[k]
            moved = position + offset
            mask = jnp.where((moved >= lower) & (moved < upper), 1.0, 0.0).astype(BF16)
            mask = jnp.concatenate([mask] * (width // 128), axis=1)
            value = padded[pl.ds(pl.multiple_of(start + MARGIN + offset, DILATION), BLOCK)]
            target[pl.ds(start, BLOCK), k * width : k * width + width] = value * mask


def build_taps_unrolled(ends_ref, source, target, sign):
    width = source.shape[1]
    count = ends_ref.shape[0]
    for rows in (slice(start, start + BLOCK) for start in range(0, LENGTH, BLOCK)):
        position = rows.start + lax.broadcasted_iota(jnp.int32, (BLOCK, 128), 0)
        lower = jnp.zeros((BLOCK, 128), jnp.int32)
        upper = jnp.full((BLOCK, 128), ends_ref[count - 1], jnp.int32)
        for j in range(count - 1):
            lower = jnp.where(position >= ends_ref[j], ends_ref[j], lower)
        for j in range(count - 2, -1, -1):
            upper = jnp.where(position < ends_ref[j], ends_ref[j], upper)
        for k in range(KERNEL):
            offset = sign * OFFSETS[k]
            moved = position + offset
            mask = jnp.where((moved >= lower) & (moved < upper), 1.0, 0.0).astype(BF16)
            mask = jnp.concatenate([mask] * (width // 128), axis=1)
            columns = slice(k * width, k * width + width)
            start = max(rows.start, -offset)
            stop = min(rows.stop, LENGTH - offset)
            value = source[start + offset : stop + offset]
            target[start:stop, columns] = value * mask[start - rows.start : stop - rows.start]
            if rows.start < start:
                target[rows.start : start, columns] = jnp.zeros((start - rows.start, width), BF16)
            if stop < rows.stop:
                target[stop : rows.stop, columns] = jnp.zeros((rows.stop - stop, width), BF16)


def dot(a, b):
    return jnp.dot(a, b, preferred_element_type=F32)


def dot_nt(a, b):
    return lax.dot_general(a, b, (((1,), (1,)), ((), ())), preferred_element_type=F32)


def assemble(net, geo, me_ref, own, peer, buffer, sems, full, beside=None, loop=False):
    core = jnp.bitwise_and(me_ref[0], 1)
    first = pltpu.make_async_copy(own, buffer.at[core], sems.at[0])
    second = pltpu.make_async_copy(peer, buffer.at[1 - core], sems.at[1])
    first.start()
    second.start()
    first.wait()
    second.wait()
    width = net.dp * geo.cols

    def body(f, first_row):
        blocks = [
            geo.unpack(buffer[d & 1, net.slot(d, f, me_ref[0], me_ref[1])])
            for d in range(net.dp)
        ]
        row = jnp.concatenate(blocks, axis=1)
        for k in range(geo.taps):
            value = row[k * geo.rows : k * geo.rows + geo.rows]
            full[pl.ds(k * geo.rows * net.fsdp + first_row, geo.rows)] = value
            if beside is not None:
                beside[pl.ds(first_row, geo.rows), k * width : k * width + width] = value

    if loop and geo.rows % 16 == 0:

        @pl.loop(0, net.fsdp)
        def _(f):
            body(f, pl.multiple_of(f * geo.rows, 16))
    else:
        for f in range(net.fsdp):
            body(f, f * geo.rows)


def distribute(net, geo, me_ref, full, buffer, sems, keep, send):
    width = net.dp * geo.cols
    for f in range(net.fsdp):
        pieces = [
            full[f * geo.rows : f * geo.rows + geo.rows, k * width : k * width + width]
            for k in range(geo.taps)
        ]
        row = pieces[0] if geo.taps == 1 else jnp.concatenate(pieces, axis=0)
        for d in range(net.dp):
            buffer[d & 1, net.slot(d, f, me_ref[0], me_ref[1])] = geo.pack(
                row[:, d * geo.cols : d * geo.cols + geo.cols]
            )
    core = jnp.bitwise_and(me_ref[0], 1)
    first = pltpu.make_async_copy(buffer.at[1 - core], send, sems.at[0])
    second = pltpu.make_async_copy(buffer.at[core], keep, sems.at[1])
    first.start()
    second.start()
    first.wait()
    second.wait()


def slots(net, geo):
    return (net.half, geo.packed, 128)


def piece_scratch(net, geo):
    return [pltpu.VMEM((2,) + slots(net, geo), BF16), pltpu.SemaphoreType.DMA((2,))]


def pack_weights(geos, *weights):
    rows = sum(geo.packed for geo in geos)

    def kernel(*refs):
        start = 0
        for geo, source in zip(geos, refs):
            refs[-1][start : start + geo.packed] = geo.pack(source[...].astype(BF16))
            start += geo.packed

    return call(
        kernel,
        "pack_weights",
        shape((rows, 128), BF16),
        [whole(w.shape) for w in weights],
        whole((rows, 128)),
        us=1.0,
    )(*weights)


def first_norm(block_input, cotangent, vec, first, held=()):
    def kernel(x_ref, cot_ref, vec_ref, *refs):
        h_ref, ht_ref, stat_ref, bias_ref = refs[-4:]

        def body(rows):
            values = x_ref[rows].astype(F32)
            center, root = statistics(values)
            normed = center * root
            hidden = gelu(normed * part(vec_ref, GAIN_ONE) + part(vec_ref, SHIFT_ONE)).astype(BF16)
            h_ref[rows] = hidden
            ht_ref[:, rows] = hidden.T
            lane = lax.broadcasted_iota(jnp.int32, (BLOCK // 2, 128), 1)
            stat_ref[rows] = jnp.where(lane == 0, values[:, :1] - center[:, :1], root)
            bias_ref[...] += jnp.sum(cot_ref[rows].astype(F32), axis=0, keepdims=True)

        bias_ref[...] = jnp.zeros((1, D), F32)
        for_rows(2, BLOCK // 2, True, body)

    return call(
        kernel,
        "first_norm",
        [
            shape((LENGTH, D), BF16),
            shape((D, LENGTH), BF16),
            shape((LENGTH, 128), F32),
            shape((1, D), F32),
        ],
        [tokens(D, first), tokens(D, first), whole(vec.shape)] + [ANY] * len(held),
        [
            tokens(D, first),
            pl.BlockSpec((D, BLOCK), lambda i: (0, first + i)),
            tokens(128, first),
            whole((1, D)),
        ],
        grid=(1,),
        aliases={3 + i: i for i in range(len(held))},
        us=1.2,
    )(block_input, cotangent, vec, *held)


def norm_out(rows, mixed, vec_ref, gain, shift_span, h_ref, ht_ref, normed_ref, root_ref):
    center, root = statistics(mixed)
    normed = center * root
    hidden = gelu(normed * part(vec_ref, gain) + part(vec_ref, shift_span)).astype(BF16)
    h_ref[rows] = hidden
    ht_ref[:, rows] = hidden.T
    normed_ref[rows] = normed
    root_ref[rows] = jnp.broadcast_to(root, (root.shape[0], 128))


NORM_SHAPES = [
    shape((LENGTH, INNER), BF16),
    shape((INNER, LENGTH), BF16),
    shape((LENGTH, INNER), F32),
    shape((LENGTH, 128), F32),
]


def wholes(shapes):
    return [whole(s.shape) for s in shapes]


def mix_one(net, geo, me, own, peer, hidden_one, vec):
    def kernel(me_ref, own_ref, peer_ref, h1_ref, vec_ref, h_ref, ht_ref, n_ref, r_ref, full, buf, sems):
        assemble(net, geo, me_ref, own_ref, peer_ref, buf, sems, full, loop=True)
        n_ref[...] = dot(h1_ref[...], full[...])

        def body(rows):
            mixed = n_ref[rows] + part(vec_ref, BIAS_ONE)
            norm_out(rows, mixed, vec_ref, GAIN_TWO, SHIFT_TWO, h_ref, ht_ref, n_ref, r_ref)

        for_rows(2 * STEPS, BLOCK // 2, True, body)

    outs = NORM_SHAPES + [shape((D, INNER), BF16)]
    return call(
        kernel,
        "mix_one",
        outs,
        [SMEM, ANY, ANY, whole((LENGTH, D)), whole(vec.shape)],
        wholes(outs),
        scratch=piece_scratch(net, geo),
        us=0.01,
    )(me, own, peer, hidden_one, vec)


def mix_two(net, geo, me, ends, own, peer, hidden_two, vec):
    def kernel(
        me_ref, ends_ref, own_ref, peer_ref, h2_ref, vec_ref, h_ref, ht_ref, n_ref, r_ref, beside, full, buf, sems, taps
    ):
        assemble(net, geo, me_ref, own_ref, peer_ref, buf, sems, full, beside)
        build_taps_unrolled(ends_ref, h2_ref, taps, 1)
        n_ref[...] = dot(taps[...], full[...])

        def body(rows):
            mixed = n_ref[rows] + part(vec_ref, BIAS_TWO)
            norm_out(rows, mixed, vec_ref, GAIN_THREE, SHIFT_THREE, h_ref, ht_ref, n_ref, r_ref)

        for_rows(STEPS, BLOCK, False, body)

    outs = NORM_SHAPES + [shape((INNER, KERNEL * INNER), BF16)]
    return call(
        kernel,
        "mix_two",
        outs,
        [SMEM, SMEM, ANY, ANY, whole((LENGTH, INNER)), whole(vec.shape)],
        wholes(outs),
        scratch=[pltpu.VMEM((KERNEL * INNER, INNER), BF16)]
        + piece_scratch(net, geo)
        + [
            pltpu.VMEM((LENGTH, KERNEL * INNER), BF16),
        ],
        us=11.7,
        vmem=WIDE_LIMIT,
    )(me, ends, own, peer, hidden_two, vec)


def norm_in(product, vec_ref, gain, shift_span, grad, n_ref, r_ref, back_ref, *sums):
    def body(start):
        grad[...] = product(pl.ds(start, HALF))
        for part_rows, rows in blocks_of(start):
            back, to_gain, to_shift = norm_backward(
                grad[part_rows],
                n_ref[rows],
                r_ref[rows][:, :1],
                part(vec_ref, gain),
                part(vec_ref, shift_span),
            )
            back = back.astype(BF16)
            back_ref[rows] = back
            for ref, value in zip(sums, (to_gain, to_shift, back.astype(F32))):
                add_rows(ref, value)

    for_halves(body, *sums)


def gradient_shapes(net, geo):
    return [shape(slots(net, geo), BF16)] * 2


def weight_gradient(net, geo, me, left, right, name="weight_gradient"):
    dims = (left.shape[0], right.shape[1])

    def kernel(me_ref, left_ref, right_ref, keep, send, full, buf, sems):
        full[...] = dot(left_ref[...], right_ref[...]).astype(BF16)
        distribute(net, geo, me_ref, full, buf, sems, keep, send)

    return call(
        kernel,
        name,
        gradient_shapes(net, geo),
        [SMEM, whole(left.shape), whole(right.shape)],
        [ANY, ANY],
        scratch=[pltpu.VMEM(dims, BF16)] + piece_scratch(net, geo),
        us=3.0 if dims[0] < dims[1] else 3.7,
    )(me, left, right)


def back_through_out(net, geo, me, own, peer, cotangent, normed, root, vec):
    def kernel(
        me_ref, own_ref, peer_ref, cot_ref, n_ref, r_ref, vec_ref, back_ref, gg_ref, gs_ref, gb_ref, full, buf, sems, grad
    ):
        assemble(net, geo, me_ref, own_ref, peer_ref, buf, sems, full)

        def product(rows):
            return dot_nt(cot_ref[rows], full[...])

        norm_in(product, vec_ref, GAIN_THREE, SHIFT_THREE, grad, n_ref, r_ref, back_ref, gg_ref, gs_ref, gb_ref)

    row = shape((1, INNER), F32)
    outs = [shape((LENGTH, INNER), BF16), row, row, row, shape((INNER, D), BF16)]
    return call(
        kernel,
        "back_through_out",
        outs,
        [SMEM, ANY, ANY] + wholes((cotangent, normed, root, vec)),
        wholes(outs),
        scratch=piece_scratch(net, geo) + [pltpu.VMEM((HALF, INNER), F32)],
        us=6.4,
    )(me, own, peer, cotangent, normed, root, vec)


def block_result(block_input, hidden_three, full_out, vec):
    half = LENGTH // 2

    def kernel(x_ref, h_ref, w_ref, vec_ref, out_ref):
        branch = dot(h_ref[...], w_ref[...]) + part(vec_ref, BIAS_THREE)
        out_ref[...] = (x_ref[...].astype(F32) + branch).astype(BF16)

    def rows_of(width):
        return pl.BlockSpec((half, width), lambda i: (i, 0))

    return call(
        kernel,
        "block_result",
        shape((LENGTH, D), BF16),
        [rows_of(D), rows_of(INNER), whole((INNER, D)), whole(vec.shape)],
        rows_of(D),
        grid=(2,),
        us=3.8,
    )(block_input, hidden_three, full_out, vec)


def conv_gradient(net, geo, me, ends, hidden_two_t, back_two):
    step = 2 * INNER
    width = KERNEL * INNER

    def kernel(me_ref, ends_ref, left_ref, back_ref, keep, send, taps, full, buf, sems, pad):
        build_taps(ends_ref, back_ref, pad, taps, -1)
        for start in range(0, width, step):
            columns = slice(start, min(start + step, width))
            full[:, columns] = dot(left_ref[...], taps[:, columns]).astype(BF16)
        distribute(net, geo, me_ref, full, buf, sems, keep, send)

    outs = gradient_shapes(net, geo) + [shape((LENGTH, width), BF16)]
    return call(
        kernel,
        "conv_gradient",
        outs,
        [SMEM, SMEM, whole((INNER, LENGTH)), whole((LENGTH, INNER))],
        [ANY, ANY, whole((LENGTH, width))],
        scratch=[pltpu.VMEM((INNER, width), BF16)]
        + piece_scratch(net, geo)
        + [pltpu.VMEM((LENGTH + 2 * MARGIN, INNER), BF16)],
        us=8.0,
        vmem=MIDDLE_LIMIT,
    )(me, ends, hidden_two_t, back_two)


def back_through_conv(taps, full_conv, normed, root, vec):
    def kernel(taps_ref, w_ref, n_ref, r_ref, vec_ref, back_ref, gg_ref, gs_ref, gb_ref, grad):
        def product(rows):
            return dot_nt(taps_ref[rows], w_ref[...])

        norm_in(product, vec_ref, GAIN_TWO, SHIFT_TWO, grad, n_ref, r_ref, back_ref, gg_ref, gs_ref, gb_ref)

    row = shape((1, INNER), F32)
    outs = [shape((LENGTH, INNER), BF16), row, row, row]
    return call(
        kernel,
        "back_through_conv",
        outs,
        wholes((taps, full_conv, normed, root, vec)),
        wholes(outs),
        scratch=[pltpu.VMEM((HALF, INNER), F32)],
        us=10.0,
    )(taps, full_conv, normed, root, vec)


def back_through_in(back_one, full_in, block_input, cotangent, stat, vec):
    def kernel(back_ref, w_ref, x_ref, cot_ref, stat_ref, vec_ref, out_ref, gg_ref, gs_ref, grad):
        @pl.when(pl.program_id(0) == 0)
        def _():
            gg_ref[...] = jnp.zeros((1, D), F32)
            gs_ref[...] = jnp.zeros((1, D), F32)

        grad[...] = dot_nt(back_ref[...], w_ref[...])
        for start in range(0, HALF, BLOCK):
            rows = slice(start, start + BLOCK)
            root = stat_ref[rows, 1:2]
            normed = (x_ref[rows].astype(F32) - stat_ref[rows, :1]) * root
            back, to_gain, to_shift = norm_backward(
                grad[rows], normed, root, part(vec_ref, GAIN_ONE), part(vec_ref, SHIFT_ONE)
            )
            out_ref[rows] = (cot_ref[rows].astype(F32) + back).astype(BF16)
            add_rows(gg_ref, to_gain)
            add_rows(gs_ref, to_shift)

    def rows_of(width):
        return pl.BlockSpec((HALF, width), lambda i: (i, 0))

    row = shape((1, D), F32)
    return call(
        kernel,
        "back_through_in",
        [shape((LENGTH, D), BF16), row, row],
        [rows_of(INNER), whole((D, INNER)), rows_of(D), rows_of(D), rows_of(128), whole(vec.shape)],
        [rows_of(D)] + [whole((1, D))] * 2,
        grid=(2,),
        scratch=[pltpu.VMEM((HALF, D), F32)],
        us=9.4,
    )(back_one, full_in, block_input, cotangent, stat, vec)


def sum_squares(owned, partial):
    rows = partial.shape[0]
    total_rows = -(-(rows + 1) // 8) * 8

    def kernel(*refs):
        out = refs[-1]
        total = jnp.zeros((1, 128), F32)
        for ref in refs[:-2]:
            value = ref[...]
            total = total + jnp.sum(value * value, axis=0, keepdims=True)
        out[...] = jnp.zeros(out.shape, F32)
        out[0:rows] = refs[-2][...]
        out[rows : rows + 1] = total

    return call(
        kernel,
        "sum_squares",
        shape((total_rows, 128), F32),
        [whole(v.shape) for v in owned] + [whole(partial.shape)],
        whole((total_rows, 128)),
        us=0.3,
    )(*owned, partial)


def adamw(weight, moment, square, gradient, rate, decay):
    new_moment = BETA_ONE * moment + (1.0 - BETA_ONE) * gradient
    new_square = BETA_TWO * square + (1.0 - BETA_TWO) * gradient * gradient
    moment_hat = new_moment * (1.0 / (1.0 - BETA_ONE**STEP))
    square_hat = new_square * (1.0 / (1.0 - BETA_TWO**STEP))
    update = moment_hat / (jnp.sqrt(square_hat) + ADAM_EPS)
    return weight - rate * (update + decay * weight), new_moment, new_square


def update_all(geos, owned, totals, weights, vectors):
    n = len(geos)
    size = vectors[0].shape[0]

    def kernel(*refs):
        owned_refs, total_ref = refs[:n], refs[n]
        ins = refs[n + 1 : n + 1 + 3 * n + 3]
        outs = refs[n + 1 + 3 * n + 3 :]
        grad_vec = total_ref[0:size]
        squares = jnp.sum(grad_vec * grad_vec, axis=0, keepdims=True) + total_ref[size : size + 1]
        norm = jnp.sqrt(jnp.sum(squares, axis=1, keepdims=True))
        outs[0][...] = norm
        clip = jnp.minimum(1.0, CLIP_LIMIT / (norm + 1e-06))
        for i, geo in enumerate(geos):
            gradient = geo.unpack(owned_refs[i][...].astype(F32)) * clip
            weight, moment, square = (r[...] for r in ins[3 * i : 3 * i + 3])
            results = adamw(weight, moment, square, gradient, RATE_MATRIX, DECAY_MATRIX)
            for ref, value in zip(outs[1 + 3 * i : 4 + 3 * i], results):
                ref[...] = value
        weight, moment, square = (r[...] for r in ins[3 * n :])
        results = adamw(weight, moment, square, grad_vec * clip, RATE_VECTOR, 0.0)
        for ref, value in zip(outs[1 + 3 * n :], results):
            ref[...] = value

    args = list(owned) + [totals] + [v for group in weights for v in group] + list(vectors)
    outs = [shape((1, 1), F32)]
    outs += [shape(v.shape, F32) for group in weights for v in group]
    outs += [shape(v.shape, F32) for v in vectors]
    return call(
        kernel,
        "update_all",
        outs,
        [whole(v.shape) for v in args],
        [whole(o.shape) for o in outs],
        us=2.0,
    )(*args)


class Sequence:
    def __init__(self):
        self.last = ()

    def after(self, *values):
        return lax.optimization_barrier(tuple(values) + self.last)[: len(values)]

    def run(self, function, *values, **options):
        result = function(*self.after(*values), **options)
        self.last = tuple(jax.tree.leaves(result))[-1:]
        return result

    def wait(self, *values):
        self.last = tuple(values) + self.last


class Gather:
    def __init__(self, net, seq, shard):
        self.net, self.seq, self.stage = net, seq, 0
        self.held, self.coming = shard[None], None

    def send(self):
        (held,) = self.seq.after(self.held)
        self.held = held
        last = self.stage == self.net.stages()
        self.coming = lax.ppermute(held, AXES, self.net.core() if last else self.net.stage(self.stage))
        self.stage += 1

    def take(self):
        self.held, self.coming = self.seq.after(self.held, self.coming)
        if self.stage <= self.net.stages():
            self.held = jnp.concatenate([self.held, self.coming], axis=0)
        self.seq.wait(self.held, self.coming)

    def step(self):
        self.take()
        self.send()

    def finish(self):
        while self.stage <= self.net.stages():
            self.step()
        self.take()


def add(a, b):
    return (a.astype(F32) + b.astype(F32)).astype(BF16)


class Reduce:
    def __init__(self, net, seq, keep, send):
        self.net, self.seq, self.stage = net, seq, net.stages()
        self.keep = keep
        (send,) = seq.after(send)
        self.coming = lax.ppermute(send, AXES, net.core())

    def step(self):
        self.stage -= 1
        self.keep, self.coming = self.seq.after(self.keep, self.coming)
        half = self.keep.shape[0] // 2
        away = add(self.keep[half:], self.coming[half:])
        keep = add(self.keep[:half], self.coming[:half])
        self.keep, away = self.seq.after(keep, away)
        self.seq.wait(self.keep, away)
        self.coming = lax.ppermute(away, AXES, self.net.stage(self.stage))

    def end(self):
        while self.stage:
            self.step()
        self.keep, self.coming = self.seq.after(self.keep, self.coming)
        held = self.keep.astype(F32) + self.coming.astype(F32)
        self.seq.wait(held)
        return held[0]


def total_sum(net, value):
    value = value + lax.ppermute(value, AXES, net.core())
    for stage in range(net.stages()):
        value = value + lax.ppermute(value, AXES, net.stage(stage))
    return value


def body(
    dp,
    fsdp,
    block_input,
    cotangent,
    protein_lengths,
    weight_in,
    moment_in,
    square_in,
    weight_conv,
    moment_conv,
    square_conv,
    weight_out,
    moment_out,
    square_out,
    vectors,
    moment_vectors,
    square_vectors,
):
    net = Network(dp, fsdp, True)
    net_ends = Network(dp, fsdp, False)
    geo_in = Geometry(1, weight_in.shape[0], weight_in.shape[1])
    geo_conv = Geometry(KERNEL, weight_conv.shape[1], weight_conv.shape[2])
    geo_out = Geometry(1, weight_out.shape[0], weight_out.shape[1])
    geos = (geo_in, geo_conv, geo_out)

    def flat(v):
        return v.reshape(-1, v.shape[-1])

    me = jnp.stack([lax.axis_index("dp"), lax.axis_index("fsdp")]).astype(jnp.int32)
    ends = jnp.cumsum(protein_lengths[0]).astype(jnp.int32)
    vec = vectors.reshape(1, -1)
    x = block_input[0]
    cot = cotangent[0]

    seq = Sequence()
    shard_in = seq.run(functools.partial(pack_weights, (geo_in,)), weight_in)
    get_in = Gather(net_ends, seq, shard_in)
    get_in.send()
    shard_conv = seq.run(functools.partial(pack_weights, (geo_conv,)), flat(weight_conv))
    get_conv = Gather(net, seq, shard_conv)
    get_conv.send()
    shard_out = seq.run(functools.partial(pack_weights, (geo_out,)), weight_out)
    get_out = Gather(net, seq, shard_out)
    seq.wait(me, ends, vec)
    norms = seq.run(first_norm, x, cot, vec, first=0)
    biases = [norms[3]]
    for step in range(1, STEPS):
        get_in.step()
        get_conv.step()
        if step == 1:
            get_out.send()
        elif step == 2:
            get_out.step()
        norms = seq.run(
            lambda x, cot, vec, *held: first_norm(x, cot, vec, step, held), x, cot, vec, *norms[:3]
        )
        biases.append(norms[3])
    h1, h1_t, stat = norms[:3]
    grad_b3 = sum(biases)
    get_in.finish()
    h2, h2_t, n2, r2, full_in = seq.run(
        functools.partial(mix_one, net_ends, geo_in), me, get_in.held, get_in.coming, h1, vec
    )
    get_out.step()
    get_conv.step()
    get_conv.finish()
    get_out.step()
    h3, h3_t, n3, r3, full_conv = seq.run(
        functools.partial(mix_two, net, geo_conv),
        me, ends, get_conv.held, get_conv.coming, h2, vec,
    )
    get_out.step()
    pieces = seq.run(
        functools.partial(weight_gradient, net_ends, geo_out, name="out_gradient"), me, h3_t, cot
    )
    sum_out = Reduce(net_ends, seq, *pieces)
    get_out.finish()
    back_two, grad_g3, grad_s3, grad_b2, full_out = seq.run(
        functools.partial(back_through_out, net, geo_out),
        me, get_out.held, get_out.coming, cot, n3, r3, vec,
    )
    sum_out.step()
    keep, send, taps = seq.run(
        functools.partial(conv_gradient, net, geo_conv), me, ends, h2_t, back_two
    )
    sum_conv = Reduce(net, seq, keep, send)
    back_one, grad_g2, grad_s2, grad_b1 = seq.run(
        back_through_conv, taps, full_conv, n2, r2, vec
    )
    sum_conv.step()
    sum_out.step()
    pieces = seq.run(
        functools.partial(weight_gradient, net_ends, geo_in, name="in_gradient"),
        me, h1_t, back_one,
    )
    sum_in = Reduce(net_ends, seq, *pieces)
    block_output = seq.run(block_result, x, h3, full_out, vec)
    sum_in.step()
    sum_conv.step()
    sum_out.step()
    input_grad, grad_g1, grad_s1 = seq.run(
        back_through_in, back_one, full_in, x, cot, stat, vec
    )
    sum_in.step()
    sum_conv.step()
    sum_out.step()
    sum_in.step()
    sum_conv.step()
    grad_out = sum_out.end()
    partial = jnp.concatenate(
        [grad_g1, grad_s1, grad_g2, grad_s2, grad_g3, grad_s3, grad_b1, grad_b2, grad_b3], axis=1
    ).reshape(-1, 128)
    seq.wait(partial)
    sum_in.step()
    grad_conv = sum_conv.end()
    grad_in = sum_in.end()

    owned = (grad_in, grad_conv, grad_out)
    totals = total_sum(net, sum_squares(owned, partial))
    results = update_all(
        geos,
        owned,
        totals,
        (
            (weight_in, moment_in, square_in),
            (flat(weight_conv), flat(moment_conv), flat(square_conv)),
            (weight_out, moment_out, square_out),
        ),
        tuple(v.reshape(-1, 128) for v in (vectors, moment_vectors, square_vectors)),
    )
    norm, news = results[0], results[1:]
    return (
        block_output[None],
        input_grad[None],
        norm[0, 0],
        *news[0:3],
        *(v.reshape(weight_conv.shape) for v in news[3:6]),
        *news[6:9],
        *(v.reshape(-1) for v in news[9:12]),
    )


def solution(mesh):
    rows = P(("dp", "fsdp"), None, None)
    matrix = P("fsdp", "dp")
    taps = P(None, "fsdp", "dp")
    weights = (matrix,) * 3 + (taps,) * 3 + (matrix,) * 3 + (P(),) * 3
    return jax.shard_map(
        functools.partial(body, mesh.shape["dp"], mesh.shape["fsdp"]),
        mesh=mesh,
        in_specs=(rows, rows, P(("dp", "fsdp"), None)) + weights,
        out_specs=(rows, rows, P()) + weights,
        check_vma=False,
    )
```

```python
import functools

import jax
import jax.numpy as jnp
from jax import lax
from jax.experimental import pallas as pl
from jax.experimental.pallas import tpu as pltpu
from jax.sharding import PartitionSpec as P

D = 1280
INNER = 640
KERNEL = 5
DILATION = 64
LENGTH = 1024
STEP = 10
MARGIN = KERNEL // 2 * DILATION
OFFSETS = tuple((k - KERNEL // 2) * DILATION for k in range(KERNEL))
BLOCK = 256
STEPS = LENGTH // BLOCK

NORM_EPS = 1e-05
ADAM_EPS = 1e-08
BETA_ONE = 0.9
BETA_TWO = 0.95
CLIP_LIMIT = 1.0
RATE_MATRIX = 0.04
RATE_VECTOR = 0.3
DECAY_MATRIX = 0.1
GELU_C = 0.7978845608
GELU_K = 0.044715

GAIN_ONE, SHIFT_ONE = (0, 1280), (1280, 1280)
GAIN_TWO, SHIFT_TWO = (2560, 640), (3200, 640)
GAIN_THREE, SHIFT_THREE = (3840, 640), (4480, 640)
BIAS_ONE, BIAS_TWO, BIAS_THREE = (5120, 640), (5760, 640), (6400, 1280)

BF16 = jnp.bfloat16
F32 = jnp.float32
AXES = ("dp", "fsdp")
VMEM_LIMIT = 18 * 1024 * 1024
MIDDLE_LIMIT = 27 * 1024 * 1024
WIDE_LIMIT = 34 * 1024 * 1024
FLOPS_PER_US = 1.15e9
EFFORT = 4


def round16(n):
    return -(-n // 16) * 16


class Geometry:
    def __init__(self, taps, rows, cols):
        self.taps, self.rows, self.cols = taps, rows, cols
        self.height = taps * rows
        self.tiles, self.rest = divmod(cols, 128)
        self.groups = 128 // self.rest if self.rest and 128 % self.rest == 0 else 1
        self.tile_rows = round16(self.height)
        self.rest_rows = round16(-(-self.height // self.groups)) if self.rest else 0
        self.packed = self.tiles * self.tile_rows + self.rest_rows

    def pack(self, value):
        pieces = [value[:, 128 * t : 128 * t + 128] for t in range(self.tiles)]
        more = self.tile_rows - self.height
        if more:
            empty = jnp.zeros((more, 128), value.dtype)
            pieces = [jnp.concatenate([piece, empty], axis=0) for piece in pieces]
        if self.rest:
            rest = value[:, 128 * self.tiles :]
            spare = self.groups * self.rest_rows - self.height
            if spare:
                rest = jnp.concatenate([rest, jnp.zeros((spare, self.rest), value.dtype)], axis=0)
            n = self.rest_rows
            parts = [rest[n * g : n * g + n] for g in range(self.groups)]
            empty = 128 - self.groups * self.rest
            if empty:
                parts.append(jnp.zeros((n, empty), value.dtype))
            pieces.append(jnp.concatenate(parts, axis=1))
        return jnp.concatenate(pieces, axis=0)

    def unpack(self, packed):
        pieces = [
            packed[self.tile_rows * t : self.tile_rows * t + self.height]
            for t in range(self.tiles)
        ]
        if self.rest:
            base = self.tiles * self.tile_rows
            n, w = self.rest_rows, self.rest
            parts = []
            for g in range(self.groups):
                have = min(n, self.height - n * g)
                if have > 0:
                    parts.append(packed[base : base + have, w * g : w * g + w])
            pieces.append(jnp.concatenate(parts, axis=0))
        return jnp.concatenate(pieces, axis=1)


class Network:
    def __init__(self, dp, fsdp, far_first):
        self.dp, self.fsdp = dp, fsdp
        self.half = dp * fsdp // 2
        far = [("f", b) for b in range(fsdp.bit_length() - 2, 0, -1)]
        near = [("f", 0)] if fsdp > 1 else []
        rows = [("d", b) for b in range(dp.bit_length() - 2, 0, -1)]
        if far_first:
            self.order = (far + near + rows, far[::-1] + rows + near)
        else:
            self.order = (
                far[:1] + near + rows + far[1:],
                far[::-1][:1] + rows + near + far[::-1][1:],
            )

    def flip(self, stage, device):
        d, f = divmod(device, self.fsdp)
        kind, bit = self.order[d & 1][stage]
        if kind == "f":
            f ^= 1 << bit
        else:
            d ^= 1 << bit
        return d * self.fsdp + f

    def stage(self, stage):
        return [(i, self.flip(stage, i)) for i in range(self.dp * self.fsdp)]

    def core(self):
        return [(i, i ^ self.fsdp) for i in range(self.dp * self.fsdp)]

    def stages(self):
        return len(self.order[0])

    def slot(self, d, f, me_d, me_f):
        d_bits = jnp.bitwise_xor(me_d, d)
        f_bits = jnp.bitwise_xor(me_f, f)
        total = jnp.int32(0)
        for i, (kind, bit) in enumerate(self.order[d & 1]):
            source = f_bits if kind == "f" else d_bits
            total = total + (jnp.bitwise_and(lax.shift_right_logical(source, bit), 1) << i)
        return total


def call(kernel, name, out_shape, in_specs, out_specs, grid=(), scratch=(), us=1.0, aliases=None, vmem=VMEM_LIMIT):
    return pl.pallas_call(
        kernel,
        name=name,
        grid=grid,
        out_shape=out_shape,
        in_specs=in_specs,
        out_specs=out_specs,
        scratch_shapes=list(scratch),
        input_output_aliases=aliases or {},
        compiler_params=pltpu.CompilerParams(vmem_limit_bytes=vmem),
        cost_estimate=pl.CostEstimate(
            flops=int(EFFORT * us * FLOPS_PER_US), bytes_accessed=0, transcendentals=0
        ),
    )


def whole(shape):
    return pl.BlockSpec(shape, lambda *_: (0,) * len(shape))


def tokens(width, first=0):
    return pl.BlockSpec((BLOCK, width), lambda i: (first + i, 0))


SMEM = pl.BlockSpec(memory_space=pltpu.SMEM)
ANY = pl.BlockSpec(memory_space=pl.ANY)


def shape(dims, dtype):
    return jax.ShapeDtypeStruct(dims, dtype)


def part(vec_ref, span):
    return vec_ref[:, span[0] : span[0] + span[1]]


def add_rows(ref, value):
    ref[...] += jnp.sum(value, axis=0, keepdims=True)


HALF = LENGTH // 2


def for_halves(body, *sums):
    for ref in sums:
        ref[...] = jnp.zeros(ref.shape, ref.dtype)

    @pl.loop(0, 2)
    def _(step):
        body(pl.multiple_of(step * HALF, HALF))


def blocks_of(start):
    return [
        (slice(offset, offset + BLOCK), pl.ds(pl.multiple_of(start + offset, BLOCK), BLOCK))
        for offset in range(0, HALF, BLOCK)
    ]


def for_rows(count, size, loop, body):
    if loop:

        @pl.loop(0, count)
        def _(step):
            body(pl.ds(pl.multiple_of(step * size, size), size))
    else:
        for step in range(count):
            body(slice(step * size, step * size + size))


def statistics(values):
    width = values.shape[1]
    mean = jnp.sum(values, axis=1, keepdims=True) * (1.0 / width)
    center = values - mean
    spread = jnp.sum(center * center, axis=1, keepdims=True) * (1.0 / width)
    return center, lax.rsqrt(spread + NORM_EPS)


def gelu(a):
    t = jnp.tanh(GELU_C * (a + GELU_K * (a * a * a)))
    return 0.5 * a * (1.0 + t)


def gelu_slope(a):
    square = a * a
    t = jnp.tanh(GELU_C * a * (1.0 + GELU_K * square))
    half = 0.5 * (1.0 + t)
    return half + half * (1.0 - t) * a * (GELU_C + (3.0 * GELU_C * GELU_K) * square)


def norm_backward(grad, normed, root, gain, shift):
    width = grad.shape[1]
    d_a = grad * gelu_slope(normed * gain + shift)
    scaled = d_a * gain
    mean_one = jnp.sum(scaled, axis=1, keepdims=True) * (1.0 / width)
    mean_two = jnp.sum(scaled * normed, axis=1, keepdims=True) * (1.0 / width)
    return root * (scaled - mean_one - normed * mean_two), d_a * normed, d_a


def build_taps(ends_ref, source, padded, target, sign):
    width = source.shape[1]
    count = ends_ref.shape[0]
    empty = jnp.zeros((MARGIN, width), BF16)
    padded[0:MARGIN] = empty
    padded[MARGIN : MARGIN + LENGTH] = source[...]
    padded[MARGIN + LENGTH : MARGIN + LENGTH + MARGIN] = empty

    @pl.loop(0, STEPS)
    def _(step):
        start = pl.multiple_of(step * BLOCK, BLOCK)
        position = start + lax.broadcasted_iota(jnp.int32, (BLOCK, 128), 0)
        lower = jnp.zeros((BLOCK, 128), jnp.int32)
        upper = jnp.full((BLOCK, 128), ends_ref[count - 1], jnp.int32)
        for j in range(count - 1):
            lower = jnp.where(position >= ends_ref[j], ends_ref[j], lower)
        for j in range(count - 2, -1, -1):
            upper = jnp.where(position < ends_ref[j], ends_ref[j], upper)
        for k in range(KERNEL):
            offset = sign * OFFSETS[k]
            moved = position + offset
            mask = jnp.where((moved >= lower) & (moved < upper), 1.0, 0.0).astype(BF16)
            mask = jnp.concatenate([mask] * (width // 128), axis=1)
            value = padded[pl.ds(pl.multiple_of(start + MARGIN + offset, DILATION), BLOCK)]
            target[pl.ds(start, BLOCK), k * width : k * width + width] = value * mask


def build_taps_unrolled(ends_ref, source, target, sign):
    width = source.shape[1]
    count = ends_ref.shape[0]
    for rows in (slice(start, start + BLOCK) for start in range(0, LENGTH, BLOCK)):
        position = rows.start + lax.broadcasted_iota(jnp.int32, (BLOCK, 128), 0)
        lower = jnp.zeros((BLOCK, 128), jnp.int32)
        upper = jnp.full((BLOCK, 128), ends_ref[count - 1], jnp.int32)
        for j in range(count - 1):
            lower = jnp.where(position >= ends_ref[j], ends_ref[j], lower)
        for j in range(count - 2, -1, -1):
            upper = jnp.where(position < ends_ref[j], ends_ref[j], upper)
        for k in range(KERNEL):
            offset = sign * OFFSETS[k]
            moved = position + offset
            mask = jnp.where((moved >= lower) & (moved < upper), 1.0, 0.0).astype(BF16)
            mask = jnp.concatenate([mask] * (width // 128), axis=1)
            columns = slice(k * width, k * width + width)
            start = max(rows.start, -offset)
            stop = min(rows.stop, LENGTH - offset)
            value = source[start + offset : stop + offset]
            target[start:stop, columns] = value * mask[start - rows.start : stop - rows.start]
            if rows.start < start:
                target[rows.start : start, columns] = jnp.zeros((start - rows.start, width), BF16)
            if stop < rows.stop:
                target[stop : rows.stop, columns] = jnp.zeros((rows.stop - stop, width), BF16)


def dot(a, b):
    return jnp.dot(a, b, preferred_element_type=F32)


def dot_nt(a, b):
    return lax.dot_general(a, b, (((1,), (1,)), ((), ())), preferred_element_type=F32)


def assemble(net, geo, me_ref, own, peer, buffer, sems, full, beside=None, loop=False):
    core = jnp.bitwise_and(me_ref[0], 1)
    first = pltpu.make_async_copy(own, buffer.at[core], sems.at[0])
    second = pltpu.make_async_copy(peer, buffer.at[1 - core], sems.at[1])
    first.start()
    second.start()
    first.wait()
    second.wait()
    width = net.dp * geo.cols

    def body(f, first_row):
        blocks = [
            geo.unpack(buffer[d & 1, net.slot(d, f, me_ref[0], me_ref[1])])
            for d in range(net.dp)
        ]
        row = jnp.concatenate(blocks, axis=1)
        for k in range(geo.taps):
            value = row[k * geo.rows : k * geo.rows + geo.rows]
            full[pl.ds(k * geo.rows * net.fsdp + first_row, geo.rows)] = value
            if beside is not None:
                beside[pl.ds(first_row, geo.rows), k * width : k * width + width] = value

    if loop and geo.rows % 16 == 0:

        @pl.loop(0, net.fsdp)
        def _(f):
            body(f, pl.multiple_of(f * geo.rows, 16))
    else:
        for f in range(net.fsdp):
            body(f, f * geo.rows)


def distribute(net, geo, me_ref, full, buffer, sems, keep, send):
    width = net.dp * geo.cols
    for f in range(net.fsdp):
        pieces = [
            full[f * geo.rows : f * geo.rows + geo.rows, k * width : k * width + width]
            for k in range(geo.taps)
        ]
        row = pieces[0] if geo.taps == 1 else jnp.concatenate(pieces, axis=0)
        for d in range(net.dp):
            buffer[d & 1, net.slot(d, f, me_ref[0], me_ref[1])] = geo.pack(
                row[:, d * geo.cols : d * geo.cols + geo.cols]
            )
    core = jnp.bitwise_and(me_ref[0], 1)
    first = pltpu.make_async_copy(buffer.at[1 - core], send, sems.at[0])
    second = pltpu.make_async_copy(buffer.at[core], keep, sems.at[1])
    first.start()
    second.start()
    first.wait()
    second.wait()


def slots(net, geo):
    return (net.half, geo.packed, 128)


def piece_scratch(net, geo):
    return [pltpu.VMEM((2,) + slots(net, geo), BF16), pltpu.SemaphoreType.DMA((2,))]


def pack_weights(geos, *weights):
    rows = sum(geo.packed for geo in geos)

    def kernel(*refs):
        start = 0
        for geo, source in zip(geos, refs):
            refs[-1][start : start + geo.packed] = geo.pack(source[...].astype(BF16))
            start += geo.packed

    return call(
        kernel,
        "pack_weights",
        shape((rows, 128), BF16),
        [whole(w.shape) for w in weights],
        whole((rows, 128)),
        us=1.0,
    )(*weights)


def first_norm(block_input, cotangent, vec, first, held=()):
    def kernel(x_ref, cot_ref, vec_ref, *refs):
        h_ref, ht_ref, stat_ref, bias_ref = refs[-4:]

        def body(rows):
            values = x_ref[rows].astype(F32)
            center, root = statistics(values)
            normed = center * root
            hidden = gelu(normed * part(vec_ref, GAIN_ONE) + part(vec_ref, SHIFT_ONE)).astype(BF16)
            h_ref[rows] = hidden
            ht_ref[:, rows] = hidden.T
            lane = lax.broadcasted_iota(jnp.int32, (BLOCK // 2, 128), 1)
            stat_ref[rows] = jnp.where(lane == 0, values[:, :1] - center[:, :1], root)
            bias_ref[...] += jnp.sum(cot_ref[rows].astype(F32), axis=0, keepdims=True)

        @pl.when(pl.program_id(0) == 0)
        def _():
            bias_ref[...] = jnp.zeros((1, D), F32)

        for_rows(2, BLOCK // 2, True, body)

    return call(
        kernel,
        "first_norm",
        [
            shape((LENGTH, D), BF16),
            shape((D, LENGTH), BF16),
            shape((LENGTH, 128), F32),
            shape((1, D), F32),
        ],
        [tokens(D, first), tokens(D, first), whole(vec.shape)] + [ANY] * len(held),
        [
            tokens(D, first),
            pl.BlockSpec((D, BLOCK), lambda i: (0, first + i)),
            tokens(128, first),
            whole((1, D)),
        ],
        grid=(2,),
        aliases={3 + i: i for i in range(len(held))},
        us=2.8,
    )(block_input, cotangent, vec, *held)


def norm_out(rows, mixed, vec_ref, gain, shift_span, h_ref, ht_ref, normed_ref, root_ref):
    center, root = statistics(mixed)
    normed = center * root
    hidden = gelu(normed * part(vec_ref, gain) + part(vec_ref, shift_span)).astype(BF16)
    h_ref[rows] = hidden
    ht_ref[:, rows] = hidden.T
    normed_ref[rows] = normed
    root_ref[rows] = jnp.broadcast_to(root, (root.shape[0], 128))


NORM_SHAPES = [
    shape((LENGTH, INNER), BF16),
    shape((INNER, LENGTH), BF16),
    shape((LENGTH, INNER), F32),
    shape((LENGTH, 128), F32),
]


def wholes(shapes):
    return [whole(s.shape) for s in shapes]


def mix_one(net, geo, me, own, peer, hidden_one, vec):
    def kernel(me_ref, own_ref, peer_ref, h1_ref, vec_ref, h_ref, ht_ref, n_ref, r_ref, full, buf, sems):
        assemble(net, geo, me_ref, own_ref, peer_ref, buf, sems, full, loop=True)

        def body(rows):
            mixed = dot(h1_ref[rows], full[...]) + part(vec_ref, BIAS_ONE)
            norm_out(rows, mixed, vec_ref, GAIN_TWO, SHIFT_TWO, h_ref, ht_ref, n_ref, r_ref)

        for_rows(2 * STEPS, BLOCK // 2, True, body)

    outs = NORM_SHAPES + [shape((D, INNER), BF16)]
    return call(
        kernel,
        "mix_one",
        outs,
        [SMEM, ANY, ANY, whole((LENGTH, D)), whole(vec.shape)],
        wholes(outs),
        scratch=piece_scratch(net, geo),
        us=0.01,
    )(me, own, peer, hidden_one, vec)


def mix_two(net, geo, me, ends, own, peer, hidden_two, vec):
    def kernel(
        me_ref, ends_ref, own_ref, peer_ref, h2_ref, vec_ref, h_ref, ht_ref, n_ref, r_ref, beside, full, buf, sems, taps
    ):
        assemble(net, geo, me_ref, own_ref, peer_ref, buf, sems, full, beside)
        build_taps_unrolled(ends_ref, h2_ref, taps, 1)
        n_ref[...] = dot(taps[...], full[...])

        def body(rows):
            mixed = n_ref[rows] + part(vec_ref, BIAS_TWO)
            norm_out(rows, mixed, vec_ref, GAIN_THREE, SHIFT_THREE, h_ref, ht_ref, n_ref, r_ref)

        for_rows(STEPS, BLOCK, False, body)

    outs = NORM_SHAPES + [shape((INNER, KERNEL * INNER), BF16)]
    return call(
        kernel,
        "mix_two",
        outs,
        [SMEM, SMEM, ANY, ANY, whole((LENGTH, INNER)), whole(vec.shape)],
        wholes(outs),
        scratch=[pltpu.VMEM((KERNEL * INNER, INNER), BF16)]
        + piece_scratch(net, geo)
        + [
            pltpu.VMEM((LENGTH, KERNEL * INNER), BF16),
        ],
        us=11.7,
        vmem=WIDE_LIMIT,
    )(me, ends, own, peer, hidden_two, vec)


def norm_in(product, vec_ref, gain, shift_span, grad, n_ref, r_ref, back_ref, *sums):
    def body(start):
        grad[...] = product(pl.ds(start, HALF))
        for part_rows, rows in blocks_of(start):
            back, to_gain, to_shift = norm_backward(
                grad[part_rows],
                n_ref[rows],
                r_ref[rows][:, :1],
                part(vec_ref, gain),
                part(vec_ref, shift_span),
            )
            back = back.astype(BF16)
            back_ref[rows] = back
            for ref, value in zip(sums, (to_gain, to_shift, back.astype(F32))):
                add_rows(ref, value)

    for_halves(body, *sums)


def gradient_shapes(net, geo):
    return [shape(slots(net, geo), BF16)] * 2


def weight_gradient(net, geo, me, left, right, name="weight_gradient"):
    dims = (left.shape[0], right.shape[1])

    def kernel(me_ref, left_ref, right_ref, keep, send, full, buf, sems):
        full[...] = dot(left_ref[...], right_ref[...]).astype(BF16)
        distribute(net, geo, me_ref, full, buf, sems, keep, send)

    return call(
        kernel,
        name,
        gradient_shapes(net, geo),
        [SMEM, whole(left.shape), whole(right.shape)],
        [ANY, ANY],
        scratch=[pltpu.VMEM(dims, BF16)] + piece_scratch(net, geo),
        us=3.0 if dims[0] < dims[1] else 3.7,
    )(me, left, right)


def back_through_out(net, geo, me, own, peer, cotangent, normed, root, vec):
    def kernel(
        me_ref, own_ref, peer_ref, cot_ref, n_ref, r_ref, vec_ref, back_ref, gg_ref, gs_ref, gb_ref, full, buf, sems, grad
    ):
        assemble(net, geo, me_ref, own_ref, peer_ref, buf, sems, full)

        def product(rows):
            return dot_nt(cot_ref[rows], full[...])

        norm_in(product, vec_ref, GAIN_THREE, SHIFT_THREE, grad, n_ref, r_ref, back_ref, gg_ref, gs_ref, gb_ref)

    row = shape((1, INNER), F32)
    outs = [shape((LENGTH, INNER), BF16), row, row, row, shape((INNER, D), BF16)]
    return call(
        kernel,
        "back_through_out",
        outs,
        [SMEM, ANY, ANY] + wholes((cotangent, normed, root, vec)),
        wholes(outs),
        scratch=piece_scratch(net, geo) + [pltpu.VMEM((HALF, INNER), F32)],
        us=6.4,
    )(me, own, peer, cotangent, normed, root, vec)


def block_result(block_input, hidden_three, full_out, vec):
    half = LENGTH // 2

    def kernel(x_ref, h_ref, w_ref, vec_ref, out_ref):
        branch = dot(h_ref[...], w_ref[...]) + part(vec_ref, BIAS_THREE)
        out_ref[...] = (x_ref[...].astype(F32) + branch).astype(BF16)

    def rows_of(width):
        return pl.BlockSpec((half, width), lambda i: (i, 0))

    return call(
        kernel,
        "block_result",
        shape((LENGTH, D), BF16),
        [rows_of(D), rows_of(INNER), whole((INNER, D)), whole(vec.shape)],
        rows_of(D),
        grid=(2,),
        us=3.8,
    )(block_input, hidden_three, full_out, vec)


def conv_gradient(net, geo, me, ends, hidden_two_t, back_two):
    step = 2 * INNER
    width = KERNEL * INNER

    def kernel(me_ref, ends_ref, left_ref, back_ref, keep, send, taps, full, buf, sems, pad):
        build_taps(ends_ref, back_ref, pad, taps, -1)
        for start in range(0, width, step):
            columns = slice(start, min(start + step, width))
            full[:, columns] = dot(left_ref[...], taps[:, columns]).astype(BF16)
        distribute(net, geo, me_ref, full, buf, sems, keep, send)

    outs = gradient_shapes(net, geo) + [shape((LENGTH, width), BF16)]
    return call(
        kernel,
        "conv_gradient",
        outs,
        [SMEM, SMEM, whole((INNER, LENGTH)), whole((LENGTH, INNER))],
        [ANY, ANY, whole((LENGTH, width))],
        scratch=[pltpu.VMEM((INNER, width), BF16)]
        + piece_scratch(net, geo)
        + [pltpu.VMEM((LENGTH + 2 * MARGIN, INNER), BF16)],
        us=8.0,
        vmem=MIDDLE_LIMIT,
    )(me, ends, hidden_two_t, back_two)


def back_through_conv(taps, full_conv, normed, root, vec):
    def kernel(taps_ref, w_ref, n_ref, r_ref, vec_ref, back_ref, gg_ref, gs_ref, gb_ref, grad):
        def product(rows):
            return dot_nt(taps_ref[rows], w_ref[...])

        norm_in(product, vec_ref, GAIN_TWO, SHIFT_TWO, grad, n_ref, r_ref, back_ref, gg_ref, gs_ref, gb_ref)

    row = shape((1, INNER), F32)
    outs = [shape((LENGTH, INNER), BF16), row, row, row]
    return call(
        kernel,
        "back_through_conv",
        outs,
        wholes((taps, full_conv, normed, root, vec)),
        wholes(outs),
        scratch=[pltpu.VMEM((HALF, INNER), F32)],
        us=10.0,
    )(taps, full_conv, normed, root, vec)


def back_through_in(back_one, full_in, block_input, cotangent, stat, vec):
    def kernel(back_ref, w_ref, x_ref, cot_ref, stat_ref, vec_ref, out_ref, gg_ref, gs_ref, grad):
        @pl.when(pl.program_id(0) == 0)
        def _():
            gg_ref[...] = jnp.zeros((1, D), F32)
            gs_ref[...] = jnp.zeros((1, D), F32)

        grad[...] = dot_nt(back_ref[...], w_ref[...])
        for start in range(0, HALF, BLOCK):
            rows = slice(start, start + BLOCK)
            root = stat_ref[rows, 1:2]
            normed = (x_ref[rows].astype(F32) - stat_ref[rows, :1]) * root
            back, to_gain, to_shift = norm_backward(
                grad[rows], normed, root, part(vec_ref, GAIN_ONE), part(vec_ref, SHIFT_ONE)
            )
            out_ref[rows] = (cot_ref[rows].astype(F32) + back).astype(BF16)
            add_rows(gg_ref, to_gain)
            add_rows(gs_ref, to_shift)

    def rows_of(width):
        return pl.BlockSpec((HALF, width), lambda i: (i, 0))

    row = shape((1, D), F32)
    return call(
        kernel,
        "back_through_in",
        [shape((LENGTH, D), BF16), row, row],
        [rows_of(INNER), whole((D, INNER)), rows_of(D), rows_of(D), rows_of(128), whole(vec.shape)],
        [rows_of(D)] + [whole((1, D))] * 2,
        grid=(2,),
        scratch=[pltpu.VMEM((HALF, D), F32)],
        us=9.4,
    )(back_one, full_in, block_input, cotangent, stat, vec)


def sum_squares(owned, pieces):
    rows = sum(piece.shape[1] for piece in pieces) // 128
    total_rows = -(-(rows + 1) // 8) * 8
    n = len(owned)

    def kernel(*refs):
        out = refs[-1]
        total = jnp.zeros((1, 128), F32)
        for ref in refs[:n]:
            value = ref[...]
            total = total + jnp.sum(value * value, axis=0, keepdims=True)
        out[...] = jnp.zeros(out.shape, F32)
        row = 0
        for ref in refs[n:-1]:
            for start in range(0, ref.shape[1], 128):
                out[row : row + 1] = ref[:, start : start + 128]
                row += 1
        out[rows : rows + 1] = total

    return call(
        kernel,
        "sum_squares",
        shape((total_rows, 128), F32),
        [whole(v.shape) for v in (*owned, *pieces)],
        whole((total_rows, 128)),
        us=0.3,
    )(*owned, *pieces)


def adamw(weight, moment, square, gradient, rate, decay):
    new_moment = BETA_ONE * moment + (1.0 - BETA_ONE) * gradient
    new_square = BETA_TWO * square + (1.0 - BETA_TWO) * gradient * gradient
    moment_hat = new_moment * (1.0 / (1.0 - BETA_ONE**STEP))
    square_hat = new_square * (1.0 / (1.0 - BETA_TWO**STEP))
    update = moment_hat / (jnp.sqrt(square_hat) + ADAM_EPS)
    return weight - rate * (update + decay * weight), new_moment, new_square


def update_all(geos, owned, totals, weights, vectors):
    n = len(geos)
    size = vectors[0].shape[0]

    def kernel(*refs):
        owned_refs, total_ref = refs[:n], refs[n]
        ins = refs[n + 1 : n + 1 + 3 * n + 3]
        outs, held = refs[n + 1 + 3 * n + 3 : -1], refs[-1]

        def update(i, rows, gradient):
            weight, moment, square = (r[rows] for r in ins[3 * i : 3 * i + 3])
            results = adamw(weight, moment, square, gradient, RATE_MATRIX, DECAY_MATRIX)
            for ref, value in zip(outs[1 + 3 * i : 4 + 3 * i], results):
                ref[rows] = value

        grad_vec = total_ref[0:size]
        squares = jnp.sum(grad_vec * grad_vec, axis=0, keepdims=True) + total_ref[size : size + 1]
        norm = jnp.sqrt(jnp.sum(squares, axis=1, keepdims=True))
        outs[0][...] = norm
        clip = jnp.minimum(1.0, CLIP_LIMIT / (norm + 1e-06))
        for i, geo in enumerate(geos):
            gradient = geo.unpack(owned_refs[i][...].astype(F32)) * clip
            if geo.taps == 1 or geo.rows % 8:
                update(i, slice(None), gradient)
            else:
                held[...] = gradient

                @pl.loop(0, geo.taps)
                def _(k):
                    rows = pl.ds(pl.multiple_of(k * geo.rows, 8), geo.rows)
                    update(i, rows, held[rows])

        weight, moment, square = (r[...] for r in ins[3 * n :])
        results = adamw(weight, moment, square, grad_vec * clip, RATE_VECTOR, 0.0)
        for ref, value in zip(outs[1 + 3 * n :], results):
            ref[...] = value

    args = list(owned) + [totals] + [v for group in weights for v in group] + list(vectors)
    outs = [shape((1, 1), F32)]
    outs += [shape(v.shape, F32) for group in weights for v in group]
    outs += [shape(v.shape, F32) for v in vectors]
    return call(
        kernel,
        "update_all",
        outs,
        [whole(v.shape) for v in args],
        [whole(o.shape) for o in outs],
        scratch=[pltpu.VMEM(weights[1][0].shape, F32)],
        us=2.0,
    )(*args)


class Sequence:
    def __init__(self):
        self.last = ()

    def after(self, *values):
        return lax.optimization_barrier(tuple(values) + self.last)[: len(values)]

    def run(self, function, *values, **options):
        result = function(*self.after(*values), **options)
        self.last = tuple(jax.tree.leaves(result))[-1:]
        return result

    def wait(self, *values):
        self.last = tuple(values) + self.last


class Gather:
    def __init__(self, net, seq, shard):
        self.net, self.seq, self.stage = net, seq, 0
        self.held, self.coming = shard[None], None

    def send(self):
        (held,) = self.seq.after(self.held)
        self.held = held
        last = self.stage == self.net.stages()
        self.coming = lax.ppermute(held, AXES, self.net.core() if last else self.net.stage(self.stage))
        self.stage += 1

    def take(self):
        self.held, self.coming = self.seq.after(self.held, self.coming)
        if self.stage <= self.net.stages():
            self.held = jnp.concatenate([self.held, self.coming], axis=0)
        self.seq.wait(self.held, self.coming)

    def step(self):
        self.take()
        self.send()

    def finish(self):
        while self.stage <= self.net.stages():
            self.step()
        self.take()


def add(a, b):
    return (a.astype(F32) + b.astype(F32)).astype(BF16)


class Reduce:
    def __init__(self, net, seq, keep, send):
        self.net, self.seq, self.stage = net, seq, net.stages()
        self.keep = keep
        (send,) = seq.after(send)
        self.coming = lax.ppermute(send, AXES, net.core())

    def step(self):
        self.stage -= 1
        self.keep, self.coming = self.seq.after(self.keep, self.coming)
        half = self.keep.shape[0] // 2
        away = add(self.keep[half:], self.coming[half:])
        keep = add(self.keep[:half], self.coming[:half])
        self.keep, away = self.seq.after(keep, away)
        self.seq.wait(self.keep, away)
        self.coming = lax.ppermute(away, AXES, self.net.stage(self.stage))

    def end(self):
        while self.stage:
            self.step()
        self.keep, self.coming = self.seq.after(self.keep, self.coming)
        held = self.keep.astype(F32) + self.coming.astype(F32)
        self.seq.wait(held)
        return held[0]


def total_sum(net, value):
    value = value + lax.ppermute(value, AXES, net.core())
    for stage in range(net.stages()):
        value = value + lax.ppermute(value, AXES, net.stage(stage))
    return value


def body(
    dp,
    fsdp,
    block_input,
    cotangent,
    protein_lengths,
    weight_in,
    moment_in,
    square_in,
    weight_conv,
    moment_conv,
    square_conv,
    weight_out,
    moment_out,
    square_out,
    vectors,
    moment_vectors,
    square_vectors,
):
    net = Network(dp, fsdp, True)
    net_ends = Network(dp, fsdp, False)
    geo_in = Geometry(1, weight_in.shape[0], weight_in.shape[1])
    geo_conv = Geometry(KERNEL, weight_conv.shape[1], weight_conv.shape[2])
    geo_out = Geometry(1, weight_out.shape[0], weight_out.shape[1])
    geos = (geo_in, geo_conv, geo_out)

    def flat(v):
        return v.reshape(-1, v.shape[-1])

    me = jnp.stack([lax.axis_index("dp"), lax.axis_index("fsdp")]).astype(jnp.int32)
    ends = jnp.cumsum(protein_lengths[0]).astype(jnp.int32)
    vec = vectors.reshape(1, -1)
    x = block_input[0]
    cot = cotangent[0]

    seq = Sequence()
    shard_in = seq.run(functools.partial(pack_weights, (geo_in,)), weight_in)
    get_in = Gather(net_ends, seq, shard_in)
    get_in.send()
    shard_conv = seq.run(functools.partial(pack_weights, (geo_conv,)), flat(weight_conv))
    get_conv = Gather(net, seq, shard_conv)
    get_conv.send()
    shard_out = seq.run(functools.partial(pack_weights, (geo_out,)), weight_out)
    get_out = Gather(net, seq, shard_out)
    seq.wait(me, ends, vec)
    norms = seq.run(first_norm, x, cot, vec, first=0)
    get_in.step()
    get_conv.step()
    get_out.send()
    h1, h1_t, stat, half_b3 = seq.run(
        lambda x, cot, vec, *held: first_norm(x, cot, vec, STEPS // 2, held), x, cot, vec, *norms[:3]
    )
    grad_b3 = norms[3] + half_b3
    get_in.step()
    get_conv.step()
    get_out.step()
    get_in.step()
    get_conv.step()
    get_in.finish()
    h2, h2_t, n2, r2, full_in = seq.run(
        functools.partial(mix_one, net_ends, geo_in), me, get_in.held, get_in.coming, h1, vec
    )
    get_out.step()
    get_conv.step()
    get_conv.finish()
    get_out.step()
    h3, h3_t, n3, r3, full_conv = seq.run(
        functools.partial(mix_two, net, geo_conv),
        me, ends, get_conv.held, get_conv.coming, h2, vec,
    )
    get_out.step()
    pieces = seq.run(
        functools.partial(weight_gradient, net_ends, geo_out, name="out_gradient"), me, h3_t, cot
    )
    sum_out = Reduce(net_ends, seq, *pieces)
    get_out.finish()
    back_two, grad_g3, grad_s3, grad_b2, full_out = seq.run(
        functools.partial(back_through_out, net, geo_out),
        me, get_out.held, get_out.coming, cot, n3, r3, vec,
    )
    sum_out.step()
    keep, send, taps = seq.run(
        functools.partial(conv_gradient, net, geo_conv), me, ends, h2_t, back_two
    )
    sum_conv = Reduce(net, seq, keep, send)
    back_one, grad_g2, grad_s2, grad_b1 = seq.run(
        back_through_conv, taps, full_conv, n2, r2, vec
    )
    sum_conv.step()
    sum_out.step()
    pieces = seq.run(
        functools.partial(weight_gradient, net_ends, geo_in, name="in_gradient"),
        me, h1_t, back_one,
    )
    sum_in = Reduce(net_ends, seq, *pieces)
    block_output = seq.run(block_result, x, h3, full_out, vec)
    sum_in.step()
    sum_conv.step()
    sum_out.step()
    input_grad, grad_g1, grad_s1 = seq.run(
        back_through_in, back_one, full_in, x, cot, stat, vec
    )
    sum_in.step()
    sum_conv.step()
    sum_out.step()
    sum_in.step()
    sum_conv.step()
    grad_out = sum_out.end()
    sum_in.step()
    grad_conv = sum_conv.end()
    grad_in = sum_in.end()

    owned = (grad_in, grad_conv, grad_out)
    pieces = (grad_g1, grad_s1, grad_g2, grad_s2, grad_g3, grad_s3, grad_b1, grad_b2, grad_b3)
    totals = total_sum(net, sum_squares(owned, pieces))
    results = update_all(
        geos,
        owned,
        totals,
        (
            (weight_in, moment_in, square_in),
            (flat(weight_conv), flat(moment_conv), flat(square_conv)),
            (weight_out, moment_out, square_out),
        ),
        tuple(v.reshape(-1, 128) for v in (vectors, moment_vectors, square_vectors)),
    )
    norm, news = results[0], results[1:]
    return (
        block_output[None],
        input_grad[None],
        norm[0, 0],
        *news[0:3],
        *(v.reshape(weight_conv.shape) for v in news[3:6]),
        *news[6:9],
        *(v.reshape(-1) for v in news[9:12]),
    )


def solution(mesh):
    rows = P(("dp", "fsdp"), None, None)
    matrix = P("fsdp", "dp")
    taps = P(None, "fsdp", "dp")
    weights = (matrix,) * 3 + (taps,) * 3 + (matrix,) * 3 + (P(),) * 3
    return jax.shard_map(
        functools.partial(body, mesh.shape["dp"], mesh.shape["fsdp"]),
        mesh=mesh,
        in_specs=(rows, rows, P(("dp", "fsdp"), None)) + weights,
        out_specs=(rows, rows, P()) + weights,
        check_vma=False,
    )
```

```python
import functools

import jax
import jax.numpy as jnp
from jax import lax
from jax.experimental import pallas as pl
from jax.experimental.pallas import tpu as pltpu
from jax.sharding import PartitionSpec as P

D = 1280
INNER = 640
KERNEL = 5
DILATION = 64
LENGTH = 1024
STEP = 10
MARGIN = KERNEL // 2 * DILATION
OFFSETS = tuple((k - KERNEL // 2) * DILATION for k in range(KERNEL))
BLOCK = 256
STEPS = LENGTH // BLOCK

NORM_EPS = 1e-05
ADAM_EPS = 1e-08
BETA_ONE = 0.9
BETA_TWO = 0.95
CLIP_LIMIT = 1.0
RATE_MATRIX = 0.04
RATE_VECTOR = 0.3
DECAY_MATRIX = 0.1
GELU_C = 0.7978845608
GELU_K = 0.044715

GAIN_ONE, SHIFT_ONE = (0, 1280), (1280, 1280)
GAIN_TWO, SHIFT_TWO = (2560, 640), (3200, 640)
GAIN_THREE, SHIFT_THREE = (3840, 640), (4480, 640)
BIAS_ONE, BIAS_TWO, BIAS_THREE = (5120, 640), (5760, 640), (6400, 1280)

BF16 = jnp.bfloat16
F32 = jnp.float32
AXES = ("dp", "fsdp")
VMEM_LIMIT = 18 * 1024 * 1024
MIDDLE_LIMIT = 27 * 1024 * 1024
WIDE_LIMIT = 34 * 1024 * 1024
FLOPS_PER_US = 1.15e9
EFFORT = 4


def round16(n):
    return -(-n // 16) * 16


class Geometry:
    def __init__(self, taps, rows, cols):
        self.taps, self.rows, self.cols = taps, rows, cols
        self.height = taps * rows
        self.tiles, self.rest = divmod(cols, 128)
        self.groups = 128 // self.rest if self.rest and 128 % self.rest == 0 else 1
        self.tile_rows = round16(self.height)
        self.rest_rows = round16(-(-self.height // self.groups)) if self.rest else 0
        self.packed = self.tiles * self.tile_rows + self.rest_rows

    def pack(self, value):
        pieces = [value[:, 128 * t : 128 * t + 128] for t in range(self.tiles)]
        more = self.tile_rows - self.height
        if more:
            empty = jnp.zeros((more, 128), value.dtype)
            pieces = [jnp.concatenate([piece, empty], axis=0) for piece in pieces]
        if self.rest:
            rest = value[:, 128 * self.tiles :]
            spare = self.groups * self.rest_rows - self.height
            if spare:
                rest = jnp.concatenate([rest, jnp.zeros((spare, self.rest), value.dtype)], axis=0)
            n = self.rest_rows
            parts = [rest[n * g : n * g + n] for g in range(self.groups)]
            empty = 128 - self.groups * self.rest
            if empty:
                parts.append(jnp.zeros((n, empty), value.dtype))
            pieces.append(jnp.concatenate(parts, axis=1))
        return jnp.concatenate(pieces, axis=0)

    def unpack(self, packed):
        pieces = [
            packed[self.tile_rows * t : self.tile_rows * t + self.height]
            for t in range(self.tiles)
        ]
        if self.rest:
            base = self.tiles * self.tile_rows
            n, w = self.rest_rows, self.rest
            parts = []
            for g in range(self.groups):
                have = min(n, self.height - n * g)
                if have > 0:
                    parts.append(packed[base : base + have, w * g : w * g + w])
            pieces.append(jnp.concatenate(parts, axis=0))
        return jnp.concatenate(pieces, axis=1)


class Network:
    def __init__(self, dp, fsdp, far_first):
        self.dp, self.fsdp = dp, fsdp
        self.half = dp * fsdp // 2
        far = [("f", b) for b in range(fsdp.bit_length() - 2, 0, -1)]
        near = [("f", 0)] if fsdp > 1 else []
        rows = [("d", b) for b in range(dp.bit_length() - 2, 0, -1)]
        if far_first:
            self.order = (far + near + rows, far[::-1] + rows + near)
        else:
            self.order = (
                far[:1] + near + rows + far[1:],
                far[::-1][:1] + rows + near + far[::-1][1:],
            )

    def flip(self, stage, device):
        d, f = divmod(device, self.fsdp)
        kind, bit = self.order[d & 1][stage]
        if kind == "f":
            f ^= 1 << bit
        else:
            d ^= 1 << bit
        return d * self.fsdp + f

    def stage(self, stage):
        return [(i, self.flip(stage, i)) for i in range(self.dp * self.fsdp)]

    def core(self):
        return [(i, i ^ self.fsdp) for i in range(self.dp * self.fsdp)]

    def stages(self):
        return len(self.order[0])

    def slot(self, d, f, me_d, me_f):
        d_bits = jnp.bitwise_xor(me_d, d)
        f_bits = jnp.bitwise_xor(me_f, f)
        total = jnp.int32(0)
        for i, (kind, bit) in enumerate(self.order[d & 1]):
            source = f_bits if kind == "f" else d_bits
            total = total + (jnp.bitwise_and(lax.shift_right_logical(source, bit), 1) << i)
        return total


def call(kernel, name, out_shape, in_specs, out_specs, grid=(), scratch=(), us=1.0, aliases=None, vmem=VMEM_LIMIT):
    return pl.pallas_call(
        kernel,
        name=name,
        grid=grid,
        out_shape=out_shape,
        in_specs=in_specs,
        out_specs=out_specs,
        scratch_shapes=list(scratch),
        input_output_aliases=aliases or {},
        compiler_params=pltpu.CompilerParams(vmem_limit_bytes=vmem),
        cost_estimate=pl.CostEstimate(
            flops=int(EFFORT * us * FLOPS_PER_US), bytes_accessed=0, transcendentals=0
        ),
    )


def whole(shape):
    return pl.BlockSpec(shape, lambda *_: (0,) * len(shape))


def tokens(width, first=0):
    return pl.BlockSpec((BLOCK, width), lambda i: (first + i, 0))


SMEM = pl.BlockSpec(memory_space=pltpu.SMEM)
ANY = pl.BlockSpec(memory_space=pl.ANY)


def shape(dims, dtype):
    return jax.ShapeDtypeStruct(dims, dtype)


def part(vec_ref, span):
    return vec_ref[:, span[0] : span[0] + span[1]]


def add_rows(ref, value):
    ref[...] += jnp.sum(value, axis=0, keepdims=True)


HALF = LENGTH // 2


def for_halves(body, *sums):
    for ref in sums:
        ref[...] = jnp.zeros(ref.shape, ref.dtype)

    @pl.loop(0, 2)
    def _(step):
        body(pl.multiple_of(step * HALF, HALF))


def blocks_of(start):
    return [
        (slice(offset, offset + BLOCK), pl.ds(pl.multiple_of(start + offset, BLOCK), BLOCK))
        for offset in range(0, HALF, BLOCK)
    ]


def for_rows(count, size, loop, body):
    if loop:

        @pl.loop(0, count)
        def _(step):
            body(pl.ds(pl.multiple_of(step * size, size), size))
    else:
        for step in range(count):
            body(slice(step * size, step * size + size))


def statistics(values):
    width = values.shape[1]
    mean = jnp.sum(values, axis=1, keepdims=True) * (1.0 / width)
    center = values - mean
    spread = jnp.sum(center * center, axis=1, keepdims=True) * (1.0 / width)
    return center, lax.rsqrt(spread + NORM_EPS)


def gelu(a):
    t = jnp.tanh(GELU_C * (a + GELU_K * (a * a * a)))
    return 0.5 * a * (1.0 + t)


def gelu_slope(a):
    square = a * a
    t = jnp.tanh(GELU_C * a * (1.0 + GELU_K * square))
    half = 0.5 * (1.0 + t)
    return half + half * (1.0 - t) * a * (GELU_C + (3.0 * GELU_C * GELU_K) * square)


def norm_backward(grad, normed, root, gain, shift):
    width = grad.shape[1]
    d_a = grad * gelu_slope(normed * gain + shift)
    scaled = d_a * gain
    mean_one = jnp.sum(scaled, axis=1, keepdims=True) * (1.0 / width)
    mean_two = jnp.sum(scaled * normed, axis=1, keepdims=True) * (1.0 / width)
    return root * (scaled - mean_one - normed * mean_two), d_a * normed, d_a


def build_taps(ends_ref, source, padded, target, sign):
    width = source.shape[1]
    count = ends_ref.shape[0]
    empty = jnp.zeros((MARGIN, width), BF16)
    padded[0:MARGIN] = empty
    padded[MARGIN : MARGIN + LENGTH] = source[...]
    padded[MARGIN + LENGTH : MARGIN + LENGTH + MARGIN] = empty

    @pl.loop(0, STEPS)
    def _(step):
        start = pl.multiple_of(step * BLOCK, BLOCK)
        position = start + lax.broadcasted_iota(jnp.int32, (BLOCK, 128), 0)
        lower = jnp.zeros((BLOCK, 128), jnp.int32)
        upper = jnp.full((BLOCK, 128), ends_ref[count - 1], jnp.int32)
        for j in range(count - 1):
            lower = jnp.where(position >= ends_ref[j], ends_ref[j], lower)
        for j in range(count - 2, -1, -1):
            upper = jnp.where(position < ends_ref[j], ends_ref[j], upper)
        for k in range(KERNEL):
            offset = sign * OFFSETS[k]
            moved = position + offset
            mask = jnp.where((moved >= lower) & (moved < upper), 1.0, 0.0).astype(BF16)
            mask = jnp.concatenate([mask] * (width // 128), axis=1)
            value = padded[pl.ds(pl.multiple_of(start + MARGIN + offset, DILATION), BLOCK)]
            target[pl.ds(start, BLOCK), k * width : k * width + width] = value * mask


def build_taps_unrolled(ends_ref, source, target, sign):
    width = source.shape[1]
    count = ends_ref.shape[0]
    for rows in (slice(start, start + BLOCK) for start in range(0, LENGTH, BLOCK)):
        position = rows.start + lax.broadcasted_iota(jnp.int32, (BLOCK, 128), 0)
        lower = jnp.zeros((BLOCK, 128), jnp.int32)
        upper = jnp.full((BLOCK, 128), ends_ref[count - 1], jnp.int32)
        for j in range(count - 1):
            lower = jnp.where(position >= ends_ref[j], ends_ref[j], lower)
        for j in range(count - 2, -1, -1):
            upper = jnp.where(position < ends_ref[j], ends_ref[j], upper)
        for k in range(KERNEL):
            offset = sign * OFFSETS[k]
            moved = position + offset
            mask = jnp.where((moved >= lower) & (moved < upper), 1.0, 0.0).astype(BF16)
            mask = jnp.concatenate([mask] * (width // 128), axis=1)
            columns = slice(k * width, k * width + width)
            start = max(rows.start, -offset)
            stop = min(rows.stop, LENGTH - offset)
            value = source[start + offset : stop + offset]
            target[start:stop, columns] = value * mask[start - rows.start : stop - rows.start]
            if rows.start < start:
                target[rows.start : start, columns] = jnp.zeros((start - rows.start, width), BF16)
            if stop < rows.stop:
                target[stop : rows.stop, columns] = jnp.zeros((rows.stop - stop, width), BF16)


def dot(a, b):
    return jnp.dot(a, b, preferred_element_type=F32)


def dot_nt(a, b):
    return lax.dot_general(a, b, (((1,), (1,)), ((), ())), preferred_element_type=F32)


def assemble(net, geo, me_ref, own, peer, buffer, sems, full, beside=None, loop=False):
    core = jnp.bitwise_and(me_ref[0], 1)
    first = pltpu.make_async_copy(own, buffer.at[core], sems.at[0])
    second = pltpu.make_async_copy(peer, buffer.at[1 - core], sems.at[1])
    first.start()
    second.start()
    first.wait()
    second.wait()
    width = net.dp * geo.cols

    def body(f, first_row):
        blocks = [
            geo.unpack(buffer[d & 1, net.slot(d, f, me_ref[0], me_ref[1])])
            for d in range(net.dp)
        ]
        row = jnp.concatenate(blocks, axis=1)
        for k in range(geo.taps):
            value = row[k * geo.rows : k * geo.rows + geo.rows]
            full[pl.ds(k * geo.rows * net.fsdp + first_row, geo.rows)] = value
            if beside is not None:
                beside[pl.ds(first_row, geo.rows), k * width : k * width + width] = value

    if loop and geo.rows % 16 == 0:

        @pl.loop(0, net.fsdp)
        def _(f):
            body(f, pl.multiple_of(f * geo.rows, 16))
    else:
        for f in range(net.fsdp):
            body(f, f * geo.rows)


def distribute(net, geo, me_ref, full, buffer, sems, keep, send):
    width = net.dp * geo.cols
    for f in range(net.fsdp):
        pieces = [
            full[f * geo.rows : f * geo.rows + geo.rows, k * width : k * width + width]
            for k in range(geo.taps)
        ]
        row = pieces[0] if geo.taps == 1 else jnp.concatenate(pieces, axis=0)
        for d in range(net.dp):
            buffer[d & 1, net.slot(d, f, me_ref[0], me_ref[1])] = geo.pack(
                row[:, d * geo.cols : d * geo.cols + geo.cols]
            )
    core = jnp.bitwise_and(me_ref[0], 1)
    first = pltpu.make_async_copy(buffer.at[1 - core], send, sems.at[0])
    second = pltpu.make_async_copy(buffer.at[core], keep, sems.at[1])
    first.start()
    second.start()
    first.wait()
    second.wait()


def slots(net, geo):
    return (net.half, geo.packed, 128)


def piece_scratch(net, geo):
    return [pltpu.VMEM((2,) + slots(net, geo), BF16), pltpu.SemaphoreType.DMA((2,))]


def pack_weights(geos, *weights):
    rows = sum(geo.packed for geo in geos)

    def kernel(*refs):
        start = 0
        for geo, source in zip(geos, refs):
            refs[-1][start : start + geo.packed] = geo.pack(source[...].astype(BF16))
            start += geo.packed

    return call(
        kernel,
        "pack_weights",
        shape((rows, 128), BF16),
        [whole(w.shape) for w in weights],
        whole((rows, 128)),
        us=1.0,
    )(*weights)


def first_norm(block_input, cotangent, vec, first, held=()):
    def kernel(x_ref, cot_ref, vec_ref, *refs):
        h_ref, ht_ref, stat_ref, bias_ref = refs[-4:]

        def body(rows):
            values = x_ref[rows].astype(F32)
            center, root = statistics(values)
            normed = center * root
            hidden = gelu(normed * part(vec_ref, GAIN_ONE) + part(vec_ref, SHIFT_ONE)).astype(BF16)
            h_ref[rows] = hidden
            ht_ref[:, rows] = hidden.T
            lane = lax.broadcasted_iota(jnp.int32, (BLOCK // 2, 128), 1)
            stat_ref[rows] = jnp.where(lane == 0, values[:, :1] - center[:, :1], root)
            bias_ref[...] += jnp.sum(cot_ref[rows].astype(F32), axis=0, keepdims=True)

        @pl.when(pl.program_id(0) == 0)
        def _():
            bias_ref[...] = jnp.zeros((1, D), F32)

        for_rows(2, BLOCK // 2, True, body)

    return call(
        kernel,
        "first_norm",
        [
            shape((LENGTH, D), BF16),
            shape((D, LENGTH), BF16),
            shape((LENGTH, 128), F32),
            shape((1, D), F32),
        ],
        [tokens(D, first), tokens(D, first), whole(vec.shape)] + [ANY] * len(held),
        [
            tokens(D, first),
            pl.BlockSpec((D, BLOCK), lambda i: (0, first + i)),
            tokens(128, first),
            whole((1, D)),
        ],
        grid=(2,),
        aliases={3 + i: i for i in range(len(held))},
        us=2.8,
    )(block_input, cotangent, vec, *held)


def norm_out(rows, mixed, vec_ref, gain, shift_span, h_ref, ht_ref, normed_ref, root_ref):
    center, root = statistics(mixed)
    normed = center * root
    hidden = gelu(normed * part(vec_ref, gain) + part(vec_ref, shift_span)).astype(BF16)
    h_ref[rows] = hidden
    ht_ref[:, rows] = hidden.T
    normed_ref[rows] = normed
    root_ref[rows] = jnp.broadcast_to(root, (root.shape[0], 128))


NORM_SHAPES = [
    shape((LENGTH, INNER), BF16),
    shape((INNER, LENGTH), BF16),
    shape((LENGTH, INNER), F32),
    shape((LENGTH, 128), F32),
]


def wholes(shapes):
    return [whole(s.shape) for s in shapes]


def mix_one(net, geo, me, own, peer, hidden_one, vec):
    def kernel(me_ref, own_ref, peer_ref, h1_ref, vec_ref, h_ref, ht_ref, n_ref, r_ref, full, buf, sems):
        assemble(net, geo, me_ref, own_ref, peer_ref, buf, sems, full, loop=True)

        def body(rows):
            mixed = dot(h1_ref[rows], full[...]) + part(vec_ref, BIAS_ONE)
            norm_out(rows, mixed, vec_ref, GAIN_TWO, SHIFT_TWO, h_ref, ht_ref, n_ref, r_ref)

        for_rows(2 * STEPS, BLOCK // 2, True, body)

    outs = NORM_SHAPES + [shape((D, INNER), BF16)]
    return call(
        kernel,
        "mix_one",
        outs,
        [SMEM, ANY, ANY, whole((LENGTH, D)), whole(vec.shape)],
        wholes(outs),
        scratch=piece_scratch(net, geo),
        us=0.01,
    )(me, own, peer, hidden_one, vec)


def mix_two(net, geo, me, ends, own, peer, hidden_two, vec):
    def kernel(
        me_ref, ends_ref, own_ref, peer_ref, h2_ref, vec_ref, h_ref, ht_ref, n_ref, r_ref, beside, full, buf, sems, taps
    ):
        assemble(net, geo, me_ref, own_ref, peer_ref, buf, sems, full, beside)
        build_taps_unrolled(ends_ref, h2_ref, taps, 1)
        n_ref[...] = dot(taps[...], full[...])

        def body(rows):
            mixed = n_ref[rows] + part(vec_ref, BIAS_TWO)
            norm_out(rows, mixed, vec_ref, GAIN_THREE, SHIFT_THREE, h_ref, ht_ref, n_ref, r_ref)

        for_rows(STEPS, BLOCK, False, body)

    outs = NORM_SHAPES + [shape((INNER, KERNEL * INNER), BF16)]
    return call(
        kernel,
        "mix_two",
        outs,
        [SMEM, SMEM, ANY, ANY, whole((LENGTH, INNER)), whole(vec.shape)],
        wholes(outs),
        scratch=[pltpu.VMEM((KERNEL * INNER, INNER), BF16)]
        + piece_scratch(net, geo)
        + [
            pltpu.VMEM((LENGTH, KERNEL * INNER), BF16),
        ],
        us=11.7,
        vmem=WIDE_LIMIT,
    )(me, ends, own, peer, hidden_two, vec)


def norm_in(product, vec_ref, gain, shift_span, grad, n_ref, r_ref, back_ref, *sums):
    def body(start):
        grad[...] = product(pl.ds(start, HALF))
        for part_rows, rows in blocks_of(start):
            back, to_gain, to_shift = norm_backward(
                grad[part_rows],
                n_ref[rows],
                r_ref[rows][:, :1],
                part(vec_ref, gain),
                part(vec_ref, shift_span),
            )
            back = back.astype(BF16)
            back_ref[rows] = back
            for ref, value in zip(sums, (to_gain, to_shift, back.astype(F32))):
                add_rows(ref, value)

    for_halves(body, *sums)


def gradient_shapes(net, geo):
    return [shape(slots(net, geo), BF16)] * 2


def weight_gradient(net, geo, me, left, right, name="weight_gradient"):
    dims = (left.shape[0], right.shape[1])

    def kernel(me_ref, left_ref, right_ref, keep, send, full, buf, sems):
        full[...] = dot(left_ref[...], right_ref[...]).astype(BF16)
        distribute(net, geo, me_ref, full, buf, sems, keep, send)

    return call(
        kernel,
        name,
        gradient_shapes(net, geo),
        [SMEM, whole(left.shape), whole(right.shape)],
        [ANY, ANY],
        scratch=[pltpu.VMEM(dims, BF16)] + piece_scratch(net, geo),
        us=3.0 if dims[0] < dims[1] else 3.7,
    )(me, left, right)


def back_through_out(net, geo, me, own, peer, cotangent, normed, root, vec):
    def kernel(
        me_ref, own_ref, peer_ref, cot_ref, n_ref, r_ref, vec_ref, back_ref, gg_ref, gs_ref, gb_ref, full, buf, sems, grad
    ):
        assemble(net, geo, me_ref, own_ref, peer_ref, buf, sems, full)

        def product(rows):
            return dot_nt(cot_ref[rows], full[...])

        norm_in(product, vec_ref, GAIN_THREE, SHIFT_THREE, grad, n_ref, r_ref, back_ref, gg_ref, gs_ref, gb_ref)

    row = shape((1, INNER), F32)
    outs = [shape((LENGTH, INNER), BF16), row, row, row, shape((INNER, D), BF16)]
    return call(
        kernel,
        "back_through_out",
        outs,
        [SMEM, ANY, ANY] + wholes((cotangent, normed, root, vec)),
        wholes(outs),
        scratch=piece_scratch(net, geo) + [pltpu.VMEM((HALF, INNER), F32)],
        us=6.4,
    )(me, own, peer, cotangent, normed, root, vec)


def block_result(block_input, hidden_three, full_out, vec):
    half = LENGTH // 2

    def kernel(x_ref, h_ref, w_ref, vec_ref, out_ref):
        branch = dot(h_ref[...], w_ref[...]) + part(vec_ref, BIAS_THREE)
        out_ref[...] = (x_ref[...].astype(F32) + branch).astype(BF16)

    def rows_of(width):
        return pl.BlockSpec((half, width), lambda i: (i, 0))

    return call(
        kernel,
        "block_result",
        shape((LENGTH, D), BF16),
        [rows_of(D), rows_of(INNER), whole((INNER, D)), whole(vec.shape)],
        rows_of(D),
        grid=(2,),
        us=3.8,
    )(block_input, hidden_three, full_out, vec)


def conv_gradient(net, geo, me, ends, hidden_two_t, back_two):
    step = 2 * INNER
    width = KERNEL * INNER

    def kernel(me_ref, ends_ref, left_ref, back_ref, keep, send, taps, full, buf, sems, pad):
        build_taps(ends_ref, back_ref, pad, taps, -1)
        for start in range(0, width, step):
            columns = slice(start, min(start + step, width))
            full[:, columns] = dot(left_ref[...], taps[:, columns]).astype(BF16)
        distribute(net, geo, me_ref, full, buf, sems, keep, send)

    outs = gradient_shapes(net, geo) + [shape((LENGTH, width), BF16)]
    return call(
        kernel,
        "conv_gradient",
        outs,
        [SMEM, SMEM, whole((INNER, LENGTH)), whole((LENGTH, INNER))],
        [ANY, ANY, whole((LENGTH, width))],
        scratch=[pltpu.VMEM((INNER, width), BF16)]
        + piece_scratch(net, geo)
        + [pltpu.VMEM((LENGTH + 2 * MARGIN, INNER), BF16)],
        us=8.0,
        vmem=MIDDLE_LIMIT,
    )(me, ends, hidden_two_t, back_two)


def back_through_conv(taps, full_conv, normed, root, vec):
    def kernel(taps_ref, w_ref, n_ref, r_ref, vec_ref, back_ref, gg_ref, gs_ref, gb_ref, grad):
        def product(rows):
            return dot_nt(taps_ref[rows], w_ref[...])

        norm_in(product, vec_ref, GAIN_TWO, SHIFT_TWO, grad, n_ref, r_ref, back_ref, gg_ref, gs_ref, gb_ref)

    row = shape((1, INNER), F32)
    outs = [shape((LENGTH, INNER), BF16), row, row, row]
    return call(
        kernel,
        "back_through_conv",
        outs,
        wholes((taps, full_conv, normed, root, vec)),
        wholes(outs),
        scratch=[pltpu.VMEM((HALF, INNER), F32)],
        us=10.0,
    )(taps, full_conv, normed, root, vec)


def back_through_in(back_one, full_in, block_input, cotangent, stat, vec):
    def kernel(back_ref, w_ref, x_ref, cot_ref, stat_ref, vec_ref, out_ref, gg_ref, gs_ref, grad):
        @pl.when(pl.program_id(0) == 0)
        def _():
            gg_ref[...] = jnp.zeros((1, D), F32)
            gs_ref[...] = jnp.zeros((1, D), F32)

        grad[...] = dot_nt(back_ref[...], w_ref[...])
        for start in range(0, HALF, BLOCK):
            rows = slice(start, start + BLOCK)
            root = stat_ref[rows, 1:2]
            normed = (x_ref[rows].astype(F32) - stat_ref[rows, :1]) * root
            back, to_gain, to_shift = norm_backward(
                grad[rows], normed, root, part(vec_ref, GAIN_ONE), part(vec_ref, SHIFT_ONE)
            )
            out_ref[rows] = (cot_ref[rows].astype(F32) + back).astype(BF16)
            add_rows(gg_ref, to_gain)
            add_rows(gs_ref, to_shift)

    def rows_of(width):
        return pl.BlockSpec((HALF, width), lambda i: (i, 0))

    row = shape((1, D), F32)
    return call(
        kernel,
        "back_through_in",
        [shape((LENGTH, D), BF16), row, row],
        [rows_of(INNER), whole((D, INNER)), rows_of(D), rows_of(D), rows_of(128), whole(vec.shape)],
        [rows_of(D)] + [whole((1, D))] * 2,
        grid=(2,),
        scratch=[pltpu.VMEM((HALF, D), F32)],
        us=9.4,
    )(back_one, full_in, block_input, cotangent, stat, vec)


def sum_squares(owned, pieces):
    rows = sum(piece.shape[1] for piece in pieces) // 128
    total_rows = -(-(rows + 1) // 8) * 8
    n = len(owned)

    def kernel(*refs):
        out = refs[-1]
        total = jnp.zeros((1, 128), F32)
        for ref in refs[:n]:
            value = ref[...]
            total = total + jnp.sum(value * value, axis=0, keepdims=True)
        out[...] = jnp.zeros(out.shape, F32)
        row = 0
        for ref in refs[n:-1]:
            for start in range(0, ref.shape[1], 128):
                out[row : row + 1] = ref[:, start : start + 128]
                row += 1
        out[rows : rows + 1] = total

    return call(
        kernel,
        "sum_squares",
        shape((total_rows, 128), F32),
        [whole(v.shape) for v in (*owned, *pieces)],
        whole((total_rows, 128)),
        us=0.3,
    )(*owned, *pieces)


def adamw(weight, moment, square, gradient, rate, decay):
    new_moment = BETA_ONE * moment + (1.0 - BETA_ONE) * gradient
    new_square = BETA_TWO * square + (1.0 - BETA_TWO) * gradient * gradient
    moment_hat = new_moment * (1.0 / (1.0 - BETA_ONE**STEP))
    square_hat = new_square * (1.0 / (1.0 - BETA_TWO**STEP))
    update = moment_hat / (jnp.sqrt(square_hat) + ADAM_EPS)
    return weight - rate * (update + decay * weight), new_moment, new_square


def update_all(geos, owned, totals, weights, vectors):
    n = len(geos)
    size = vectors[0].shape[0]

    def kernel(*refs):
        owned_refs, total_ref = refs[:n], refs[n]
        ins = refs[n + 1 : n + 1 + 3 * n + 3]
        outs, held = refs[n + 1 + 3 * n + 3 : -1], refs[-1]

        def update(i, rows, gradient):
            weight, moment, square = (r[rows] for r in ins[3 * i : 3 * i + 3])
            results = adamw(weight, moment, square, gradient, RATE_MATRIX, DECAY_MATRIX)
            for ref, value in zip(outs[1 + 3 * i : 4 + 3 * i], results):
                ref[rows] = value

        grad_vec = total_ref[0:size]
        squares = jnp.sum(grad_vec * grad_vec, axis=0, keepdims=True) + total_ref[size : size + 1]
        norm = jnp.sqrt(jnp.sum(squares, axis=1, keepdims=True))
        outs[0][...] = norm
        clip = jnp.minimum(1.0, CLIP_LIMIT / (norm + 1e-06))
        for i, geo in enumerate(geos):
            gradient = geo.unpack(owned_refs[i][...].astype(F32)) * clip
            if geo.taps == 1 or geo.rows % 8:
                update(i, slice(None), gradient)
            else:
                held[...] = gradient

                @pl.loop(0, geo.taps)
                def _(k):
                    rows = pl.ds(pl.multiple_of(k * geo.rows, 8), geo.rows)
                    update(i, rows, held[rows])

        weight, moment, square = (r[...] for r in ins[3 * n :])
        results = adamw(weight, moment, square, grad_vec * clip, RATE_VECTOR, 0.0)
        for ref, value in zip(outs[1 + 3 * n :], results):
            ref[...] = value

    args = list(owned) + [totals] + [v for group in weights for v in group] + list(vectors)
    outs = [shape((1, 1), F32)]
    outs += [shape(v.shape, F32) for group in weights for v in group]
    outs += [shape(v.shape, F32) for v in vectors]
    return call(
        kernel,
        "update_all",
        outs,
        [whole(v.shape) for v in args],
        [whole(o.shape) for o in outs],
        scratch=[pltpu.VMEM(weights[1][0].shape, F32)],
        us=2.0,
    )(*args)


class Sequence:
    def __init__(self):
        self.last = ()

    def after(self, *values):
        return lax.optimization_barrier(tuple(values) + self.last)[: len(values)]

    def run(self, function, *values, **options):
        result = function(*self.after(*values), **options)
        self.last = tuple(jax.tree.leaves(result))[-1:]
        return result

    def wait(self, *values):
        self.last = tuple(values) + self.last


class Gather:
    def __init__(self, net, seq, shard):
        self.net, self.seq, self.stage = net, seq, 0
        self.held, self.coming = shard[None], None

    def send(self):
        (held,) = self.seq.after(self.held)
        self.held = held
        last = self.stage == self.net.stages()
        self.coming = lax.ppermute(held, AXES, self.net.core() if last else self.net.stage(self.stage))
        self.stage += 1

    def take(self):
        self.held, self.coming = self.seq.after(self.held, self.coming)
        if self.stage <= self.net.stages():
            self.held = jnp.concatenate([self.held, self.coming], axis=0)
        self.seq.wait(self.held, self.coming)

    def step(self):
        self.take()
        self.send()

    def finish(self):
        while self.stage <= self.net.stages():
            self.step()
        self.take()


def add(a, b):
    return (a.astype(F32) + b.astype(F32)).astype(BF16)


class Reduce:
    def __init__(self, net, seq, keep, send):
        self.net, self.seq, self.stage = net, seq, net.stages()
        self.keep = keep
        (send,) = seq.after(send)
        self.coming = lax.ppermute(send, AXES, net.core())

    def step(self):
        self.stage -= 1
        self.keep, self.coming = self.seq.after(self.keep, self.coming)
        half = self.keep.shape[0] // 2
        away = add(self.keep[half:], self.coming[half:])
        keep = add(self.keep[:half], self.coming[:half])
        self.keep, away = self.seq.after(keep, away)
        self.seq.wait(self.keep, away)
        self.coming = lax.ppermute(away, AXES, self.net.stage(self.stage))

    def end(self):
        while self.stage:
            self.step()
        self.keep, self.coming = self.seq.after(self.keep, self.coming)
        held = self.keep.astype(F32) + self.coming.astype(F32)
        self.seq.wait(held)
        return held[0]


def total_sum(net, value):
    value = value + lax.ppermute(value, AXES, net.core())
    for stage in range(net.stages()):
        value = value + lax.ppermute(value, AXES, net.stage(stage))
    return value


def body(
    dp,
    fsdp,
    block_input,
    cotangent,
    protein_lengths,
    weight_in,
    moment_in,
    square_in,
    weight_conv,
    moment_conv,
    square_conv,
    weight_out,
    moment_out,
    square_out,
    vectors,
    moment_vectors,
    square_vectors,
):
    net = Network(dp, fsdp, True)
    net_ends = Network(dp, fsdp, False)
    geo_in = Geometry(1, weight_in.shape[0], weight_in.shape[1])
    geo_conv = Geometry(KERNEL, weight_conv.shape[1], weight_conv.shape[2])
    geo_out = Geometry(1, weight_out.shape[0], weight_out.shape[1])
    geos = (geo_in, geo_conv, geo_out)

    def flat(v):
        return v.reshape(-1, v.shape[-1])

    me = jnp.stack([lax.axis_index("dp"), lax.axis_index("fsdp")]).astype(jnp.int32)
    ends = jnp.cumsum(protein_lengths[0]).astype(jnp.int32)
    vec = vectors.reshape(1, -1)
    x = block_input[0]
    cot = cotangent[0]

    seq = Sequence()
    shard_in = seq.run(functools.partial(pack_weights, (geo_in,)), weight_in)
    get_in = Gather(net_ends, seq, shard_in)
    get_in.send()
    shard_conv = seq.run(functools.partial(pack_weights, (geo_conv,)), flat(weight_conv))
    get_conv = Gather(net, seq, shard_conv)
    get_conv.send()
    shard_out = seq.run(functools.partial(pack_weights, (geo_out,)), weight_out)
    get_out = Gather(net, seq, shard_out)
    seq.wait(me, ends, vec)
    norms = seq.run(first_norm, x, cot, vec, first=0)
    get_in.step()
    get_conv.step()
    get_out.send()
    h1, h1_t, stat, half_b3 = seq.run(
        lambda x, cot, vec, *held: first_norm(x, cot, vec, STEPS // 2, held), x, cot, vec, *norms[:3]
    )
    grad_b3 = norms[3] + half_b3
    get_in.step()
    get_conv.step()
    get_out.step()
    get_in.step()
    get_conv.step()
    get_in.finish()
    h2, h2_t, n2, r2, full_in = seq.run(
        functools.partial(mix_one, net_ends, geo_in), me, get_in.held, get_in.coming, h1, vec
    )
    get_out.step()
    get_conv.step()
    get_conv.finish()
    get_out.step()
    h3, h3_t, n3, r3, full_conv = seq.run(
        functools.partial(mix_two, net, geo_conv),
        me, ends, get_conv.held, get_conv.coming, h2, vec,
    )
    get_out.step()
    pieces = seq.run(
        functools.partial(weight_gradient, net_ends, geo_out, name="out_gradient"), me, h3_t, cot
    )
    sum_out = Reduce(net_ends, seq, *pieces)
    get_out.finish()
    back_two, grad_g3, grad_s3, grad_b2, full_out = seq.run(
        functools.partial(back_through_out, net, geo_out),
        me, get_out.held, get_out.coming, cot, n3, r3, vec,
    )
    sum_out.step()
    keep, send, taps = seq.run(
        functools.partial(conv_gradient, net, geo_conv), me, ends, h2_t, back_two
    )
    sum_conv = Reduce(net, seq, keep, send)
    back_one, grad_g2, grad_s2, grad_b1 = seq.run(
        back_through_conv, taps, full_conv, n2, r2, vec
    )
    sum_conv.step()
    sum_out.step()
    pieces = seq.run(
        functools.partial(weight_gradient, net_ends, geo_in, name="in_gradient"),
        me, h1_t, back_one,
    )
    sum_in = Reduce(net_ends, seq, *pieces)
    block_output = seq.run(block_result, x, h3, full_out, vec)
    sum_in.step()
    sum_conv.step()
    input_grad, grad_g1, grad_s1 = seq.run(
        back_through_in, back_one, full_in, x, cot, stat, vec
    )
    sum_in.step()
    sum_conv.step()
    sum_out.step()
    sum_in.step()
    sum_conv.step()
    sum_out.step()
    sum_in.step()
    grad_out = sum_out.end()
    grad_conv = sum_conv.end()
    grad_in = sum_in.end()

    owned = (grad_in, grad_conv, grad_out)
    pieces = (grad_g1, grad_s1, grad_g2, grad_s2, grad_g3, grad_s3, grad_b1, grad_b2, grad_b3)
    totals = total_sum(net, sum_squares(owned, pieces))
    results = update_all(
        geos,
        owned,
        totals,
        (
            (weight_in, moment_in, square_in),
            (flat(weight_conv), flat(moment_conv), flat(square_conv)),
            (weight_out, moment_out, square_out),
        ),
        tuple(v.reshape(-1, 128) for v in (vectors, moment_vectors, square_vectors)),
    )
    norm, news = results[0], results[1:]
    return (
        block_output[None],
        input_grad[None],
        norm[0, 0],
        *news[0:3],
        *(v.reshape(weight_conv.shape) for v in news[3:6]),
        *news[6:9],
        *(v.reshape(-1) for v in news[9:12]),
    )


def solution(mesh):
    rows = P(("dp", "fsdp"), None, None)
    matrix = P("fsdp", "dp")
    taps = P(None, "fsdp", "dp")
    weights = (matrix,) * 3 + (taps,) * 3 + (matrix,) * 3 + (P(),) * 3
    return jax.shard_map(
        functools.partial(body, mesh.shape["dp"], mesh.shape["fsdp"]),
        mesh=mesh,
        in_specs=(rows, rows, P(("dp", "fsdp"), None)) + weights,
        out_specs=(rows, rows, P()) + weights,
        check_vma=False,
    )
```
